32 devices in a mesh: seq: 2 (over core), expert: 4 (over y, x), tensor: 4 (over z).
Axes of the slice: x: 2, y: 2, z: 4, core: 2. Of those that a mesh axis runs over, the one named last changes fastest.
Arguments:
- tokens: bfloat16 [1024, 4096], P(('seq', 'expert'), 'tensor'), may hold values from -100 to 100
- routes: int32 [1024, 2], P(('seq', 'expert')), may hold values from 0 to 3, all different within a row; in each aligned block of 128 rows (0 to 127, 128 to 255, ...) at most 128 rows name the same one
- route_weights: float32 [1024, 2], P(('seq', 'expert')), may hold values from 0.1 to 0.9
- norm_gain: float32 [4096], P('tensor'), may hold values from 0.1 to 1.9
- final_gain: float32 [4096], P('tensor'), may hold values from 0.1 to 1.9
- w_gate: bfloat16 [4, 4096, 14336], P('expert', None, ('seq', 'tensor')), may hold values from -0.09375 to 0.09375
- w_up: bfloat16 [4, 4096, 14336], P('expert', None, ('seq', 'tensor')), may hold values from -0.09375 to 0.09375
- w_down: bfloat16 [4, 14336, 4096], P('expert', ('seq', 'tensor')), may hold values from -0.09375 to 0.09375
- head_weight: bfloat16 [4096, 32000], P(None, ('expert', 'tensor')), may hold values from -100 to 100
- targets: int32 [1024], P('seq'), may hold values from 0 to 31999
Outputs:
- loss: float32 [1024], P(('seq', 'expert', 'tensor'))
The draws below stay inside these ranges and needn't reach their ends.
Inputs may be any that keep to these rules, and one draw needn't show every extreme that they name: Within each aligned block of 128 rows no expert is named by more than 128 routes, a bound that some block reaches; the two experts of a row differ.
All inputs are finite; a program needn't handle non-finite values.
Results may differ from the reference program's by a relative error of at most 0.00365.
Values may be sent and summed in bfloat16 or wider, within the bound.
No kernel may reach another device: no remote copies, remote signals or barrier semaphores. Data moves between devices by JAX's collectives and lax.ppermute only.
A program may use at most 192 MiB of HBM per device.

```python
import math
import jax
import jax.numpy as jnp
import numpy as np
from jax import lax

D = 4096
FF = 14336
VOCAB = 32000
TOPK = 2
TOK_DEV = 128
EXPERTS = 4
CAP = 128
TOKENS = 1024


def draw_tokens(key, part):
    key_base, key_column, key_row = jax.random.split(key, 3)
    column = jnp.arange(D, dtype=jnp.float32) / D
    column_scale = (3.0 ** column)[None, :] * jnp.exp(jax.random.uniform(key_column, (1, D), minval=0.0, maxval=1.1))
    base_draw = jax.random.truncated_normal(key_base, -4.0, 4.0, (TOKENS, D))
    row_scale = jnp.exp(jax.random.uniform(key_row, (TOKENS, 1), minval=0.0, maxval=math.log(10.0)))
    values = 0.15 * row_scale * base_draw * column_scale
    return values.astype(jnp.bfloat16)


def draw_head_weight(key, part):
    key_base = jax.random.fold_in(key, 0)
    base_draw = jax.random.truncated_normal(key_base, -4.0, 4.0, (D, VOCAB)) * (3.0 * D ** (-0.5))
    values = base_draw
    return values.astype(jnp.bfloat16)


def plant(values, key, low, high):
    longest = values.shape.index(max(values.shape))
    spots = []
    for shift in (0, 1):
        where = [jax.random.randint(jax.random.fold_in(key, axis), (), 0, length) for axis, length in enumerate(values.shape)]
        where[longest] = (where[longest] + shift) % values.shape[longest]
        spots.append(tuple(where))
    return values.at[spots[0]].set(low).at[spots[1]].set(high)


def block_scale(key, extent, pieces, least, largest):
    def one(position, shards_of):
        steps = jax.random.uniform(jax.random.fold_in(jax.random.fold_in(key, 6), position), (shards_of,), jnp.float32, least / len(pieces), largest / len(pieces))
        return jnp.repeat(jnp.exp(steps), extent[position] // shards_of).reshape((-1,) + (1,) * (len(extent) - position - 1))

    factor_of = one(*pieces[0])
    for cut in pieces[1:]:
        factor_of = factor_of * one(*cut)
    return factor_of


def rank_bounds(number_of, slope):
    loads = [(1 << 20) // math.isqrt(rank ** slope) + 1 for rank in range(1, number_of + 1)]
    width = 1 + sum(loads) // (1 << 30)
    return np.cumsum(np.array([max(1, weight // width) for weight in loads]))


def ranked_ids(key, shape, count, lean):
    listing = rank_bounds(count, lean)
    ticket = jax.random.randint(jax.random.fold_in(key, 1), shape, 0, int(listing[count - 1]))
    rank = jnp.searchsorted(jnp.asarray(listing, jnp.int32), ticket, side="right")
    return jax.random.permutation(jax.random.fold_in(key, 2), count)[rank].astype(jnp.int32)


def assign_block(key, own, number, rows, number_of, top, most, slope):
    sequence = jax.random.permutation(key, number_of)
    packed, common = portions_of(number_of, rows * top, most, slope, True), portions_of(number_of, rows * top, most, slope, False)
    places = jnp.arange(number_of)

    def named(tallies, offset_by):
        used = int((tallies > 0).sum())
        fixed = max(1, used // 4)
        moved = fixed + (places - fixed + offset_by * (used - fixed)) % max(1, number_of - fixed)
        return jnp.zeros((number_of,), jnp.int32).at[sequence[jnp.where(places < fixed, places, moved)]].set(jnp.asarray(tallies, jnp.int32))

    tallies = jnp.where(number % 4 == 0, named(packed, number // 4), named(common, number - number // 4 - 1))
    mixed = jax.random.permutation(jax.random.fold_in(own, 3), number_of)
    source_of, taker = mixed[0:number_of // 2 * 2:2], mixed[1:number_of // 2 * 2:2]
    room = jnp.minimum(tallies[source_of] - 1, most - tallies[taker]) // 2
    room = jnp.where((source_of == sequence[0]) | (taker == sequence[0]) | (tallies[taker] == 0), 0, jnp.maximum(room, 0))
    moved = jax.random.randint(jax.random.fold_in(own, 4), (number_of // 2,), 0, 1 << 20) % (room + 1)
    tallies = tallies.at[source_of].add(-moved).at[taker].add(moved)
    labels = jnp.searchsorted(jnp.cumsum(tallies), jnp.arange(rows * top), side="right").astype(jnp.int32)
    table = labels.reshape(top, rows).T
    table = table[jax.random.permutation(jax.random.fold_in(own, 1), rows)]
    offset_by = jax.random.randint(jax.random.fold_in(own, 2), (rows, 1), 0, top)
    return jnp.take_along_axis(table, (jnp.arange(top)[None, :] + offset_by) % top, axis=1)


def portions_of(count, total, most, lean, full):
    portions = [(1 << 20) // math.isqrt(grade ** lean) + 1 for grade in range(1, count + 1)]
    largest = most if full else min(most, max(-(-total // count), total * portions[0] // sum(portions)))
    least = 1 if total - largest >= count - 1 else 0
    counts, rest = [largest] + [least] * (count - 1), total - largest - least * (count - 1)
    while rest > 0:
        free = [i for i in range(1, count) if counts[i] < largest] or [i for i in range(1, count) if counts[i] < most]
        whole, remaining = sum([portions[i] for i in free]), rest
        for i in free:
            addition = min(most - counts[i], max(1, remaining * portions[i] // whole), rest)
            counts[i] = counts[i] + addition
            rest = rest - addition
    return np.array(counts)


def scatter_about(rng, shape, deviation, reach, cuts=(), kind=jnp.bfloat16):
    drawn = jax.random.normal(rng, shape, jnp.float32) * deviation
    if len(cuts) > 0:
        drawn = block_scale(rng, shape, cuts, -0.22, 0.18) * drawn
    return jnp.clip(drawn, min=-reach, max=reach).astype(kind)


def setup_inputs(seed: int = 0) -> dict:
    seeds = jax.random.split(jax.random.key(seed), 11)
    tokens = draw_tokens(jax.random.fold_in(seeds[10], 71), 0)
    routes_keys = jax.random.split(jax.random.fold_in(seeds[1], 1), TOKENS // TOK_DEV)
    routes_turns = jax.random.permutation(jax.random.fold_in(seeds[1], 3), TOKENS // TOK_DEV)
    routes = jax.vmap(lambda own, number: assign_block(jax.random.fold_in(seeds[1], 2), own, number, TOK_DEV, EXPERTS, TOPK, CAP, 2))(routes_keys, routes_turns).reshape((TOKENS, TOPK))
    route_weights = jnp.clip(0.1 + 0.79999997 * jax.random.uniform(seeds[2], (TOKENS, TOPK), jnp.float32) ** block_scale(seeds[2], (TOKENS, TOPK), ((0, 8),), -0.2, 0.2), 0.1, 0.9)
    norm_gain = jnp.clip(1.0 + 0.18 * jax.random.normal(seeds[3], (D,), jnp.float32), 0.1, 1.9)
    final_gain = jnp.clip(1.0 + 0.18 * jax.random.normal(seeds[4], (D,), jnp.float32), 0.1, 1.9)
    w_gate = scatter_about(seeds[5], (EXPERTS, D, FF), D ** -0.5, 0.09375, ((0, 4), (2, 8)))
    w_up = scatter_about(seeds[6], (EXPERTS, D, FF), D ** -0.5, 0.09375, ((0, 4), (2, 8)))
    w_down = scatter_about(seeds[7], (EXPERTS, FF, D), (FF // 4) ** -0.5, 0.09375, ((0, 4), (1, 8)))
    head_weight = draw_head_weight(jax.random.fold_in(seeds[10], 71), 0)
    targets = plant(ranked_ids(seeds[9], (TOKENS,), VOCAB, 2), jax.random.fold_in(seeds[9], 3), 0, VOCAB - 1).astype(jnp.int32)
    return {"tokens": tokens, "routes": routes, "route_weights": route_weights, "norm_gain": norm_gain, "final_gain": final_gain, "w_gate": w_gate, "w_up": w_up, "w_down": w_down, "head_weight": head_weight, "targets": targets}


epsilon = 1e-05

def reference(tokens, routes, route_weights, norm_gain, final_gain, w_gate, w_up, w_down, head_weight, targets):
    token_float = tokens.astype(jnp.float32)
    normed = (token_float * lax.rsqrt(lax.optimization_barrier(jnp.mean(token_float * token_float, axis=1, keepdims=True)) + epsilon) * norm_gain[None, :]).astype(jnp.bfloat16)
    flat_routes = routes.reshape(-1)
    flat_weights = route_weights.reshape(-1)
    limit = TOKENS // TOK_DEV * CAP

    def per_expert(mixed_rows, expert_id):
        keys = (flat_routes != expert_id).astype(jnp.int32)
        row_order = jnp.argsort(keys, stable=True)[:limit].astype(jnp.int32)
        token_index = row_order // 2
        row_block = normed[token_index].astype(jnp.float32)
        gate_mat = lax.dynamic_index_in_dim(w_gate, expert_id, 0, False).astype(jnp.float32)
        up_mat = lax.dynamic_index_in_dim(w_up, expert_id, 0, False).astype(jnp.float32)
        down_mat = lax.dynamic_index_in_dim(w_down, expert_id, 0, False).astype(jnp.float32)
        gate_part = jnp.dot(row_block, gate_mat, precision=lax.Precision.HIGHEST)
        up_part = jnp.dot(row_block, up_mat, precision=lax.Precision.HIGHEST)
        hidden = (jax.nn.silu(gate_part) * up_part).astype(jnp.bfloat16)
        expert_out = jnp.dot(hidden.astype(jnp.float32), down_mat, precision=lax.Precision.HIGHEST).astype(jnp.bfloat16)
        is_live = flat_routes[row_order] == expert_id
        weight_live = jnp.where(is_live, flat_weights[row_order], jnp.zeros_like(flat_weights[row_order]))
        mixed_rows = mixed_rows.at[token_index].add(weight_live[:, None] * expert_out.astype(jnp.float32))
        return (mixed_rows, None)
    mixed_start = jnp.zeros(token_float.shape, jnp.float32)
    mixed_rows, unused = lax.scan(per_expert, mixed_start, jnp.arange(EXPERTS, dtype=jnp.int32))
    residual = (token_float + mixed_rows).astype(jnp.bfloat16)
    residual_float = residual.astype(jnp.float32)
    final_rows = (residual_float * lax.rsqrt(lax.optimization_barrier(jnp.mean(residual_float * residual_float, axis=1, keepdims=True)) + epsilon) * final_gain[None, :]).astype(jnp.bfloat16)
    logits = jnp.dot(final_rows.astype(jnp.float32), head_weight.astype(jnp.float32), precision=lax.Precision.HIGHEST)
    row_top = lax.optimization_barrier(jnp.max(logits, axis=1))
    row_total = lax.optimization_barrier(jnp.sum(jnp.exp(logits - row_top[:, None]), axis=1))
    target_logit = jnp.take_along_axis(logits, targets[:, None].astype(jnp.int32), axis=1)[:, 0]
    return row_top + jnp.log(row_total) - target_logit
```

```python
import functools

import jax
import jax.numpy as jnp
from jax import lax
from jax.experimental import pallas as pl
from jax.experimental.pallas import tpu as pltpu
from jax.sharding import PartitionSpec as P

epsilon = 1e-05
LANES = 128
VMEM_BYTES = 56 * 1024 * 1024
MIB = 1024 * 1024


def params(limit=VMEM_BYTES):
    return pltpu.CompilerParams(vmem_limit_bytes=limit)


def whole():
    return pl.BlockSpec(memory_space=pltpu.VMEM)


def scalars():
    return pl.BlockSpec(memory_space=pltpu.SMEM)


def anywhere():
    return pl.BlockSpec(memory_space=pl.ANY)


def swap(x, axis, distance):
    size = lax.axis_size(axis)
    return lax.ppermute(x, axis, [(i, i ^ distance) for i in range(size)])


def gather_near(x, axis):
    return [x] + [swap(x, axis, d) for d in range(1, lax.axis_size(axis))]


def gather_plane(x, axis, first):
    if lax.axis_size(axis) != 4:
        return gather_near(x, axis)
    second = 3 - first
    near = swap(x, axis, first)
    side = swap(x, axis, second)
    far = swap(side, axis, first)
    pieces = {0: x, first: near, second: side, 3: far}
    return [pieces[d] for d in range(4)]


def norm_kernel(own_rows, where, *refs):
    count = (len(refs) - 3) // 2
    slices, gains = refs[:count], refs[count : 2 * count]
    small_ref, rows_ref, raw_ref = refs[2 * count :]
    rows, width = slices[0].shape
    full_width = width * count
    total = jnp.zeros((rows, 1), jnp.float32)
    for piece in slices:
        value = piece[...].astype(jnp.float32)
        total = total + jnp.sum(value * value, axis=1, keepdims=True)
    scale = lax.rsqrt(total / full_width + epsilon)
    start = pl.multiple_of(where[count], own_rows)
    for d in range(count):
        columns = pl.ds(pl.multiple_of(where[d], width), width)
        value = slices[d][...].astype(jnp.float32)
        rows_ref[:, columns] = (value * scale * gains[d][...]).astype(jnp.bfloat16)
        raw_ref[:, columns] = slices[d][pl.ds(start, own_rows), :]
    rows_ref[:, full_width:] = small_ref[...]


def norm_rows(where, slices, gains, small, own_rows):
    rows, width = slices[0].shape
    full_width = width * len(slices)
    return pl.pallas_call(
        functools.partial(norm_kernel, own_rows),
        out_shape=(
            jax.ShapeDtypeStruct((rows, full_width + LANES), jnp.bfloat16),
            jax.ShapeDtypeStruct((own_rows, full_width), jnp.bfloat16),
        ),
        in_specs=[scalars()] + [whole()] * (2 * len(slices) + 1),
        out_specs=(whole(), whole()),
        compiler_params=params(),
        cost_estimate=pl.CostEstimate(
            flops=6 * rows * full_width, bytes_accessed=4 * rows * full_width, transcendentals=rows
        ),
        name="norm_rows",
    )(where, *slices, *gains, small)


def hidden_kernel(pieces, full_width, where, *refs):
    piece_refs = refs[:pieces]
    gate_ref, up_ref, out_ref, rows_scr, weight_scr, sems = refs[pieces:]

    @pl.when(pl.program_id(0) == 0)
    def _():
        copies = []
        start = 0
        for i in range(pieces):
            count = piece_refs[i].shape[0]
            copies.append(
                pltpu.make_async_copy(
                    piece_refs[i], rows_scr.at[pl.ds(start, count), :], sems.at[i]
                )
            )
            start += count
        for copy in copies:
            copy.start()
        for copy in copies:
            copy.wait()
        small = rows_scr[:, full_width:].astype(jnp.float32)
        lane = lax.broadcasted_iota(jnp.int32, small.shape, 1)
        first = where[0] * 3
        mine = (lane >= first) & (lane < first + 3)
        weight = jnp.sum(jnp.where(mine, small, 0.0), axis=1, keepdims=True)
        weight_scr[...] = jnp.broadcast_to(weight, weight_scr.shape)

    rows = rows_scr[:, :full_width]
    gate = jnp.dot(rows, gate_ref[0], preferred_element_type=jnp.float32)
    up = jnp.dot(rows, up_ref[0], preferred_element_type=jnp.float32)
    hidden = gate / (1.0 + jnp.exp(-gate)) * up * weight_scr[:, :1]
    out_ref[...] = hidden.astype(jnp.bfloat16)


def hidden_rows(where, pieces, w_gate, w_up):
    rows = sum(p.shape[0] for p in pieces)
    full_width, hidden = w_gate.shape[1:]
    tile = 256 if hidden % 256 == 0 else hidden
    weight_spec = pl.BlockSpec((1, full_width, tile), lambda i: (0, 0, i))
    return pl.pallas_call(
        functools.partial(hidden_kernel, len(pieces), full_width),
        out_shape=jax.ShapeDtypeStruct((rows, hidden), jnp.bfloat16),
        grid=(hidden // tile,),
        in_specs=[scalars()] + [anywhere()] * len(pieces) + [weight_spec, weight_spec],
        out_specs=pl.BlockSpec((rows, tile), lambda i: (0, i)),
        scratch_shapes=[
            pltpu.VMEM((rows, full_width + LANES), jnp.bfloat16),
            pltpu.VMEM((rows, LANES), jnp.float32),
            pltpu.SemaphoreType.DMA((len(pieces),)),
        ],
        compiler_params=params(),
        cost_estimate=pl.CostEstimate(
            flops=4 * rows * full_width * hidden,
            bytes_accessed=4 * full_width * hidden + 2 * rows * (full_width + hidden),
            transcendentals=rows * hidden,
        ),
        name="hidden_rows",
    )(where, *pieces, w_gate, w_up)


def down_kernel(hidden_ref, down_ref, *outs):
    out = jnp.dot(hidden_ref[...], down_ref[0], preferred_element_type=jnp.float32)
    part = out.shape[0] // len(outs)
    for i in range(len(outs)):
        outs[i][...] = out[i * part : (i + 1) * part].astype(jnp.bfloat16)


def down_rows(hidden, w_down, parts):
    rows, depth = hidden.shape
    full_width = w_down.shape[2]
    tile = 512 if full_width % 512 == 0 else full_width
    shape = jax.ShapeDtypeStruct((rows // parts, full_width), jnp.bfloat16)
    return pl.pallas_call(
        down_kernel,
        out_shape=(shape,) * parts,
        grid=(full_width // tile,),
        in_specs=[
            pl.BlockSpec((rows, depth), lambda i: (0, 0)),
            pl.BlockSpec((1, depth, tile), lambda i: (0, 0, i)),
        ],
        out_specs=(pl.BlockSpec((rows // parts, tile), lambda i: (0, i)),) * parts,
        compiler_params=params(),
        cost_estimate=pl.CostEstimate(
            flops=2 * rows * depth * full_width,
            bytes_accessed=2 * depth * full_width + 2 * rows * (depth + full_width),
            transcendentals=0,
        ),
        name="down_rows",
    )(hidden, w_down)


def final_kernel(where, parts, raw_ref, *refs):
    gains, out_ref = refs[:-1], refs[-1]
    width = gains[0].shape[1]
    residual = raw_ref[...].astype(jnp.float32)
    mixed = parts[0][...].astype(jnp.float32)
    for part in parts[1:]:
        mixed = mixed + part[...].astype(jnp.float32)
    residual = (residual + mixed).astype(jnp.bfloat16).astype(jnp.float32)
    total = jnp.sum(residual * residual, axis=1, keepdims=True)
    scale = lax.rsqrt(total / residual.shape[1] + epsilon)
    out_ref[...] = (residual * scale).astype(jnp.float32)
    for d in range(len(gains)):
        columns = pl.ds(pl.multiple_of(where[d], width), width)
        out_ref[:, columns] = out_ref[:, columns] * gains[d][...]


def final_rows(where, parts, raw, gains):
    rows, full_width = raw.shape

    def body(where_ref, *refs):
        final_kernel(where_ref, refs[: len(parts)], refs[len(parts)], *refs[len(parts) + 1 :])

    return pl.pallas_call(
        body,
        out_shape=jax.ShapeDtypeStruct((rows, full_width), jnp.float32),
        in_specs=[scalars()] + [whole()] * (len(parts) + 1 + len(gains)),
        out_specs=whole(),
        compiler_params=params(),
        cost_estimate=pl.CostEstimate(
            flops=8 * rows * full_width, bytes_accessed=14 * rows * full_width, transcendentals=rows
        ),
        name="final_rows",
    )(where, *parts, raw, *gains).astype(jnp.bfloat16)


def head_kernel(pieces, vocab_part, tile, *refs):
    piece_refs = refs[:pieces]
    head_ref, target_ref, out_ref, rows_scr, top_scr, total_scr, hit_scr, sems = refs[pieces:]
    step = pl.program_id(0)

    @pl.when(step == 0)
    def _():
        copies = []
        start = 0
        for i in range(pieces):
            count = piece_refs[i].shape[0]
            copies.append(
                pltpu.make_async_copy(
                    piece_refs[i], rows_scr.at[pl.ds(start, count), :], sems.at[i]
                )
            )
            start += count
        for copy in copies:
            copy.start()
        for copy in copies:
            copy.wait()
        top_scr[...] = jnp.full(top_scr.shape, -jnp.inf, jnp.float32)
        total_scr[...] = jnp.zeros(total_scr.shape, jnp.float32)
        hit_scr[...] = jnp.zeros(hit_scr.shape, jnp.float32)

    logits = jnp.dot(rows_scr[...], head_ref[...], preferred_element_type=jnp.float32)
    column = lax.broadcasted_iota(jnp.int32, logits.shape, 1) + step * tile
    logits = jnp.where(column < vocab_part, logits, -jnp.inf)
    old_top = top_scr[:, :1]
    top = jnp.maximum(old_top, jnp.max(logits, axis=1, keepdims=True))
    total = total_scr[:, :1] * jnp.exp(old_top - top) + jnp.sum(
        jnp.exp(logits - top), axis=1, keepdims=True
    )
    hit = (column == target_ref[:, :1]) & (column < vocab_part)
    target = hit_scr[:, :1] + jnp.sum(jnp.where(hit, logits, 0.0), axis=1, keepdims=True)
    top_scr[...] = jnp.broadcast_to(top, top_scr.shape)
    total_scr[...] = jnp.broadcast_to(total, total_scr.shape)
    hit_scr[...] = jnp.broadcast_to(target, hit_scr.shape)

    @pl.when(step == pl.num_programs(0) - 1)
    def _():
        lane = lax.broadcasted_iota(jnp.int32, out_ref.shape, 1)
        out_ref[...] = jnp.where(
            lane == 0, top_scr[...], jnp.where(lane == 1, total_scr[...], hit_scr[...])
        )


def head_terms(pieces, head_weight, targets):
    rows = sum(p.shape[0] for p in pieces)
    full_width, vocab_part = head_weight.shape
    tile = 512
    return pl.pallas_call(
        functools.partial(head_kernel, len(pieces), vocab_part, tile),
        out_shape=jax.ShapeDtypeStruct((rows, LANES), jnp.float32),
        grid=(pl.cdiv(vocab_part, tile),),
        in_specs=[anywhere()] * len(pieces)
        + [
            pl.BlockSpec((full_width, tile), lambda i: (0, i)),
            pl.BlockSpec((rows, 1), lambda i: (0, 0)),
        ],
        out_specs=pl.BlockSpec((rows, LANES), lambda i: (0, 0)),
        scratch_shapes=[
            pltpu.VMEM((rows, full_width), jnp.bfloat16),
            pltpu.VMEM((rows, LANES), jnp.float32),
            pltpu.VMEM((rows, LANES), jnp.float32),
            pltpu.VMEM((rows, LANES), jnp.float32),
            pltpu.SemaphoreType.DMA((len(pieces),)),
        ],
        compiler_params=params(),
        cost_estimate=pl.CostEstimate(
            flops=2 * rows * full_width * vocab_part,
            bytes_accessed=2 * full_width * (vocab_part + rows),
            transcendentals=rows * vocab_part,
        ),
        name="head_terms",
    )(*pieces, head_weight, targets)


def join_terms(parts):
    top = functools.reduce(jnp.maximum, [p[..., 0] for p in parts])
    total = sum(p[..., 1] * jnp.exp(p[..., 0] - top) for p in parts)
    target = sum(p[..., 2] for p in parts)
    return jnp.stack([top, total, target], axis=-1)


def flip(x, axis, index):
    size = x.shape[axis]
    bit = 1
    while bit < size:
        shape = x.shape[:axis] + (size // (2 * bit), 2, bit) + x.shape[axis + 1 :]
        turned = jnp.flip(x.reshape(shape), axis + 1).reshape(x.shape)
        x = jnp.where((index & bit) != 0, turned, x)
        bit *= 2
    return x


def route_columns(routes, route_weights, experts):
    ids = jnp.arange(experts, dtype=jnp.int32)
    weight = jnp.zeros((routes.shape[0], experts), jnp.float32)
    for j in range(routes.shape[1]):
        weight = weight + jnp.where(routes[:, j : j + 1] == ids, route_weights[:, j : j + 1], 0.0)
    high = lax.reduce_precision(weight, 8, 7)
    middle = lax.reduce_precision(weight - high, 8, 7)
    low = weight - high - middle
    parts = jnp.stack([high, middle, low], axis=-1).reshape(routes.shape[0], 3 * experts)
    parts = jnp.pad(parts, ((0, 0), (0, LANES - 3 * experts)))
    return parts.astype(jnp.bfloat16)


def on_device(
    tokens, routes, route_weights, norm_gain, final_gain, w_gate, w_up, w_down, head_weight, targets
):
    tok_rows, width = tokens.shape
    n_expert = lax.axis_size("expert")
    n_tensor = lax.axis_size("tensor")
    my_expert = lax.axis_index("expert")
    my_tensor = lax.axis_index("tensor")
    experts = w_gate.shape[0] * n_expert
    full_width = width * n_tensor
    own = tok_rows // n_tensor
    splits = 2 if own % 32 == 0 else 1
    sub = own // splits
    rows = sub * n_tensor
    vocab_part = head_weight.shape[1]
    f32 = jnp.float32

    near = jnp.arange(n_tensor, dtype=jnp.int32) ^ my_tensor
    where = jnp.concatenate([near * width, (my_tensor * sub)[None]]).astype(jnp.int32)
    mine = my_expert.astype(jnp.int32)[None]

    def part_of(x, h):
        return x.reshape((n_tensor, splits, sub) + x.shape[1:])[:, h].reshape(
            (rows,) + x.shape[1:]
        )

    small = route_columns(routes, route_weights, experts)
    gains = gather_near(jnp.stack([norm_gain, final_gain]), "tensor")
    norm_gains = [g[0:1] for g in gains]
    final_gains = [g[1:2] for g in gains]

    pieces, raws = [], []
    for h in range(splits):
        slices = gather_near(part_of(tokens, h), "tensor")
        normed, raw = norm_rows(where, slices, norm_gains, part_of(small, h), sub)
        plane = gather_plane(normed, "expert", 1 + h % 2)
        other = [swap(p, "seq", 1) for p in plane]
        pieces.append(plane + other)
        raws.append(raw)

    finals = []
    for h in range(splits):
        hidden = hidden_rows(mine, pieces[h], w_gate, w_up)
        kept, sent = down_rows(hidden, w_down, 2)
        got = swap(sent, "seq", 1)
        kept = kept.reshape(n_expert, rows, full_width)
        got = got.reshape(n_expert, rows, full_width)

        def both(d):
            return kept[d].astype(f32) + got[d].astype(f32)

        if n_expert == 4:
            first = 1 + h % 2
            second = 3 - first
            sending = jnp.stack([both(first), both(3)]).astype(jnp.bfloat16)
            arrived = swap(sending, "expert", first)
            passing = (both(second) + arrived[1].astype(f32)).astype(jnp.bfloat16)
            last = swap(passing, "expert", second)
            total = both(0) + arrived[0].astype(f32) + last.astype(f32)
        else:
            total = both(0)
            for d in range(1, n_expert):
                total = total + swap(both(d).astype(jnp.bfloat16), "expert", d).astype(f32)
        total = total.astype(jnp.bfloat16).reshape(n_tensor, sub, full_width)

        parts = [lax.dynamic_index_in_dim(total, my_tensor, 0, False)]
        for d in range(1, n_tensor):
            out = lax.dynamic_index_in_dim(total, my_tensor ^ d, 0, False)
            parts.append(swap(out, "tensor", d))
        finals.append(final_rows(where, parts, raws[h], final_gains))

    start = (my_expert * n_tensor + my_tensor) * vocab_part
    local = (targets - start).astype(jnp.int32).reshape(n_expert, n_tensor, splits, sub)
    local = flip(flip(local, 0, my_expert), 1, my_tensor)
    terms = []
    for h in range(splits):
        column = jnp.concatenate(gather_near(finals[h], "tensor"), axis=0)
        plane = gather_plane(column, "expert", 1 + h % 2)
        terms.append(
            head_terms(plane, head_weight, local[:, :, h].reshape(-1, 1)).reshape(
                n_expert, n_tensor, sub, LANES
            )[..., :3]
        )
    terms = jnp.stack(terms, axis=2)
    joined = join_terms(
        [terms[:, 0]] + [swap(terms[:, d], "tensor", d) for d in range(1, n_tensor)]
    )
    joined = join_terms(
        [joined[0]] + [swap(joined[d], "expert", d) for d in range(1, n_expert)]
    )
    return (joined[..., 0] + jnp.log(joined[..., 1]) - joined[..., 2]).reshape(own)


def solution(mesh):
    return jax.shard_map(
        on_device,
        mesh=mesh,
        in_specs=(
            P(("seq", "expert"), "tensor"),
            P(("seq", "expert"), None),
            P(("seq", "expert"), None),
            P("tensor"),
            P("tensor"),
            P("expert", None, ("seq", "tensor")),
            P("expert", None, ("seq", "tensor")),
            P("expert", ("seq", "tensor"), None),
            P(None, ("expert", "tensor")),
            P("seq"),
        ),
        out_specs=P(("seq", "expert", "tensor")),
        check_vma=False,
    )
```

```python
import functools

import jax
import jax.numpy as jnp
from jax import lax
from jax.experimental import pallas as pl
from jax.experimental.pallas import tpu as pltpu
from jax.sharding import PartitionSpec as P

epsilon = 1e-05
LANES = 128
VMEM_BYTES = 56 * 1024 * 1024


def params(limit=VMEM_BYTES):
    return pltpu.CompilerParams(vmem_limit_bytes=limit)


def whole():
    return pl.BlockSpec(memory_space=pltpu.VMEM)


def anywhere():
    return pl.BlockSpec(memory_space=pl.ANY)


def swap(x, axis, distance):
    size = lax.axis_size(axis)
    return lax.ppermute(x, axis, [(i, i ^ distance) for i in range(size)])


def gather_near(x, axis):
    return [x] + [swap(x, axis, d) for d in range(1, lax.axis_size(axis))]


def gather_plane(x, axis):
    if lax.axis_size(axis) != 4:
        return gather_near(x, axis)
    half = x.shape[0] // 2
    one, two = swap(x, axis, 1), swap(x, axis, 2)
    return [x, one, two, swap(two[:half], axis, 1), swap(one[half:], axis, 2)]


def load_pieces(piece_refs, scratch, sems):
    copies = []
    start = 0
    for i in range(len(piece_refs)):
        count = piece_refs[i].shape[0]
        copies.append(
            pltpu.make_async_copy(piece_refs[i], scratch.at[pl.ds(start, count), :], sems.at[i])
        )
        start += count
    for copy in copies:
        copy.start()
    for copy in copies:
        copy.wait()


def norm_kernel(splits, part, count, *refs):
    slices, gains = refs[:count], refs[count : 2 * count]
    routes_ref, weights_ref = refs[2 * count : 2 * count + 2]
    rows_ref, raw_ref = refs[-2:]
    rows, width = slices[0].shape
    full_width = width * count
    own_rows = rows // count
    me = lax.axis_index("tensor")
    total = jnp.zeros((rows, 1), jnp.float32)
    for piece in slices:
        value = piece[...].astype(jnp.float32)
        total = total + jnp.sum(value * value, axis=1, keepdims=True)
    scale = lax.rsqrt(total / full_width + epsilon)
    start = pl.multiple_of(me * own_rows, own_rows)
    for d in range(count):
        columns = pl.ds(pl.multiple_of((me ^ d) * width, width), width)
        value = slices[d][...].astype(jnp.float32)
        rows_ref[:, columns] = (value * scale * gains[d][0:1, :]).astype(jnp.bfloat16)
        raw_ref[:, columns] = slices[d][pl.ds(start, own_rows), :]
    lane = lax.broadcasted_iota(jnp.int32, (own_rows, LANES), 1)
    expert = lane // 3
    kind = lane - expert * 3
    for i in range(count):
        block = pl.ds((i * splits + part) * own_rows, own_rows)
        weight = jnp.zeros((own_rows, LANES), jnp.float32)
        for j in range(routes_ref.shape[1]):
            named = routes_ref[block, j : j + 1] == expert
            weight = weight + jnp.where(named, weights_ref[block, j : j + 1], 0.0)
        high = weight.astype(jnp.bfloat16).astype(jnp.float32)
        middle = (weight - high).astype(jnp.bfloat16).astype(jnp.float32)
        low = weight - high - middle
        value = jnp.where(kind == 0, high, jnp.where(kind == 1, middle, low))
        rows_ref[i * own_rows : (i + 1) * own_rows, full_width:] = value.astype(jnp.bfloat16)


def norm_rows(slices, gains, routes, route_weights, splits, part, after):
    rows, width = slices[0].shape
    count = len(slices)
    full_width = width * count
    return pl.pallas_call(
        functools.partial(norm_kernel, splits, part, count),
        out_shape=(
            jax.ShapeDtypeStruct((rows, full_width + LANES), jnp.bfloat16),
            jax.ShapeDtypeStruct((rows // count, full_width), jnp.bfloat16),
        ),
        in_specs=[whole()] * (2 * count + 2) + [anywhere()] * len(after),
        out_specs=(whole(), whole()),
        compiler_params=params(),
        cost_estimate=pl.CostEstimate(
            flops=6 * rows * full_width, bytes_accessed=4 * rows * full_width, transcendentals=rows
        ),
        name="norm_rows",
    )(*slices, *gains, routes, route_weights, *after)


def hidden_kernel(pieces, streams, after, *refs):
    piece_refs = refs[:pieces]
    gate_refs = refs[pieces : pieces + streams]
    up_refs = refs[pieces + streams : pieces + 2 * streams]
    out_ref, rows_scr, weight_scr, sems = refs[pieces + 2 * streams + after :]
    depth = gate_refs[0].shape[1]

    @pl.when(pl.program_id(0) == 0)
    def _():
        load_pieces(piece_refs, rows_scr, sems)
        small = rows_scr[:, depth * streams :].astype(jnp.float32)
        lane = lax.broadcasted_iota(jnp.int32, small.shape, 1)
        first = lax.axis_index("expert") * 3
        mine = (lane >= first) & (lane < first + 3)
        weight = jnp.sum(jnp.where(mine, small, 0.0), axis=1, keepdims=True)
        weight_scr[...] = jnp.broadcast_to(0.5 * weight, weight_scr.shape)

    def product(refs):
        total = None
        for i in range(streams):
            rows = rows_scr[:, i * depth : (i + 1) * depth]
            term = jnp.dot(rows, refs[i][0], preferred_element_type=jnp.float32)
            total = term if total is None else total + term
        return total

    gate = product(gate_refs)
    up = product(up_refs)
    hidden = gate * (1.0 + jnp.tanh(0.5 * gate)) * up * weight_scr[:, :1]
    out_ref[...] = hidden.astype(jnp.bfloat16)


def hidden_rows(pieces, w_gate, w_up, after):
    rows = sum(p.shape[0] for p in pieces)
    full_width, hidden = w_gate.shape[1:]
    tile = 256 if hidden % 256 == 0 else hidden
    streams = 2
    depth = full_width // streams
    weight_specs = [
        pl.BlockSpec((1, depth, tile), lambda i, part=part: (0, part, i)) for part in range(streams)
    ]
    return pl.pallas_call(
        functools.partial(hidden_kernel, len(pieces), streams, len(after)),
        out_shape=jax.ShapeDtypeStruct((rows, hidden), jnp.bfloat16),
        grid=(hidden // tile,),
        in_specs=[anywhere()] * len(pieces) + weight_specs * 2 + [anywhere()] * len(after),
        out_specs=pl.BlockSpec((rows, tile), lambda i: (0, i)),
        scratch_shapes=[
            pltpu.VMEM((rows, full_width + LANES), jnp.bfloat16),
            pltpu.VMEM((rows, LANES), jnp.float32),
            pltpu.SemaphoreType.DMA((len(pieces),)),
        ],
        compiler_params=params(),
        cost_estimate=pl.CostEstimate(
            flops=4 * rows * full_width * hidden,
            bytes_accessed=4 * full_width * hidden + 2 * rows * (full_width + hidden),
            transcendentals=rows * hidden,
        ),
        name="hidden_rows",
    )(*pieces, *[w_gate] * streams, *[w_up] * streams, *after)


def down_kernel(streams, after, hidden_ref, *refs):
    outs = refs[streams + after :]
    part = hidden_ref.shape[0] // len(outs)
    for j in range(streams):
        out = jnp.dot(hidden_ref[...], refs[j][0], preferred_element_type=jnp.float32)
        columns = slice(j * out.shape[1], (j + 1) * out.shape[1])
        for i in range(len(outs)):
            outs[i][:, columns] = out[i * part : (i + 1) * part].astype(jnp.bfloat16)


def down_rows(hidden, w_down, parts, after):
    rows, depth = hidden.shape
    full_width = w_down.shape[2]
    tile = 512 if full_width % 512 == 0 else full_width
    streams = 2
    narrow = tile // streams
    shape = jax.ShapeDtypeStruct((rows // parts, full_width), jnp.bfloat16)
    return pl.pallas_call(
        functools.partial(down_kernel, streams, len(after)),
        out_shape=(shape,) * parts,
        grid=(full_width // tile,),
        in_specs=[pl.BlockSpec((rows, depth), lambda i: (0, 0))]
        + [
            pl.BlockSpec((1, depth, narrow), lambda i, part=part: (0, 0, streams * i + part))
            for part in range(streams)
        ]
        + [anywhere()] * len(after),
        out_specs=(pl.BlockSpec((rows // parts, tile), lambda i: (0, i)),) * parts,
        compiler_params=params(),
        cost_estimate=pl.CostEstimate(
            flops=2 * rows * depth * full_width,
            bytes_accessed=2 * depth * full_width + 2 * rows * (depth + full_width),
            transcendentals=0,
        ),
        name="down_rows",
    )(hidden, *[w_down] * streams, *after)


def final_kernel(parts, gains_count, *refs):
    part_refs, raw_ref = refs[:parts], refs[parts]
    gains = refs[parts + 1 : parts + 1 + gains_count]
    out_ref, work = refs[parts + 1 + gains_count :]
    width = gains[0].shape[1]
    me = lax.axis_index("tensor")
    mixed = part_refs[0][...].astype(jnp.float32)
    for part in part_refs[1:]:
        mixed = mixed + part[...].astype(jnp.float32)
    residual = raw_ref[...].astype(jnp.float32) + mixed
    residual = residual.astype(jnp.bfloat16).astype(jnp.float32)
    total = jnp.sum(residual * residual, axis=1, keepdims=True)
    scale = lax.rsqrt(total / residual.shape[1] + epsilon)
    work[...] = residual * scale
    for d in range(gains_count):
        columns = pl.ds(pl.multiple_of((me ^ d) * width, width), width)
        out_ref[:, columns] = (work[:, columns] * gains[d][1:2, :]).astype(jnp.bfloat16)


def final_rows(parts, raw, gains):
    rows, full_width = raw.shape
    return pl.pallas_call(
        functools.partial(final_kernel, len(parts), len(gains)),
        out_shape=jax.ShapeDtypeStruct((rows, full_width), jnp.bfloat16),
        in_specs=[whole()] * (len(parts) + 1 + len(gains)),
        out_specs=whole(),
        scratch_shapes=[pltpu.VMEM((rows, full_width), jnp.float32)],
        compiler_params=params(),
        cost_estimate=pl.CostEstimate(
            flops=8 * rows * full_width, bytes_accessed=12 * rows * full_width, transcendentals=rows
        ),
        name="final_rows",
    )(*parts, raw, *gains)


def head_kernel(pieces, *refs):
    piece_refs = refs[:pieces]
    head_ref, target_ref, out_ref, rows_scr, sems = refs[pieces:]
    step = pl.program_id(0)
    tile = head_ref.shape[0]

    @pl.when(step == 0)
    def _():
        load_pieces(piece_refs, rows_scr, sems)
        lane = lax.broadcasted_iota(jnp.int32, out_ref.shape, 0)
        out_ref[...] = jnp.where(lane == 0, -jnp.inf, 0.0)

    logits = lax.dot_general(
        head_ref[...],
        rows_scr[...],
        (((1,), (1,)), ((), ())),
        preferred_element_type=jnp.float32,
    )
    word = lax.broadcasted_iota(jnp.int32, logits.shape, 0) + step * tile
    old_top, old_total = out_ref[0:1, :], out_ref[1:2, :]
    top = jnp.maximum(old_top, jnp.max(logits, axis=0, keepdims=True))
    out_ref[0:1, :] = top
    out_ref[1:2, :] = old_total * jnp.exp(old_top - top) + jnp.sum(
        jnp.exp(logits - top), axis=0, keepdims=True
    )
    hit = word == target_ref[...]
    out_ref[2:3, :] += jnp.sum(jnp.where(hit, logits, 0.0), axis=0, keepdims=True)


def head_terms(pieces, head_rows, targets):
    rows = sum(p.shape[0] for p in pieces)
    vocab_part, full_width = head_rows.shape
    tile = 400 if vocab_part % 400 == 0 else vocab_part
    return pl.pallas_call(
        functools.partial(head_kernel, len(pieces)),
        out_shape=jax.ShapeDtypeStruct((8, rows), jnp.float32),
        grid=(vocab_part // tile,),
        in_specs=[anywhere()] * len(pieces)
        + [
            pl.BlockSpec((tile, full_width), lambda i: (i, 0)),
            pl.BlockSpec((1, rows), lambda i: (0, 0)),
        ],
        out_specs=pl.BlockSpec((8, rows), lambda i: (0, 0)),
        scratch_shapes=[
            pltpu.VMEM((rows, full_width), jnp.bfloat16),
            pltpu.SemaphoreType.DMA((len(pieces),)),
        ],
        compiler_params=params(),
        cost_estimate=pl.CostEstimate(
            flops=2 * rows * full_width * vocab_part,
            bytes_accessed=2 * full_width * (vocab_part + rows),
            transcendentals=rows * vocab_part,
        ),
        name="head_terms",
    )(*pieces, head_rows, targets)


def join_terms(parts):
    top = functools.reduce(jnp.maximum, [p[0] for p in parts])
    total = sum(p[1] * jnp.exp(p[0] - top) for p in parts)
    target = sum(p[2] for p in parts)
    return jnp.stack([top, total, target])


def flip(x, axis, index):
    size = x.shape[axis]
    bit = 1
    while bit < size:
        shape = x.shape[:axis] + (size // (2 * bit), 2, bit) + x.shape[axis + 1 :]
        turned = jnp.flip(x.reshape(shape), axis + 1).reshape(x.shape)
        x = jnp.where((index & bit) != 0, turned, x)
        bit *= 2
    return x


def sum_plane(kept, got):
    f32, b16 = jnp.float32, jnp.bfloat16
    count, rows = kept.shape[:2]

    def both(d, part=slice(None)):
        return kept[d, part].astype(f32) + got[d, part].astype(f32)

    if count != 4:
        total = both(0)
        for d in range(1, count):
            total = total + swap(both(d).astype(b16), "expert", d).astype(f32)
        return total.astype(b16), []
    upper, lower = slice(0, rows // 2), slice(rows // 2, rows)
    one = jnp.stack([both(1, upper), both(3, upper)]).astype(b16)
    two = jnp.stack([both(2, lower), both(3, lower)]).astype(b16)
    from_one, from_two = swap(one, "expert", 1), swap(two, "expert", 2)
    pass_two = (both(2, upper) + from_one[1].astype(f32)).astype(b16)
    pass_one = (both(1, lower) + from_two[1].astype(f32)).astype(b16)
    last_two, last_one = swap(pass_two, "expert", 2), swap(pass_one, "expert", 1)
    total = jnp.concatenate(
        [
            both(0, upper) + from_one[0].astype(f32) + last_two.astype(f32),
            both(0, lower) + from_two[0].astype(f32) + last_one.astype(f32),
        ]
    )
    return total.astype(b16), [one, two, pass_one, pass_two]


def on_device(
    tokens, routes, route_weights, norm_gain, final_gain, w_gate, w_up, w_down, head_weight, targets
):
    tok_rows, width = tokens.shape
    n_expert = lax.axis_size("expert")
    n_tensor = lax.axis_size("tensor")
    my_expert = lax.axis_index("expert")
    my_tensor = lax.axis_index("tensor")
    full_width = width * n_tensor
    own = tok_rows // n_tensor
    splits = 2 if own % 32 == 0 else 1
    sub = own // splits
    rows = sub * n_tensor
    vocab_part = head_weight.shape[1]

    parts = tokens.reshape(n_tensor, splits, sub, width)
    slices = [gather_near(parts[:, h].reshape(rows, width), "tensor") for h in range(splits)]
    gains = gather_near(jnp.stack([norm_gain, final_gain]), "tensor")
    pieces, raws = [], []
    after = []
    for h in range(splits):
        normed, raw = norm_rows(slices[h], gains, routes, route_weights, splits, h, after)
        plane = gather_plane(normed, "expert")
        pieces.append(plane + [swap(p, "seq", 1) for p in plane])
        raws.append(raw)
        after = plane[1:3]

    finals = []
    sent = [[], []]
    for h in range(splits):
        hidden = hidden_rows(pieces[h], w_gate, w_up, sent[0])
        kept, other = down_rows(hidden, w_down, 2, sent[1])
        got = swap(other, "seq", 1)
        shape = (n_expert, rows, full_width)
        total, moved = sum_plane(kept.reshape(shape), got.reshape(shape))
        sent = [moved[:2], moved[2:]]
        total = total.reshape(n_tensor, sub, full_width)
        mine = [lax.dynamic_index_in_dim(total, my_tensor, 0, False)]
        for d in range(1, n_tensor):
            out = lax.dynamic_index_in_dim(total, my_tensor ^ d, 0, False)
            mine.append(swap(out, "tensor", d))
        finals.append(final_rows(mine, raws[h], gains))

    start = (my_expert * n_tensor + my_tensor) * vocab_part
    local = (targets - start).astype(jnp.int32).reshape(n_expert, n_tensor, splits, sub)
    local = flip(flip(local, 0, my_expert), 1, my_tensor)
    head_rows = head_weight.T
    terms = []
    for h in range(splits):
        column = jnp.concatenate(gather_near(finals[h], "tensor"), axis=0)
        plane = gather_plane(column, "expert")
        term = head_terms(plane, head_rows, local[:, :, h].reshape(1, -1))
        terms.append(term[:3].reshape(3, n_expert, n_tensor, sub))
    terms = jnp.stack(terms, axis=3)
    joined = join_terms(
        [terms[:, :, 0]] + [swap(terms[:, :, d], "tensor", d) for d in range(1, n_tensor)]
    )
    joined = join_terms(
        [joined[:, 0]] + [swap(joined[:, d], "expert", d) for d in range(1, n_expert)]
    )
    return (joined[0] + jnp.log(joined[1]) - joined[2]).reshape(own)


def solution(mesh):
    return jax.shard_map(
        on_device,
        mesh=mesh,
        in_specs=(
            P(("seq", "expert"), "tensor"),
            P(("seq", "expert"), None),
            P(("seq", "expert"), None),
            P("tensor"),
            P("tensor"),
            P("expert", None, ("seq", "tensor")),
            P("expert", None, ("seq", "tensor")),
            P("expert", ("seq", "tensor"), None),
            P(None, ("expert", "tensor")),
            P("seq"),
        ),
        out_specs=P(("seq", "expert", "tensor")),
        check_vma=False,
    )
```

```python
import functools

import jax
import jax.numpy as jnp
from jax import lax
from jax.experimental import pallas as pl
from jax.experimental.pallas import tpu as pltpu
from jax.sharding import PartitionSpec as P

epsilon = 1e-05
LANES = 128
LARGEST = 512
MIB = 1024 * 1024
VMEM_BYTES = 56 * 1024 * 1024


def params(limit=VMEM_BYTES):
    return pltpu.CompilerParams(vmem_limit_bytes=limit)


def whole():
    return pl.BlockSpec(memory_space=pltpu.VMEM)


def anywhere():
    return pl.BlockSpec(memory_space=pl.ANY)


def swap(x, axis, distance):
    size = lax.axis_size(axis)
    return lax.ppermute(x, axis, [(i, i ^ distance) for i in range(size)])


def gather_near(x, axis):
    return [x] + [swap(x, axis, d) for d in range(1, lax.axis_size(axis))]


def gather_plane(x, axis):
    if lax.axis_size(axis) != 4:
        return gather_near(x, axis)
    half = x.shape[0] // 2
    one, two = swap(x, axis, 1), swap(x, axis, 2)
    return [x, one, two, swap(two[:half], axis, 1), swap(one[half:], axis, 2)]


def load_pieces(piece_refs, scratch, sems):
    copies = []
    start = 0
    for i in range(len(piece_refs)):
        count = piece_refs[i].shape[0]
        copies.append(
            pltpu.make_async_copy(piece_refs[i], scratch.at[pl.ds(start, count), :], sems.at[i])
        )
        start += count
    for copy in copies:
        copy.start()
    for copy in copies:
        copy.wait()


def split_three(x):
    high = lax.reduce_precision(x, 8, 7)
    middle = lax.reduce_precision(x - high, 8, 7)
    return jnp.stack([high, middle, x - high - middle])


def gain_row(ref, index):
    tail = ref[ref.shape[0] - 16 :, :].astype(jnp.float32)
    first = 3 * index
    return tail[first : first + 1] + tail[first + 1 : first + 2] + tail[first + 2 : first + 3]


def norm_kernel(splits, part, count, *refs):
    slices, gains = refs[:count], refs[count : 2 * count]
    routes_ref, weights_ref = refs[2 * count : 2 * count + 2]
    rows_ref, raw_ref = refs[-2:]
    rows = rows_ref.shape[0]
    width = slices[0].shape[1]
    full_width = width * count
    own_rows = rows // count
    me = lax.axis_index("tensor")
    total = jnp.zeros((rows, 1), jnp.float32)
    for piece in slices:
        value = piece[:rows, :].astype(jnp.float32)
        total = total + jnp.sum(value * value, axis=1, keepdims=True)
    scale = lax.rsqrt(total / full_width + epsilon)
    start = pl.multiple_of(me * own_rows, own_rows)
    for d in range(count):
        columns = pl.ds(pl.multiple_of((me ^ d) * width, width), width)
        value = slices[d][:rows, :].astype(jnp.float32)
        rows_ref[:, columns] = (value * scale * gain_row(gains[d], 0)).astype(jnp.bfloat16)
        raw_ref[:, columns] = slices[d][pl.ds(start, own_rows), :]
    lane = lax.broadcasted_iota(jnp.int32, (own_rows, LANES), 1)
    expert = lane // 3
    kind = lane - expert * 3
    for i in range(count):
        block = pl.ds((i * splits + part) * own_rows, own_rows)
        weight = jnp.zeros((own_rows, LANES), jnp.float32)
        for j in range(routes_ref.shape[1]):
            named = routes_ref[block, j : j + 1] == expert
            weight = weight + jnp.where(named, weights_ref[block, j : j + 1], 0.0)
        high = weight.astype(jnp.bfloat16).astype(jnp.float32)
        middle = (weight - high).astype(jnp.bfloat16).astype(jnp.float32)
        low = weight - high - middle
        value = jnp.where(kind == 0, high, jnp.where(kind == 1, middle, low))
        rows_ref[i * own_rows : (i + 1) * own_rows, full_width:] = value.astype(jnp.bfloat16)


def norm_rows(slices, gains, routes, route_weights, splits, part, rows, after):
    width = slices[0].shape[1]
    count = len(slices)
    full_width = width * count
    return pl.pallas_call(
        functools.partial(norm_kernel, splits, part, count),
        out_shape=(
            jax.ShapeDtypeStruct((rows, full_width + LANES), jnp.bfloat16),
            jax.ShapeDtypeStruct((rows // count, full_width), jnp.bfloat16),
        ),
        in_specs=[whole()] * (2 * count + 2) + [anywhere()] * len(after),
        out_specs=(whole(), whole()),
        compiler_params=params(6 * MIB),
        cost_estimate=pl.CostEstimate(
            flops=6 * rows * full_width, bytes_accessed=4 * rows * full_width, transcendentals=rows
        ),
        name="norm_rows",
    )(*slices, *gains, routes, route_weights, *after)


def stage_kernel(source_ref, target_ref, sem):
    copy = pltpu.make_async_copy(source_ref, target_ref, sem)
    copy.start()
    copy.wait()


def stage(weight):
    return pl.pallas_call(
        stage_kernel,
        out_shape=pltpu.VMEM(weight.shape, weight.dtype),
        in_specs=[anywhere()],
        out_specs=anywhere(),
        scratch_shapes=[pltpu.SemaphoreType.DMA],
        compiler_params=params(MIB),
        cost_estimate=pl.CostEstimate(
            flops=0, bytes_accessed=4 * weight.size, transcendentals=0
        ),
        name="stage",
    )(pltpu.with_memory_space_constraint(weight, pltpu.HBM))


def hidden_kernel(pieces, after, tile, *refs):
    piece_refs = refs[:pieces]
    gate_ref, up_ref = refs[pieces : pieces + 2]
    out_ref, rows_scr, weight_scr, gate_scr, sems, gate_sems = refs[pieces + 2 + after :]
    full_width, hidden_part = gate_ref.shape[1:]
    steps = hidden_part // tile

    def columns(i):
        return pl.ds(pl.multiple_of(i * tile, tile), tile)

    def fetch(i):
        slot = lax.rem(i, 2)
        return pltpu.make_async_copy(
            gate_ref.at[0, :, columns(i)], gate_scr.at[slot], gate_sems.at[slot]
        )

    fetch(0).start()
    load_pieces(piece_refs, rows_scr, sems)
    small = rows_scr[:, full_width:].astype(jnp.float32)
    lane = lax.broadcasted_iota(jnp.int32, small.shape, 1)
    first = lax.axis_index("expert") * 3
    mine = (lane >= first) & (lane < first + 3)
    weight = jnp.sum(jnp.where(mine, small, 0.0), axis=1, keepdims=True)
    weight_scr[...] = jnp.broadcast_to(0.5 * weight, weight_scr.shape)

    @pl.loop(0, steps)
    def _(i):
        @pl.when(i + 1 < steps)
        def _():
            fetch(i + 1).start()

        rows = rows_scr[:, :full_width]
        up = jnp.dot(rows, up_ref[0, :, columns(i)], preferred_element_type=jnp.float32)
        fetch(i).wait()
        gate_block = gate_scr[lax.rem(i, 2)]
        gate = jnp.dot(rows, gate_block, preferred_element_type=jnp.float32)
        hidden = gate * (1.0 + jnp.tanh(0.5 * gate)) * up * weight_scr[:, :1]
        out_ref[:, columns(i)] = hidden.astype(jnp.bfloat16)


def hidden_rows(pieces, w_gate, w_up, after):
    rows = sum(p.shape[0] for p in pieces)
    full_width, hidden = w_gate.shape[1:]
    tile = next(t for t in (256, 128, hidden) if hidden % t == 0)
    return pl.pallas_call(
        functools.partial(hidden_kernel, len(pieces), len(after), tile),
        out_shape=jax.ShapeDtypeStruct((rows, hidden), jnp.bfloat16),
        in_specs=[anywhere()] * (len(pieces) + 1) + [whole()] + [anywhere()] * len(after),
        out_specs=whole(),
        scratch_shapes=[
            pltpu.VMEM((rows, full_width + LANES), jnp.bfloat16),
            pltpu.VMEM((rows, LANES), jnp.float32),
            pltpu.VMEM((2, full_width, tile), jnp.bfloat16),
            pltpu.SemaphoreType.DMA((len(pieces),)),
            pltpu.SemaphoreType.DMA((2,)),
        ],
        compiler_params=params((8 + rows // 64) * MIB),
        cost_estimate=pl.CostEstimate(
            flops=4 * rows * full_width * hidden,
            bytes_accessed=2 * rows * (full_width + hidden),
            transcendentals=rows * hidden,
        ),
        name="hidden_rows",
    )(*pieces, w_gate, w_up, *after)


def down_kernel(start, hidden_ref, down_ref, *refs):
    out_ref = refs[-1]
    full_width = out_ref.shape[1]
    tile = 512 if full_width % 512 == 0 else full_width

    @pl.loop(0, full_width // tile)
    def _(i):
        columns = pl.ds(pl.multiple_of(i * tile, tile), tile)
        rows = hidden_ref[start : start + out_ref.shape[0], :]
        out = jnp.dot(rows, down_ref[0, :, columns], preferred_element_type=jnp.float32)
        out_ref[:, columns] = out.astype(jnp.bfloat16)


def down_rows(hidden, w_down, start, rows, after):
    depth, full_width = w_down.shape[1:]
    return pl.pallas_call(
        functools.partial(down_kernel, start),
        out_shape=jax.ShapeDtypeStruct((rows, full_width), jnp.bfloat16),
        in_specs=[whole()] * 2 + [anywhere()] * len(after),
        out_specs=whole(),
        compiler_params=params((4 + rows // 64) * MIB),
        cost_estimate=pl.CostEstimate(
            flops=2 * rows * depth * full_width,
            bytes_accessed=2 * rows * (depth + full_width),
            transcendentals=0,
        ),
        name="down_rows",
    )(hidden, w_down, *after)


def many_rows(pieces, w_gate, w_up, w_down):
    outs = []
    while pieces:
        count = 1
        while count < len(pieces) and sum(p.shape[0] for p in pieces[: count + 1]) <= LARGEST:
            count += 1
        hidden = hidden_rows(pieces[:count], w_gate, w_up, [])
        outs.append(down_rows(hidden, w_down, 0, hidden.shape[0], []))
        pieces = pieces[count:]
    return jnp.concatenate(outs)


def final_kernel(parts, gains_count, *refs):
    part_refs, raw_ref = refs[:parts], refs[parts]
    gains = refs[parts + 1 : parts + 1 + gains_count]
    out_ref, work = refs[parts + 1 + gains_count :]
    width = gains[0].shape[1]
    me = lax.axis_index("tensor")
    mixed = part_refs[0][...].astype(jnp.float32)
    for part in part_refs[1:]:
        mixed = mixed + part[...].astype(jnp.float32)
    residual = raw_ref[...].astype(jnp.float32) + mixed
    residual = residual.astype(jnp.bfloat16).astype(jnp.float32)
    total = jnp.sum(residual * residual, axis=1, keepdims=True)
    scale = lax.rsqrt(total / residual.shape[1] + epsilon)
    work[...] = residual * scale
    for d in range(gains_count):
        columns = pl.ds(pl.multiple_of((me ^ d) * width, width), width)
        out_ref[:, columns] = (work[:, columns] * gain_row(gains[d], 1)).astype(jnp.bfloat16)


def final_rows(parts, raw, gains):
    rows, full_width = raw.shape
    return pl.pallas_call(
        functools.partial(final_kernel, len(parts), len(gains)),
        out_shape=jax.ShapeDtypeStruct((rows, full_width), jnp.bfloat16),
        in_specs=[whole()] * (len(parts) + 1 + len(gains)),
        out_specs=whole(),
        scratch_shapes=[pltpu.VMEM((rows, full_width), jnp.float32)],
        compiler_params=params(6 * MIB),
        cost_estimate=pl.CostEstimate(
            flops=8 * rows * full_width, bytes_accessed=12 * rows * full_width, transcendentals=rows
        ),
        name="final_rows",
    )(*parts, raw, *gains)


def head_kernel(pieces, *refs):
    piece_refs = refs[:pieces]
    head_ref, target_ref, out_ref, rows_scr, sems = refs[pieces:]
    vocab_part = head_ref.shape[0]
    tile = 400 if vocab_part % 400 == 0 else vocab_part
    load_pieces(piece_refs, rows_scr, sems)
    lane = lax.broadcasted_iota(jnp.int32, out_ref.shape, 0)
    out_ref[...] = jnp.where(lane == 0, -jnp.inf, 0.0)

    @pl.loop(0, vocab_part // tile)
    def _(i):
        start = pl.multiple_of(i * tile, tile)
        logits = lax.dot_general(
            head_ref[pl.ds(start, tile), :],
            rows_scr[...],
            (((1,), (1,)), ((), ())),
            preferred_element_type=jnp.float32,
        )
        word = lax.broadcasted_iota(jnp.int32, logits.shape, 0) + start
        old_top, old_total = out_ref[0:1, :], out_ref[1:2, :]
        top = jnp.maximum(old_top, jnp.max(logits, axis=0, keepdims=True))
        out_ref[0:1, :] = top
        out_ref[1:2, :] = old_total * jnp.exp(old_top - top) + jnp.sum(
            jnp.exp(logits - top), axis=0, keepdims=True
        )
        hit = word == target_ref[...]
        out_ref[2:3, :] += jnp.sum(jnp.where(hit, logits, 0.0), axis=0, keepdims=True)


def head_terms(pieces, head_rows, targets):
    rows = sum(p.shape[0] for p in pieces)
    vocab_part, full_width = head_rows.shape
    return pl.pallas_call(
        functools.partial(head_kernel, len(pieces)),
        out_shape=jax.ShapeDtypeStruct((8, rows), jnp.float32),
        in_specs=[anywhere()] * len(pieces) + [whole()] * 2,
        out_specs=whole(),
        scratch_shapes=[
            pltpu.VMEM((rows, full_width), jnp.bfloat16),
            pltpu.SemaphoreType.DMA((len(pieces),)),
        ],
        compiler_params=params((6 + rows // 64) * MIB),
        cost_estimate=pl.CostEstimate(
            flops=2 * rows * full_width * vocab_part,
            bytes_accessed=2 * full_width * rows,
            transcendentals=rows * vocab_part,
        ),
        name="head_terms",
    )(*pieces, head_rows, targets)


def join_terms(parts):
    top = functools.reduce(jnp.maximum, [p[0] for p in parts])
    total = sum(p[1] * jnp.exp(p[0] - top) for p in parts)
    target = sum(p[2] for p in parts)
    return jnp.stack([top, total, target])


def flip(x, axis, index):
    size = x.shape[axis]
    bit = 1
    while bit < size:
        shape = x.shape[:axis] + (size // (2 * bit), 2, bit) + x.shape[axis + 1 :]
        turned = jnp.flip(x.reshape(shape), axis + 1).reshape(x.shape)
        x = jnp.where((index & bit) != 0, turned, x)
        bit *= 2
    return x


def sum_plane(kept, got):
    f32, b16 = jnp.float32, jnp.bfloat16
    count, rows = kept.shape[:2]

    def both(d, part=slice(None)):
        return kept[d, part].astype(f32) + got[d, part].astype(f32)

    if count != 4:
        total = both(0)
        for d in range(1, count):
            total = total + swap(both(d).astype(b16), "expert", d).astype(f32)
        return total.astype(b16), []
    upper, lower = slice(0, rows // 2), slice(rows // 2, rows)
    one = jnp.stack([both(1, upper), both(3, upper)]).astype(b16)
    two = jnp.stack([both(2, lower), both(3, lower)]).astype(b16)
    from_one, from_two = swap(one, "expert", 1), swap(two, "expert", 2)
    pass_two = (both(2, upper) + from_one[1].astype(f32)).astype(b16)
    pass_one = (both(1, lower) + from_two[1].astype(f32)).astype(b16)
    last_two, last_one = swap(pass_two, "expert", 2), swap(pass_one, "expert", 1)
    total = jnp.concatenate(
        [
            both(0, upper) + from_one[0].astype(f32) + last_two.astype(f32),
            both(0, lower) + from_two[0].astype(f32) + last_one.astype(f32),
        ]
    )
    return total.astype(b16), [one, two, pass_one, pass_two]


def on_device(
    tokens, routes, route_weights, norm_gain, final_gain, w_gate, w_up, w_down, head_weight, targets
):
    tok_rows, width = tokens.shape
    n_expert = lax.axis_size("expert")
    n_tensor = lax.axis_size("tensor")
    my_expert = lax.axis_index("expert")
    my_tensor = lax.axis_index("tensor")
    full_width = width * n_tensor
    own = tok_rows // n_tensor
    splits = 2 if own % 32 == 0 else 1
    sub = own // splits
    rows = sub * n_tensor
    vocab_part = head_weight.shape[1]

    parts = tokens.reshape(n_tensor, splits, sub, width)
    rider = jnp.concatenate([split_three(norm_gain), split_three(final_gain)])
    rider = jnp.pad(rider, ((0, 16 - rider.shape[0]), (0, 0))).astype(jnp.bfloat16)
    slices = []
    for h in range(splits):
        part = parts[:, h].reshape(rows, width)
        slices.append(
            gather_near(part if h else jnp.concatenate([part, rider]), "tensor")
        )
    gains = slices[0]
    planes, raws = [], []
    after = []
    for h in range(splits):
        normed, raw = norm_rows(slices[h], gains, routes, route_weights, splits, h, rows, after)
        plane = gather_plane(normed, "expert")
        planes.append(plane)
        raws.append(raw)
        after = plane[1:3]

    w_gate = pltpu.with_memory_space_constraint(w_gate, pltpu.HBM)
    staged = stage(w_up)
    finals = []
    begun, moved = [], []
    last = None
    for h in range(splits):
        nearer, later = [], []
        if h + 1 < splits:
            nearer, later = planes[h + 1][:1], planes[h + 1][1:3]
        away = [swap(p, "seq", 1) for p in planes[h]]
        if 2 * n_expert * rows <= LARGEST:
            hidden = hidden_rows(planes[h] + away, w_gate, w_up if h else staged, begun + nearer)
            hidden = pltpu.with_memory_space_constraint(hidden, pltpu.VMEM)
            half = hidden.shape[0] // 2
            other = down_rows(hidden, w_down, half, half, moved + later)
            kept = down_rows(hidden, w_down, 0, half, [] if last is None else [last])
        else:
            kept, other = many_rows(planes[h], w_gate, w_up, w_down), many_rows(
                away, w_gate, w_up, w_down
            )
        got = swap(other, "seq", 1)
        shape = (n_expert, rows, full_width)
        total, sums = sum_plane(kept.reshape(shape), got.reshape(shape))
        begun, moved = sums[:2], sums[2:]
        last = total
        total = total.reshape(n_tensor, sub, full_width)
        mine = [lax.dynamic_index_in_dim(total, my_tensor, 0, False)]
        for d in range(1, n_tensor):
            out = lax.dynamic_index_in_dim(total, my_tensor ^ d, 0, False)
            mine.append(swap(out, "tensor", d))
        finals.append(final_rows(mine, raws[h], gains))

    start = (my_expert * n_tensor + my_tensor) * vocab_part
    local = (targets - start).astype(jnp.int32).reshape(n_expert, n_tensor, splits, sub)
    local = flip(flip(local, 0, my_expert), 1, my_tensor)
    head_rows = pltpu.with_memory_space_constraint(head_weight.T, pltpu.VMEM)
    terms = []
    for h in range(splits):
        column = jnp.concatenate(gather_near(finals[h], "tensor"), axis=0)
        plane = gather_plane(column, "expert")
        term = head_terms(plane, head_rows, local[:, :, h].reshape(1, -1))
        terms.append(term[:3].reshape(3, n_expert, n_tensor, sub))
    terms = jnp.stack(terms, axis=3)
    joined = join_terms(
        [terms[:, :, 0]] + [swap(terms[:, :, d], "tensor", d) for d in range(1, n_tensor)]
    )
    joined = join_terms(
        [joined[:, 0]] + [swap(joined[:, d], "expert", d) for d in range(1, n_expert)]
    )
    return (joined[0] + jnp.log(joined[1]) - joined[2]).reshape(own)


def solution(mesh):
    return jax.shard_map(
        on_device,
        mesh=mesh,
        in_specs=(
            P(("seq", "expert"), "tensor"),
            P(("seq", "expert"), None),
            P(("seq", "expert"), None),
            P("tensor"),
            P("tensor"),
            P("expert", None, ("seq", "tensor")),
            P("expert", None, ("seq", "tensor")),
            P("expert", ("seq", "tensor"), None),
            P(None, ("expert", "tensor")),
            P("seq"),
        ),
        out_specs=P(("seq", "expert", "tensor")),
        check_vma=False,
    )
```

```python
import functools

import jax
import jax.numpy as jnp
from jax import lax
from jax.experimental import pallas as pl
from jax.experimental.pallas import tpu as pltpu
from jax.sharding import PartitionSpec as P

epsilon = 1e-05
LANES = 128
LARGEST = 512
MIB = 1024 * 1024
VMEM_BYTES = 56 * 1024 * 1024


def params(limit=VMEM_BYTES):
    return pltpu.CompilerParams(vmem_limit_bytes=limit)


def whole():
    return pl.BlockSpec(memory_space=pltpu.VMEM)


def anywhere():
    return pl.BlockSpec(memory_space=pl.ANY)


def swap(x, axis, distance):
    size = lax.axis_size(axis)
    return lax.ppermute(x, axis, [(i, i ^ distance) for i in range(size)])


def gather_near(x, axis):
    return [x] + [swap(x, axis, d) for d in range(1, lax.axis_size(axis))]


def gather_plane(x, axis):
    if lax.axis_size(axis) != 4:
        return gather_near(x, axis)
    half = x.shape[0] // 2
    one, two = swap(x, axis, 1), swap(x, axis, 2)
    return [x, one, two, swap(two[:half], axis, 1), swap(one[half:], axis, 2)]


def load_pieces(piece_refs, scratch, sems):
    copies = []
    start = 0
    for i in range(len(piece_refs)):
        count = piece_refs[i].shape[0]
        copies.append(
            pltpu.make_async_copy(piece_refs[i], scratch.at[pl.ds(start, count), :], sems.at[i])
        )
        start += count
    for copy in copies:
        copy.start()
    for copy in copies:
        copy.wait()


def split_three(x):
    high = lax.reduce_precision(x, 8, 7)
    middle = lax.reduce_precision(x - high, 8, 7)
    return jnp.stack([high, middle, x - high - middle])


def gain_row(ref, index):
    tail = ref[ref.shape[0] - 16 :, :].astype(jnp.float32)
    first = 3 * index
    return tail[first : first + 1] + tail[first + 1 : first + 2] + tail[first + 2 : first + 3]


def norm_kernel(splits, part, count, *refs):
    slices, gains = refs[:count], refs[count : 2 * count]
    routes_ref, weights_ref = refs[2 * count : 2 * count + 2]
    rows_ref, raw_ref = refs[-2:]
    rows = rows_ref.shape[0]
    width = slices[0].shape[1]
    full_width = width * count
    own_rows = rows // count
    me = lax.axis_index("tensor")
    total = jnp.zeros((rows, 1), jnp.float32)
    for piece in slices:
        value = piece[:rows, :].astype(jnp.float32)
        total = total + jnp.sum(value * value, axis=1, keepdims=True)
    scale = lax.rsqrt(total / full_width + epsilon)
    start = pl.multiple_of(me * own_rows, own_rows)
    for d in range(count):
        columns = pl.ds(pl.multiple_of((me ^ d) * width, width), width)
        value = slices[d][:rows, :].astype(jnp.float32)
        rows_ref[:, columns] = (value * scale * gain_row(gains[d], 0)).astype(jnp.bfloat16)
        raw_ref[:, columns] = slices[d][pl.ds(start, own_rows), :]
    lane = lax.broadcasted_iota(jnp.int32, (own_rows, LANES), 1)
    expert = lane // 3
    kind = lane - expert * 3
    for i in range(count):
        block = pl.ds((i * splits + part) * own_rows, own_rows)
        weight = jnp.zeros((own_rows, LANES), jnp.float32)
        for j in range(routes_ref.shape[1]):
            named = routes_ref[block, j : j + 1] == expert
            weight = weight + jnp.where(named, weights_ref[block, j : j + 1], 0.0)
        high = weight.astype(jnp.bfloat16).astype(jnp.float32)
        middle = (weight - high).astype(jnp.bfloat16).astype(jnp.float32)
        low = weight - high - middle
        value = jnp.where(kind == 0, high, jnp.where(kind == 1, middle, low))
        rows_ref[i * own_rows : (i + 1) * own_rows, full_width:] = value.astype(jnp.bfloat16)


def norm_rows(slices, gains, routes, route_weights, splits, part, rows, after):
    width = slices[0].shape[1]
    count = len(slices)
    full_width = width * count
    return pl.pallas_call(
        functools.partial(norm_kernel, splits, part, count),
        out_shape=(
            jax.ShapeDtypeStruct((rows, full_width + LANES), jnp.bfloat16),
            jax.ShapeDtypeStruct((rows // count, full_width), jnp.bfloat16),
        ),
        in_specs=[whole()] * (2 * count + 2) + [anywhere()] * len(after),
        out_specs=(whole(), whole()),
        compiler_params=params(6 * MIB),
        cost_estimate=pl.CostEstimate(
            flops=6 * rows * full_width, bytes_accessed=4 * rows * full_width, transcendentals=rows
        ),
        name="norm_rows",
    )(*slices, *gains, routes, route_weights, *after)


def hidden_kernel(pieces, after, tile, first, steps, *refs):
    piece_refs = refs[:pieces]
    weight_refs = refs[pieces : pieces + 2]
    out_ref, rows_scr, route_scr, weight_scr, sems, weight_sems = refs[pieces + 2 + after :]
    full_width = weight_scr.shape[2]

    def fetch(i, act):
        slot = lax.rem(i, 2)
        columns = pl.ds(pl.multiple_of((first + i) * tile, tile), tile)
        for j in range(2):
            act(
                pltpu.make_async_copy(
                    weight_refs[j].at[0, :, columns],
                    weight_scr.at[j, slot],
                    weight_sems.at[j, slot],
                )
            )

    fetch(0, lambda copy: copy.start())
    load_pieces(piece_refs, rows_scr, sems)
    small = rows_scr[:, full_width:].astype(jnp.float32)
    lane = lax.broadcasted_iota(jnp.int32, small.shape, 1)
    start = lax.axis_index("expert") * 3
    mine = (lane >= start) & (lane < start + 3)
    weight = jnp.sum(jnp.where(mine, small, 0.0), axis=1, keepdims=True)
    route_scr[...] = jnp.broadcast_to(0.5 * weight, route_scr.shape)

    @pl.loop(0, steps)
    def _(i):
        fetch(i, lambda copy: copy.wait())

        @pl.when(i + 1 < steps)
        def _():
            fetch(i + 1, lambda copy: copy.start())

        slot = lax.rem(i, 2)
        rows = rows_scr[:, :full_width]
        gate = jnp.dot(rows, weight_scr[0, slot], preferred_element_type=jnp.float32)
        up = jnp.dot(rows, weight_scr[1, slot], preferred_element_type=jnp.float32)
        hidden = gate * (1.0 + jnp.tanh(0.5 * gate)) * up * route_scr[:, :1]
        columns = pl.ds(pl.multiple_of(i * tile, tile), tile)
        out_ref[:, columns] = hidden.astype(jnp.bfloat16)


def tile_of(weight):
    hidden = weight.shape[2]
    return next(t for t in (256, 128, hidden) if hidden % t == 0)


def hidden_rows(pieces, w_gate, w_up, after, first, steps, tile):
    rows = sum(p.shape[0] for p in pieces)
    full_width = w_gate.shape[1]
    hidden = steps * tile
    return pl.pallas_call(
        functools.partial(hidden_kernel, len(pieces), len(after), tile, first, steps),
        out_shape=jax.ShapeDtypeStruct((rows, hidden), jnp.bfloat16),
        in_specs=[anywhere()] * (len(pieces) + 2 + len(after)),
        out_specs=whole(),
        scratch_shapes=[
            pltpu.VMEM((rows, full_width + LANES), jnp.bfloat16),
            pltpu.VMEM((rows, LANES), jnp.float32),
            pltpu.VMEM((2, 2, full_width, tile), jnp.bfloat16),
            pltpu.SemaphoreType.DMA((len(pieces),)),
            pltpu.SemaphoreType.DMA((2, 2)),
        ],
        compiler_params=params((14 + rows // 64) * MIB),
        cost_estimate=pl.CostEstimate(
            flops=4 * rows * full_width * hidden,
            bytes_accessed=4 * full_width * hidden + 2 * rows * (full_width + hidden),
            transcendentals=rows * hidden,
        ),
        name="hidden_rows",
    )(*pieces, w_gate, w_up, *after)


def hidden_dots(pieces, w_gate, w_up):
    full_width = w_gate.shape[1]
    joined = jnp.concatenate(pieces)
    rows = joined[:, :full_width]
    small = joined[:, full_width:].astype(jnp.float32)
    lane = jnp.arange(LANES, dtype=jnp.int32)
    start = lax.axis_index("expert") * 3
    weight = jnp.sum(jnp.where((lane >= start) & (lane < start + 3), small, 0.0), axis=1)
    gate = jnp.dot(rows, w_gate[0], preferred_element_type=jnp.float32)
    up = jnp.dot(rows, w_up[0], preferred_element_type=jnp.float32)
    return (jax.nn.silu(gate) * up * weight[:, None]).astype(jnp.bfloat16)


def down_kernel(start, count, *refs):
    hidden_refs, down_ref, out_ref = refs[:count], refs[count], refs[-1]
    full_width = out_ref.shape[1]
    tile = 512 if full_width % 512 == 0 else full_width

    @pl.loop(0, full_width // tile)
    def _(i):
        columns = pl.ds(pl.multiple_of(i * tile, tile), tile)
        out = None
        depth = 0
        for hidden_ref in hidden_refs:
            rows = hidden_ref[start : start + out_ref.shape[0], :]
            block = down_ref[0, depth : depth + rows.shape[1], columns]
            term = jnp.dot(rows, block, preferred_element_type=jnp.float32)
            out = term if out is None else out + term
            depth += rows.shape[1]
        out_ref[:, columns] = out.astype(jnp.bfloat16)


def down_rows(hidden, w_down, start, rows, after):
    depth, full_width = w_down.shape[1:]
    hidden = [pltpu.with_memory_space_constraint(part, pltpu.VMEM) for part in hidden]
    return pl.pallas_call(
        functools.partial(down_kernel, start, len(hidden)),
        out_shape=jax.ShapeDtypeStruct((rows, full_width), jnp.bfloat16),
        in_specs=[whole()] * (len(hidden) + 1) + [anywhere()] * len(after),
        out_specs=whole(),
        compiler_params=params((4 + rows // 64) * MIB),
        cost_estimate=pl.CostEstimate(
            flops=2 * rows * depth * full_width,
            bytes_accessed=2 * rows * (depth + full_width),
            transcendentals=0,
        ),
        name="down_rows",
    )(*hidden, w_down, *after)


def many_rows(pieces, w_gate, w_up, w_down):
    outs = []
    tile = tile_of(w_gate)
    steps = w_gate.shape[2] // tile
    while pieces:
        count = 1
        while count < len(pieces) and sum(p.shape[0] for p in pieces[: count + 1]) <= LARGEST:
            count += 1
        hidden = hidden_rows(pieces[:count], w_gate, w_up, [], 0, steps, tile)
        outs.append(down_rows([hidden], w_down, 0, hidden.shape[0], []))
        pieces = pieces[count:]
    return jnp.concatenate(outs)


def final_kernel(parts, gains_count, *refs):
    part_refs, raw_ref = refs[:parts], refs[parts]
    gains = refs[parts + 1 : parts + 1 + gains_count]
    out_ref, work = refs[parts + 1 + gains_count :]
    width = gains[0].shape[1]
    me = lax.axis_index("tensor")
    mixed = part_refs[0][...].astype(jnp.float32)
    for part in part_refs[1:]:
        mixed = mixed + part[...].astype(jnp.float32)
    residual = raw_ref[...].astype(jnp.float32) + mixed
    residual = residual.astype(jnp.bfloat16).astype(jnp.float32)
    total = jnp.sum(residual * residual, axis=1, keepdims=True)
    scale = lax.rsqrt(total / residual.shape[1] + epsilon)
    work[...] = residual * scale
    for d in range(gains_count):
        columns = pl.ds(pl.multiple_of((me ^ d) * width, width), width)
        out_ref[:, columns] = (work[:, columns] * gain_row(gains[d], 1)).astype(jnp.bfloat16)


def final_rows(parts, raw, gains):
    rows, full_width = raw.shape
    return pl.pallas_call(
        functools.partial(final_kernel, len(parts), len(gains)),
        out_shape=jax.ShapeDtypeStruct((rows, full_width), jnp.bfloat16),
        in_specs=[whole()] * (len(parts) + 1 + len(gains)),
        out_specs=whole(),
        scratch_shapes=[pltpu.VMEM((rows, full_width), jnp.float32)],
        compiler_params=params(6 * MIB),
        cost_estimate=pl.CostEstimate(
            flops=8 * rows * full_width, bytes_accessed=12 * rows * full_width, transcendentals=rows
        ),
        name="final_rows",
    )(*parts, raw, *gains)


def head_kernel(pieces, tile, *refs):
    piece_refs = refs[:pieces]
    head_ref, target_ref, out_ref, rows_scr, head_scr, sems, head_sems = refs[pieces:]
    steps = head_ref.shape[0] // tile

    def fetch(i):
        return pltpu.make_async_copy(
            head_ref.at[pl.ds(pl.multiple_of(i * tile, tile), tile), :],
            head_scr.at[i],
            head_sems.at[i],
        )

    fetch(0).start()
    load_pieces(piece_refs, rows_scr, sems)
    for i in range(1, steps):
        fetch(i).start()
    lane = lax.broadcasted_iota(jnp.int32, out_ref.shape, 0)
    out_ref[...] = jnp.where(lane == 0, -jnp.inf, 0.0)

    @pl.loop(0, steps)
    def _(i):
        fetch(i).wait()
        logits = lax.dot_general(
            head_scr[i],
            rows_scr[...],
            (((1,), (1,)), ((), ())),
            preferred_element_type=jnp.float32,
        )
        word = lax.broadcasted_iota(jnp.int32, logits.shape, 0) + i * tile
        old_top, old_total = out_ref[0:1, :], out_ref[1:2, :]
        top = jnp.maximum(old_top, jnp.max(logits, axis=0, keepdims=True))
        out_ref[0:1, :] = top
        out_ref[1:2, :] = old_total * jnp.exp(old_top - top) + jnp.sum(
            jnp.exp(logits - top), axis=0, keepdims=True
        )
        hit = word == target_ref[...]
        out_ref[2:3, :] += jnp.sum(jnp.where(hit, logits, 0.0), axis=0, keepdims=True)


def head_terms(pieces, head_rows, targets):
    rows = sum(p.shape[0] for p in pieces)
    vocab_part, full_width = head_rows.shape
    tile = next(t for t in (400, 200, 80, 8, vocab_part) if vocab_part % t == 0)
    return pl.pallas_call(
        functools.partial(head_kernel, len(pieces), tile),
        out_shape=jax.ShapeDtypeStruct((8, rows), jnp.float32),
        in_specs=[anywhere()] * (len(pieces) + 1) + [whole()],
        out_specs=whole(),
        scratch_shapes=[
            pltpu.VMEM((rows, full_width), jnp.bfloat16),
            pltpu.VMEM((vocab_part // tile, tile, full_width), jnp.bfloat16),
            pltpu.SemaphoreType.DMA((len(pieces),)),
            pltpu.SemaphoreType.DMA((vocab_part // tile,)),
        ],
        compiler_params=params((22 + rows // 64) * MIB),
        cost_estimate=pl.CostEstimate(
            flops=2 * rows * full_width * vocab_part,
            bytes_accessed=2 * full_width * (vocab_part + rows),
            transcendentals=rows * vocab_part,
        ),
        name="head_terms",
    )(*pieces, head_rows, targets)


def join_terms(parts):
    top = functools.reduce(jnp.maximum, [p[0] for p in parts])
    total = sum(p[1] * jnp.exp(p[0] - top) for p in parts)
    target = sum(p[2] for p in parts)
    return jnp.stack([top, total, target])


def flip(x, axis, index):
    size = x.shape[axis]
    bit = 1
    while bit < size:
        shape = x.shape[:axis] + (size // (2 * bit), 2, bit) + x.shape[axis + 1 :]
        turned = jnp.flip(x.reshape(shape), axis + 1).reshape(x.shape)
        x = jnp.where((index & bit) != 0, turned, x)
        bit *= 2
    return x


def sum_plane(kept, got):
    f32, b16 = jnp.float32, jnp.bfloat16
    count, rows = kept.shape[:2]

    def both(d, part=slice(None)):
        return kept[d, part].astype(f32) + got[d, part].astype(f32)

    if count != 4:
        total = both(0)
        for d in range(1, count):
            total = total + swap(both(d).astype(b16), "expert", d).astype(f32)
        return total.astype(b16), []
    upper, lower = slice(0, rows // 2), slice(rows // 2, rows)
    one = jnp.stack([both(1, upper), both(3, upper)]).astype(b16)
    two = jnp.stack([both(2, lower), both(3, lower)]).astype(b16)
    from_one, from_two = swap(one, "expert", 1), swap(two, "expert", 2)
    pass_two = (both(2, upper) + from_one[1].astype(f32)).astype(b16)
    pass_one = (both(1, lower) + from_two[1].astype(f32)).astype(b16)
    last_two, last_one = swap(pass_two, "expert", 2), swap(pass_one, "expert", 1)
    total = jnp.concatenate(
        [
            both(0, upper) + from_one[0].astype(f32) + last_two.astype(f32),
            both(0, lower) + from_two[0].astype(f32) + last_one.astype(f32),
        ]
    )
    return total.astype(b16), [one, two, pass_one, pass_two]


def on_device(
    tokens, routes, route_weights, norm_gain, final_gain, w_gate, w_up, w_down, head_weight, targets
):
    tok_rows, width = tokens.shape
    n_expert = lax.axis_size("expert")
    n_tensor = lax.axis_size("tensor")
    my_expert = lax.axis_index("expert")
    my_tensor = lax.axis_index("tensor")
    full_width = width * n_tensor
    own = tok_rows // n_tensor
    splits = 2 if own % 32 == 0 else 1
    sub = own // splits
    rows = sub * n_tensor
    vocab_part = head_weight.shape[1]

    parts = tokens.reshape(n_tensor, splits, sub, width)
    rider = jnp.concatenate([split_three(norm_gain), split_three(final_gain)])
    rider = jnp.pad(rider, ((0, 16 - rider.shape[0]), (0, 0))).astype(jnp.bfloat16)
    slices = []
    for h in range(splits):
        part = parts[:, h].reshape(rows, width)
        slices.append(
            gather_near(part if h else jnp.concatenate([part, rider]), "tensor")
        )
    gains = slices[0]
    planes, raws = [], []
    after = []
    for h in range(splits):
        normed, raw = norm_rows(slices[h], gains, routes, route_weights, splits, h, rows, after)
        plane = gather_plane(normed, "expert")
        planes.append(plane)
        raws.append(raw)
        after = plane[1:3]

    finals = []
    begun, moved = [], []
    last = None
    for h in range(splits):
        later = planes[h + 1][1:3] if h + 1 < splits else []
        away = [swap(p, "seq", 1) for p in planes[h]]
        if 2 * n_expert * rows <= LARGEST:
            half = n_expert * rows
            everything = planes[h] + away
            if h == 0:
                hidden = [hidden_dots(everything, w_gate, w_up)]
            else:
                tile = tile_of(w_gate)
                steps = w_gate.shape[2] // tile
                cut = (steps + 1) // 2
                hidden = [
                    hidden_rows(everything, w_gate, w_up, begun, 0, cut, tile),
                    hidden_rows(everything, w_gate, w_up, moved, cut, steps - cut, tile),
                ]
            other = down_rows(hidden, w_down, half, half, later + ([] if last is None else [last]))
            kept = down_rows(hidden, w_down, 0, half, [])
        else:
            kept, other = many_rows(planes[h], w_gate, w_up, w_down), many_rows(
                away, w_gate, w_up, w_down
            )
        got = swap(other, "seq", 1)
        shape = (n_expert, rows, full_width)
        total, sums = sum_plane(kept.reshape(shape), got.reshape(shape))
        begun, moved = sums[:2], sums[2:]
        last = total
        total = total.reshape(n_tensor, sub, full_width)
        mine = [lax.dynamic_index_in_dim(total, my_tensor, 0, False)]
        for d in range(1, n_tensor):
            out = lax.dynamic_index_in_dim(total, my_tensor ^ d, 0, False)
            mine.append(swap(out, "tensor", d))
        finals.append(final_rows(mine, raws[h], gains))

    start = (my_expert * n_tensor + my_tensor) * vocab_part
    local = (targets - start).astype(jnp.int32).reshape(n_expert, n_tensor, splits, sub)
    local = flip(flip(local, 0, my_expert), 1, my_tensor)
    head_rows = pltpu.with_memory_space_constraint(head_weight.T, pltpu.HBM)
    terms = []
    for h in range(splits):
        column = jnp.concatenate(gather_near(finals[h], "tensor"), axis=0)
        plane = gather_plane(column, "expert")
        term = head_terms(plane, head_rows, local[:, :, h].reshape(1, -1))
        terms.append(term[:3].reshape(3, n_expert, n_tensor, sub))
    terms = jnp.stack(terms, axis=3)
    joined = join_terms(
        [terms[:, :, 0]] + [swap(terms[:, :, d], "tensor", d) for d in range(1, n_tensor)]
    )
    joined = join_terms(
        [joined[:, 0]] + [swap(joined[:, d], "expert", d) for d in range(1, n_expert)]
    )
    return (joined[0] + jnp.log(joined[1]) - joined[2]).reshape(own)


def solution(mesh):
    return jax.shard_map(
        on_device,
        mesh=mesh,
        in_specs=(
            P(("seq", "expert"), "tensor"),
            P(("seq", "expert"), None),
            P(("seq", "expert"), None),
            P("tensor"),
            P("tensor"),
            P("expert", None, ("seq", "tensor")),
            P("expert", None, ("seq", "tensor")),
            P("expert", ("seq", "tensor"), None),
            P(None, ("expert", "tensor")),
            P("seq"),
        ),
        out_specs=P(("seq", "expert", "tensor")),
        check_vma=False,
    )
```

```python
import functools

import jax
import jax.numpy as jnp
from jax import lax
from jax.experimental import pallas as pl
from jax.experimental.pallas import tpu as pltpu
from jax.sharding import PartitionSpec as P

epsilon = 1e-05
LANES = 128
LARGEST = 512
MIB = 1024 * 1024
VMEM_BYTES = 56 * 1024 * 1024


def params(limit=VMEM_BYTES):
    return pltpu.CompilerParams(vmem_limit_bytes=limit)


def whole():
    return pl.BlockSpec(memory_space=pltpu.VMEM)


def anywhere():
    return pl.BlockSpec(memory_space=pl.ANY)


def swap(x, axis, distance):
    size = lax.axis_size(axis)
    return lax.ppermute(x, axis, [(i, i ^ distance) for i in range(size)])


def gather_near(x, axis):
    return [x] + [swap(x, axis, d) for d in range(1, lax.axis_size(axis))]


def gather_plane(x, axis):
    if lax.axis_size(axis) != 4:
        return gather_near(x, axis)
    half = x.shape[0] // 2
    one, two = swap(x, axis, 1), swap(x, axis, 2)
    return [x, one, two, swap(two[:half], axis, 1), swap(one[half:], axis, 2)]


def load_pieces(piece_refs, scratch, sems):
    copies = []
    start = 0
    for i in range(len(piece_refs)):
        count = piece_refs[i].shape[0]
        copies.append(
            pltpu.make_async_copy(piece_refs[i], scratch.at[pl.ds(start, count), :], sems.at[i])
        )
        start += count
    for copy in copies:
        copy.start()
    for copy in copies:
        copy.wait()


def split_three(x):
    high = lax.reduce_precision(x, 8, 7)
    middle = lax.reduce_precision(x - high, 8, 7)
    return jnp.stack([high, middle, x - high - middle])


def gain_row(ref, index):
    tail = ref[ref.shape[0] - 16 :, :].astype(jnp.float32)
    first = 3 * index
    return tail[first : first + 1] + tail[first + 1 : first + 2] + tail[first + 2 : first + 3]


def norm_kernel(splits, part, count, after, *refs):
    slices, gains = refs[:count], refs[count : 2 * count]
    routes_ref, weights_ref = refs[2 * count : 2 * count + 2]
    rest = refs[2 * count + 2 + after :]
    handing_on = len(rest) > 2
    if handing_on:
        next_ref, rows_ref, raw_ref, out_ref, sem = rest
        copy = pltpu.make_async_copy(next_ref, out_ref, sem)
        copy.start()
    else:
        rows_ref, raw_ref = rest
    rows = rows_ref.shape[0]
    width = slices[0].shape[1]
    full_width = width * count
    own_rows = rows // count
    me = lax.axis_index("tensor")
    total = jnp.zeros((rows, 1), jnp.float32)
    for piece in slices:
        value = piece[:rows, :].astype(jnp.float32)
        total = total + jnp.sum(value * value, axis=1, keepdims=True)
    scale = lax.rsqrt(total / full_width + epsilon)
    start = pl.multiple_of(me * own_rows, own_rows)
    for d in range(count):
        columns = pl.ds(pl.multiple_of((me ^ d) * width, width), width)
        value = slices[d][:rows, :].astype(jnp.float32)
        rows_ref[:, columns] = (value * scale * gain_row(gains[d], 0)).astype(jnp.bfloat16)
        raw_ref[:, columns] = slices[d][pl.ds(start, own_rows), :]
    lane = lax.broadcasted_iota(jnp.int32, (own_rows, LANES), 1)
    expert = lane // 3
    kind = lane - expert * 3
    for i in range(count):
        block = pl.ds((i * splits + part) * own_rows, own_rows)
        weight = jnp.zeros((own_rows, LANES), jnp.float32)
        for j in range(routes_ref.shape[1]):
            named = routes_ref[block, j : j + 1] == expert
            weight = weight + jnp.where(named, weights_ref[block, j : j + 1], 0.0)
        high = weight.astype(jnp.bfloat16).astype(jnp.float32)
        middle = (weight - high).astype(jnp.bfloat16).astype(jnp.float32)
        low = weight - high - middle
        value = jnp.where(kind == 0, high, jnp.where(kind == 1, middle, low))
        rows_ref[i * own_rows : (i + 1) * own_rows, full_width:] = value.astype(jnp.bfloat16)
    if handing_on:
        copy.wait()


def norm_rows(slices, gains, routes, route_weights, splits, part, rows, after, following):
    width = slices[0].shape[1]
    count = len(slices)
    full_width = width * count
    return pl.pallas_call(
        functools.partial(norm_kernel, splits, part, count, len(after)),
        out_shape=(
            jax.ShapeDtypeStruct((rows, full_width + LANES), jnp.bfloat16),
            jax.ShapeDtypeStruct((rows // count, full_width), jnp.bfloat16),
        )
        + tuple(jax.ShapeDtypeStruct(f.shape, f.dtype) for f in following),
        in_specs=[whole()] * (2 * count + 2) + [anywhere()] * (len(after) + len(following)),
        out_specs=(whole(), whole()) + (anywhere(),) * len(following),
        scratch_shapes=[pltpu.SemaphoreType.DMA] * len(following),
        compiler_params=params(6 * MIB),
        cost_estimate=pl.CostEstimate(
            flops=6 * rows * full_width, bytes_accessed=4 * rows * full_width, transcendentals=rows
        ),
        name="norm_rows",
    )(*slices, *gains, routes, route_weights, *after, *following)


def hidden_kernel(pieces, after, tile, first, steps, *refs):
    piece_refs = refs[:pieces]
    weight_refs = refs[pieces : pieces + 2]
    out_ref, rows_scr, route_scr, weight_scr, sems, weight_sems = refs[pieces + 2 + after :]
    full_width = weight_scr.shape[2]

    def fetch(i, act):
        slot = lax.rem(i, 2)
        columns = pl.ds(pl.multiple_of((first + i) * tile, tile), tile)
        for j in range(2):
            act(
                pltpu.make_async_copy(
                    weight_refs[j].at[0, :, columns],
                    weight_scr.at[j, slot],
                    weight_sems.at[j, slot],
                )
            )

    fetch(0, lambda copy: copy.start())
    load_pieces(piece_refs, rows_scr, sems)
    small = rows_scr[:, full_width:].astype(jnp.float32)
    lane = lax.broadcasted_iota(jnp.int32, small.shape, 1)
    start = lax.axis_index("expert") * 3
    mine = (lane >= start) & (lane < start + 3)
    weight = jnp.sum(jnp.where(mine, small, 0.0), axis=1, keepdims=True)
    route_scr[...] = jnp.broadcast_to(0.5 * weight, route_scr.shape)

    @pl.loop(0, steps)
    def _(i):
        fetch(i, lambda copy: copy.wait())

        @pl.when(i + 1 < steps)
        def _():
            fetch(i + 1, lambda copy: copy.start())

        slot = lax.rem(i, 2)
        rows = rows_scr[:, :full_width]
        gate = jnp.dot(rows, weight_scr[0, slot], preferred_element_type=jnp.float32)
        up = jnp.dot(rows, weight_scr[1, slot], preferred_element_type=jnp.float32)
        hidden = gate * (1.0 + jnp.tanh(0.5 * gate)) * up * route_scr[:, :1]
        columns = pl.ds(pl.multiple_of(i * tile, tile), tile)
        out_ref[:, columns] = hidden.astype(jnp.bfloat16)


def tile_of(weight):
    hidden = weight.shape[2]
    return next(t for t in (256, 128, hidden) if hidden % t == 0)


def hidden_rows(pieces, w_gate, w_up, after, first, steps, tile):
    rows = sum(p.shape[0] for p in pieces)
    full_width = w_gate.shape[1]
    hidden = steps * tile
    return pl.pallas_call(
        functools.partial(hidden_kernel, len(pieces), len(after), tile, first, steps),
        out_shape=jax.ShapeDtypeStruct((rows, hidden), jnp.bfloat16),
        in_specs=[anywhere()] * (len(pieces) + 2 + len(after)),
        out_specs=whole(),
        scratch_shapes=[
            pltpu.VMEM((rows, full_width + LANES), jnp.bfloat16),
            pltpu.VMEM((rows, LANES), jnp.float32),
            pltpu.VMEM((2, 2, full_width, tile), jnp.bfloat16),
            pltpu.SemaphoreType.DMA((len(pieces),)),
            pltpu.SemaphoreType.DMA((2, 2)),
        ],
        compiler_params=params((14 + rows // 64) * MIB),
        cost_estimate=pl.CostEstimate(
            flops=4 * rows * full_width * hidden,
            bytes_accessed=4 * full_width * hidden + 2 * rows * (full_width + hidden),
            transcendentals=rows * hidden,
        ),
        name="hidden_rows",
    )(*pieces, w_gate, w_up, *after)


def down_kernel(start, count, *refs):
    hidden_refs, down_ref, out_ref = refs[:count], refs[count], refs[-1]
    full_width = out_ref.shape[1]
    tile = 512 if full_width % 512 == 0 else full_width

    @pl.loop(0, full_width // tile)
    def _(i):
        columns = pl.ds(pl.multiple_of(i * tile, tile), tile)
        out = None
        depth = 0
        for hidden_ref in hidden_refs:
            rows = hidden_ref[start : start + out_ref.shape[0], :]
            block = down_ref[0, depth : depth + rows.shape[1], columns]
            term = jnp.dot(rows, block, preferred_element_type=jnp.float32)
            out = term if out is None else out + term
            depth += rows.shape[1]
        out_ref[:, columns] = out.astype(jnp.bfloat16)


def down_rows(hidden, w_down, start, rows, after):
    depth, full_width = w_down.shape[1:]
    hidden = [pltpu.with_memory_space_constraint(part, pltpu.VMEM) for part in hidden]
    return pl.pallas_call(
        functools.partial(down_kernel, start, len(hidden)),
        out_shape=jax.ShapeDtypeStruct((rows, full_width), jnp.bfloat16),
        in_specs=[whole()] * (len(hidden) + 1) + [anywhere()] * len(after),
        out_specs=whole(),
        compiler_params=params((4 + rows // 64) * MIB),
        cost_estimate=pl.CostEstimate(
            flops=2 * rows * depth * full_width,
            bytes_accessed=2 * rows * (depth + full_width),
            transcendentals=0,
        ),
        name="down_rows",
    )(*hidden, w_down, *after)


def many_rows(pieces, w_gate, w_up, w_down):
    outs = []
    tile = tile_of(w_gate)
    steps = w_gate.shape[2] // tile
    while pieces:
        count = 1
        while count < len(pieces) and sum(p.shape[0] for p in pieces[: count + 1]) <= LARGEST:
            count += 1
        hidden = hidden_rows(pieces[:count], w_gate, w_up, [], 0, steps, tile)
        outs.append(down_rows([hidden], w_down, 0, hidden.shape[0], []))
        pieces = pieces[count:]
    return jnp.concatenate(outs)


def final_kernel(parts, gains_count, after, *refs):
    part_refs, gain_refs = refs[: parts + 1], refs[parts + 1 : parts + 1 + gains_count]
    out_ref, rows_scr, gains_scr, work, sems = refs[parts + 1 + gains_count + after :]
    width = gains_scr.shape[2]
    me = lax.axis_index("tensor")
    copies = [
        pltpu.make_async_copy(part_refs[i], rows_scr.at[i], sems.at[i]) for i in range(parts + 1)
    ]
    for d in range(gains_count):
        tail = gain_refs[d].at[pl.ds(gain_refs[d].shape[0] - 16, 16), :]
        copies.append(pltpu.make_async_copy(tail, gains_scr.at[d], sems.at[parts + 1 + d]))
    for copy in copies:
        copy.start()
    for copy in copies:
        copy.wait()
    mixed = rows_scr[0].astype(jnp.float32)
    for i in range(1, parts):
        mixed = mixed + rows_scr[i].astype(jnp.float32)
    residual = rows_scr[parts].astype(jnp.float32) + mixed
    residual = residual.astype(jnp.bfloat16).astype(jnp.float32)
    total = jnp.sum(residual * residual, axis=1, keepdims=True)
    scale = lax.rsqrt(total / residual.shape[1] + epsilon)
    work[...] = residual * scale
    for d in range(gains_count):
        columns = pl.ds(pl.multiple_of((me ^ d) * width, width), width)
        out_ref[:, columns] = (work[:, columns] * gain_row(gains_scr.at[d], 1)).astype(
            jnp.bfloat16
        )


def final_rows(parts, raw, gains, after):
    rows, full_width = raw.shape
    count = len(parts) + 1 + len(gains)
    return pl.pallas_call(
        functools.partial(final_kernel, len(parts), len(gains), len(after)),
        out_shape=jax.ShapeDtypeStruct((rows, full_width), jnp.bfloat16),
        in_specs=[anywhere()] * (count + len(after)),
        out_specs=whole(),
        scratch_shapes=[
            pltpu.VMEM((len(parts) + 1, rows, full_width), jnp.bfloat16),
            pltpu.VMEM((len(gains), 16, gains[0].shape[1]), jnp.bfloat16),
            pltpu.VMEM((rows, full_width), jnp.float32),
            pltpu.SemaphoreType.DMA((count,)),
        ],
        compiler_params=params(6 * MIB),
        cost_estimate=pl.CostEstimate(
            flops=8 * rows * full_width, bytes_accessed=12 * rows * full_width, transcendentals=rows
        ),
        name="final_rows",
    )(*parts, raw, *gains, *after)


def head_kernel(pieces, tile, sub, *refs):
    piece_refs = refs[:pieces]
    head_ref, target_ref, out_ref, rows_scr, head_scr, sems, head_sems = refs[pieces:]
    vocab_part = head_ref.shape[0]
    steps = vocab_part // tile
    my_expert, my_tensor = lax.axis_index("expert"), lax.axis_index("tensor")
    n_tensor = lax.axis_size("tensor")

    def fetch(i):
        return pltpu.make_async_copy(
            head_ref.at[pl.ds(pl.multiple_of(i * tile, tile), tile), :],
            head_scr.at[i],
            head_sems.at[i],
        )

    copies = []
    for piece_ref in piece_refs:
        for start in range(0, piece_ref.shape[0], sub):
            far_expert, far_tensor = divmod(len(copies), n_tensor)
            block = (my_expert ^ far_expert) * n_tensor + (my_tensor ^ far_tensor)
            copies.append(
                pltpu.make_async_copy(
                    piece_ref.at[pl.ds(start, sub), :],
                    rows_scr.at[pl.ds(pl.multiple_of(block * sub, sub), sub), :],
                    sems.at[len(copies)],
                )
            )
    fetch(0).start()
    for copy in copies:
        copy.start()
    for i in range(1, steps):
        fetch(i).start()
    for copy in copies:
        copy.wait()
    lane = lax.broadcasted_iota(jnp.int32, out_ref.shape, 0)
    out_ref[...] = jnp.where(lane == 0, -jnp.inf, 0.0)
    targets = target_ref[...] - (my_expert * n_tensor + my_tensor) * vocab_part

    @pl.loop(0, steps)
    def _(i):
        fetch(i).wait()
        logits = lax.dot_general(
            head_scr[i],
            rows_scr[...],
            (((1,), (1,)), ((), ())),
            preferred_element_type=jnp.float32,
        )
        word = lax.broadcasted_iota(jnp.int32, logits.shape, 0) + i * tile
        old_top, old_total = out_ref[0:1, :], out_ref[1:2, :]
        top = jnp.maximum(old_top, jnp.max(logits, axis=0, keepdims=True))
        out_ref[0:1, :] = top
        out_ref[1:2, :] = old_total * jnp.exp(old_top - top) + jnp.sum(
            jnp.exp(logits - top), axis=0, keepdims=True
        )
        hit = word == targets
        out_ref[2:3, :] += jnp.sum(jnp.where(hit, logits, 0.0), axis=0, keepdims=True)


def head_terms(pieces, head_rows, targets, sub):
    rows = sum(p.shape[0] for p in pieces)
    vocab_part, full_width = head_rows.shape
    tile = next(t for t in (400, 200, 80, 8, vocab_part) if vocab_part % t == 0)
    return pl.pallas_call(
        functools.partial(head_kernel, len(pieces), tile, sub),
        out_shape=jax.ShapeDtypeStruct((8, rows), jnp.float32),
        in_specs=[anywhere()] * (len(pieces) + 1) + [whole()],
        out_specs=whole(),
        scratch_shapes=[
            pltpu.VMEM((rows, full_width), jnp.bfloat16),
            pltpu.VMEM((vocab_part // tile, tile, full_width), jnp.bfloat16),
            pltpu.SemaphoreType.DMA((rows // sub,)),
            pltpu.SemaphoreType.DMA((vocab_part // tile,)),
        ],
        compiler_params=params((22 + rows // 64) * MIB),
        cost_estimate=pl.CostEstimate(
            flops=2 * rows * full_width * vocab_part,
            bytes_accessed=2 * full_width * (vocab_part + rows),
            transcendentals=rows * vocab_part,
        ),
        name="head_terms",
    )(*pieces, head_rows, targets)


def join_terms(parts):
    top = functools.reduce(jnp.maximum, [p[0] for p in parts])
    total = sum(p[1] * jnp.exp(p[0] - top) for p in parts)
    target = sum(p[2] for p in parts)
    return jnp.stack([top, total, target])


def join_axis(terms, axis, place, me):
    def of(d):
        return lax.dynamic_index_in_dim(terms, me ^ d, place, False)

    return join_terms([of(0)] + [swap(of(d), axis, d) for d in range(1, lax.axis_size(axis))])


def pack_kernel(kept_ref, got_ref, one_ref, two_ref, home_ref, side_ref):
    rows = home_ref.shape[0]
    half = rows // 2

    def both(d, first):
        block = slice(d * rows + first, d * rows + first + half)
        return kept_ref[block, :].astype(jnp.float32) + got_ref[block, :].astype(jnp.float32)

    one_ref[:half, :] = both(1, 0).astype(jnp.bfloat16)
    one_ref[half:, :] = both(3, 0).astype(jnp.bfloat16)
    two_ref[:half, :] = both(2, half).astype(jnp.bfloat16)
    two_ref[half:, :] = both(3, half).astype(jnp.bfloat16)
    home_ref[:half, :] = both(0, 0)
    home_ref[half:, :] = both(0, half)
    side_ref[0] = both(1, half)
    side_ref[1] = both(2, 0)


def pass_kernel(side_ref, one_ref, two_ref, *refs):
    pass_one_ref, pass_two_ref = refs[-2:]
    half = pass_one_ref.shape[0]
    pass_one_ref[...] = (side_ref[0] + two_ref[half:, :].astype(jnp.float32)).astype(jnp.bfloat16)
    pass_two_ref[...] = (side_ref[1] + one_ref[half:, :].astype(jnp.float32)).astype(jnp.bfloat16)


def total_kernel(count, home_ref, one_ref, two_ref, last_one_ref, last_two_ref, *refs):
    outs, work = refs[-count - 1 : -1], refs[-1]
    half = last_one_ref.shape[0]
    sub = outs[0].shape[0]
    me = lax.axis_index("tensor")
    upper = one_ref[:half, :].astype(jnp.float32) + last_two_ref[...].astype(jnp.float32)
    lower = two_ref[:half, :].astype(jnp.float32) + last_one_ref[...].astype(jnp.float32)
    work[:half, :] = home_ref[:half, :] + upper
    work[half:, :] = home_ref[half:, :] + lower
    for d in range(count):
        block = pl.ds(pl.multiple_of((me ^ d) * sub, sub), sub)
        outs[d][...] = work[block, :].astype(jnp.bfloat16)


def small_call(kernel, name, inputs, after, outs, scratch, limit):
    size = sum(x.size * x.dtype.itemsize for x in inputs)
    return pl.pallas_call(
        kernel,
        out_shape=tuple(jax.ShapeDtypeStruct(*out) for out in outs),
        in_specs=[whole()] * len(inputs) + [anywhere()] * len(after),
        out_specs=(whole(),) * len(outs),
        scratch_shapes=scratch,
        compiler_params=params(limit),
        cost_estimate=pl.CostEstimate(flops=size, bytes_accessed=2 * size, transcendentals=0),
        name=name,
    )(*inputs, *after)


def sum_plane(kept, got, rows, after_pass, after_total):
    f32, b16 = jnp.float32, jnp.bfloat16
    n_tensor = lax.axis_size("tensor")
    count, full_width = kept.shape[0] // rows, kept.shape[1]
    half = rows // 2
    sub = rows // n_tensor
    if count == 4 and half % 16 == 0 and sub % 16 == 0:
        one, two, home, side = small_call(
            pack_kernel,
            "pack",
            [kept, got],
            [],
            [((rows, full_width), b16)] * 2
            + [((rows, full_width), f32), ((2, half, full_width), f32)],
            [],
            10 * MIB,
        )
        from_one, from_two = swap(one, "expert", 1), swap(two, "expert", 2)
        pass_one, pass_two = small_call(
            pass_kernel,
            "pass_on",
            [side, from_one, from_two],
            after_pass,
            [((half, full_width), b16)] * 2,
            [],
            6 * MIB,
        )
        last_one, last_two = swap(pass_one, "expert", 1), swap(pass_two, "expert", 2)
        pieces = small_call(
            functools.partial(total_kernel, n_tensor),
            "total",
            [home, from_one, from_two, last_one, last_two],
            after_total,
            [((sub, full_width), b16)] * n_tensor,
            [pltpu.VMEM((rows, full_width), f32)],
            8 * MIB,
        )
        return list(pieces), [one, two], [pass_one, pass_two]
    both = (kept.astype(f32) + got.astype(f32)).reshape(count, rows, full_width)
    total = both[0]
    for d in range(1, count):
        total = total + swap(both[d].astype(b16), "expert", d).astype(f32)
    total = total.astype(b16).reshape(n_tensor, sub, full_width)
    me = lax.axis_index("tensor")
    pieces = [lax.dynamic_index_in_dim(total, me ^ d, 0, False) for d in range(n_tensor)]
    return pieces, [], []


def on_device(
    tokens, routes, route_weights, norm_gain, final_gain, w_gate, w_up, w_down, head_weight, targets
):
    tok_rows, width = tokens.shape
    n_expert = lax.axis_size("expert")
    n_tensor = lax.axis_size("tensor")
    my_expert = lax.axis_index("expert")
    my_tensor = lax.axis_index("tensor")
    full_width = width * n_tensor
    own = tok_rows // n_tensor
    splits = 2 if own % 32 == 0 else 1
    sub = own // splits
    rows = sub * n_tensor

    parts = tokens.reshape(n_tensor, splits, sub, width)
    rider = jnp.concatenate([split_three(norm_gain), split_three(final_gain)])
    rider = jnp.pad(rider, ((0, 16 - rider.shape[0]), (0, 0))).astype(jnp.bfloat16)
    blocks = [parts[:, h].reshape(rows, width) for h in range(splits)]
    gains = slices = gather_near(jnp.concatenate([blocks[0], rider]), "tensor")
    planes, raws = [], []
    after = []
    for h in range(splits):
        following = blocks[h + 1 : h + 2]
        normed, raw, *block = norm_rows(
            slices, gains, routes, route_weights, splits, h, rows, after, following
        )
        if block:
            slices = gather_near(block[0], "tensor")
        plane = gather_plane(normed, "expert")
        planes.append(plane)
        raws.append(raw)
        after = plane[3:]

    w_gate = pltpu.with_memory_space_constraint(w_gate, pltpu.HBM)
    w_up = pltpu.with_memory_space_constraint(w_up, pltpu.HBM)
    head_rows = pltpu.with_memory_space_constraint(head_weight.T, pltpu.HBM)
    target_rows = targets.reshape(n_expert, n_tensor, splits, sub)
    terms = []
    steps = {}
    for h in range(splits):
        later = planes[h + 1][1:3] if h + 1 < splits else []
        away = [swap(p, "seq", 1) for p in planes[h]]
        if 2 * n_expert * rows <= LARGEST:
            half = n_expert * rows
            everything = planes[h] + away
            tile = tile_of(w_gate)
            count = w_gate.shape[2] // tile
            cuts = [0, (count + 1) // 2, count - 1, count] if h else [0, count]
            ties = [steps.get(key, []) for key in ("packed", "passed", "totals")]
            hidden = [
                hidden_rows(
                    everything, w_gate, w_up, ties[i], cuts[i], cuts[i + 1] - cuts[i], tile
                )
                for i in range(len(cuts) - 1)
            ]
            other = down_rows(hidden, w_down, half, half, later)
            kept = down_rows(hidden, w_down, 0, half, steps.get("final", []))
        else:
            kept, other = many_rows(planes[h], w_gate, w_up, w_down), many_rows(
                away, w_gate, w_up, w_down
            )
        got = swap(other, "seq", 1)
        totals, packed, passed = sum_plane(
            kept, got, rows, steps.get("column", []), steps.get("near", [])
        )
        mine = totals[:1] + [swap(totals[d], "tensor", d) for d in range(1, n_tensor)]
        final = final_rows(mine, raws[h], gains, steps.get("far", []))
        column = gather_near(final, "tensor")
        plane = gather_plane(jnp.concatenate(column, axis=0), "expert")
        wanted = target_rows[:, :, h].reshape(1, -1)
        term = head_terms(plane, head_rows, wanted, sub)
        terms.append(term[:3].reshape(3, n_expert, n_tensor, sub))
        steps = {
            "packed": packed,
            "passed": passed,
            "totals": totals,
            "final": [final],
            "column": column[1:],
            "near": plane[1:3],
            "far": plane[3:],
        }
    terms = jnp.stack(terms, axis=3)
    joined = join_axis(terms, "tensor", 2, my_tensor)
    joined = join_axis(joined, "expert", 1, my_expert)
    return (joined[0] + jnp.log(joined[1]) - joined[2]).reshape(own)


def solution(mesh):
    return jax.shard_map(
        on_device,
        mesh=mesh,
        in_specs=(
            P(("seq", "expert"), "tensor"),
            P(("seq", "expert"), None),
            P(("seq", "expert"), None),
            P("tensor"),
            P("tensor"),
            P("expert", None, ("seq", "tensor")),
            P("expert", None, ("seq", "tensor")),
            P("expert", ("seq", "tensor"), None),
            P(None, ("expert", "tensor")),
            P("seq"),
        ),
        out_specs=P(("seq", "expert", "tensor")),
        check_vma=False,
    )
```

```python
import functools

import jax
import jax.numpy as jnp
from jax import lax
from jax.experimental import pallas as pl
from jax.experimental.pallas import tpu as pltpu
from jax.sharding import PartitionSpec as P

epsilon = 1e-05
LANES = 128
LARGEST = 512
MIB = 1024 * 1024
VMEM_BYTES = 56 * 1024 * 1024


def params(limit=VMEM_BYTES):
    return pltpu.CompilerParams(vmem_limit_bytes=limit)


def whole():
    return pl.BlockSpec(memory_space=pltpu.VMEM)


def anywhere():
    return pl.BlockSpec(memory_space=pl.ANY)


def swap(x, axis, distance):
    size = lax.axis_size(axis)
    return lax.ppermute(x, axis, [(i, i ^ distance) for i in range(size)])


def gather_near(x, axis):
    return [x] + [swap(x, axis, d) for d in range(1, lax.axis_size(axis))]


def gather_plane(x, axis, after):
    if lax.axis_size(axis) != 4:
        return gather_near(x, axis)
    half = x.shape[0] // 2
    one, two = swap(x, axis, 1), swap(x, axis, 2)
    upper, lower = move_rows([two, one], [(0, 0, half, 0, 0), (1, half, half, 1, 0)], after)
    return [x, one, two, swap(upper, axis, 1), swap(lower, axis, 2)]


def move_kernel(sources, targets, moves, *refs):
    out_refs, sems = refs[-targets - 1 : -1], refs[-1]
    copies = []
    for i, (source, start, count, target, place) in enumerate(moves):
        copies.append(
            pltpu.make_async_copy(
                refs[source].at[pl.ds(start, count), :],
                out_refs[target].at[pl.ds(place, count), :],
                sems.at[i],
            )
        )
    for copy in copies:
        copy.start()
    for copy in copies:
        copy.wait()


def move_rows(arrays, moves, after):
    targets = 1 + max(m[3] for m in moves)
    sizes = [sum(m[2] for m in moves if m[3] == t) for t in range(targets)]
    size = sum(sizes) * arrays[0].shape[1]
    return pl.pallas_call(
        functools.partial(move_kernel, len(arrays), targets, moves),
        out_shape=tuple(
            jax.ShapeDtypeStruct((rows, arrays[0].shape[1]), arrays[0].dtype) for rows in sizes
        ),
        in_specs=[anywhere()] * (len(arrays) + len(after)),
        out_specs=(anywhere(),) * targets,
        scratch_shapes=[pltpu.SemaphoreType.DMA((len(moves),))],
        compiler_params=params(MIB),
        cost_estimate=pl.CostEstimate(flops=0, bytes_accessed=4 * size, transcendentals=0),
        name="move_rows",
    )(*arrays, *after)


def stack_rows(arrays, after):
    moves = []
    place = 0
    for i, x in enumerate(arrays):
        moves.append((i, 0, x.shape[0], 0, place))
        place += x.shape[0]
    return move_rows(arrays, moves, after)[0]


def load_pieces(piece_refs, scratch, sems, then):
    copies = []
    start = 0
    for i in range(len(piece_refs)):
        count = piece_refs[i].shape[0]
        copies.append(
            pltpu.make_async_copy(piece_refs[i], scratch.at[pl.ds(start, count), :], sems.at[i])
        )
        start += count
    for copy in copies:
        copy.start()
    then()
    for copy in copies:
        copy.wait()


def split_three(x):
    high = lax.reduce_precision(x, 8, 7)
    middle = lax.reduce_precision(x - high, 8, 7)
    return jnp.stack([high, middle, x - high - middle])


def gain_row(ref, index):
    tail = ref[ref.shape[0] - 16 :, :].astype(jnp.float32)
    first = 3 * index
    return tail[first : first + 1] + tail[first + 1 : first + 2] + tail[first + 2 : first + 3]


def norm_kernel(splits, part, count, after, *refs):
    slices, gains = refs[:count], refs[count : 2 * count]
    routes_ref, weights_ref = refs[2 * count : 2 * count + 2]
    rest = refs[2 * count + 2 + after :]
    handing_on = len(rest) > 2
    if handing_on:
        next_ref, rows_ref, raw_ref, out_ref, sem = rest
        copy = pltpu.make_async_copy(next_ref, out_ref, sem)
        copy.start()
    else:
        rows_ref, raw_ref = rest
    rows = rows_ref.shape[0]
    width = slices[0].shape[1]
    full_width = width * count
    own_rows = rows // count
    me = lax.axis_index("tensor")
    total = jnp.zeros((rows, 1), jnp.float32)
    for piece in slices:
        value = piece[:rows, :].astype(jnp.float32)
        total = total + jnp.sum(value * value, axis=1, keepdims=True)
    scale = lax.rsqrt(total / full_width + epsilon)
    start = pl.multiple_of(me * own_rows, own_rows)
    for d in range(count):
        columns = pl.ds(pl.multiple_of((me ^ d) * width, width), width)
        value = slices[d][:rows, :].astype(jnp.float32)
        rows_ref[:, columns] = (value * scale * gain_row(gains[d], 0)).astype(jnp.bfloat16)
        raw_ref[:, columns] = slices[d][pl.ds(start, own_rows), :]
    lane = lax.broadcasted_iota(jnp.int32, (own_rows, LANES), 1)
    expert = lane // 3
    kind = lane - expert * 3
    for i in range(count):
        block = pl.ds((i * splits + part) * own_rows, own_rows)
        weight = jnp.zeros((own_rows, LANES), jnp.float32)
        for j in range(routes_ref.shape[1]):
            named = routes_ref[block, j : j + 1] == expert
            weight = weight + jnp.where(named, weights_ref[block, j : j + 1], 0.0)
        high = weight.astype(jnp.bfloat16).astype(jnp.float32)
        middle = (weight - high).astype(jnp.bfloat16).astype(jnp.float32)
        low = weight - high - middle
        value = jnp.where(kind == 0, high, jnp.where(kind == 1, middle, low))
        rows_ref[i * own_rows : (i + 1) * own_rows, full_width:] = value.astype(jnp.bfloat16)
    if handing_on:
        copy.wait()


def norm_rows(slices, gains, routes, route_weights, splits, part, rows, after, following):
    width = slices[0].shape[1]
    count = len(slices)
    full_width = width * count
    return pl.pallas_call(
        functools.partial(norm_kernel, splits, part, count, len(after)),
        out_shape=(
            jax.ShapeDtypeStruct((rows, full_width + LANES), jnp.bfloat16),
            jax.ShapeDtypeStruct((rows // count, full_width), jnp.bfloat16),
        )
        + tuple(jax.ShapeDtypeStruct(f.shape, f.dtype) for f in following),
        in_specs=[whole()] * (2 * count + 2) + [anywhere()] * (len(after) + len(following)),
        out_specs=(whole(), whole()) + (anywhere(),) * len(following),
        scratch_shapes=[pltpu.SemaphoreType.DMA] * len(following),
        compiler_params=params(6 * MIB),
        cost_estimate=pl.CostEstimate(
            flops=6 * rows * full_width, bytes_accessed=4 * rows * full_width, transcendentals=rows
        ),
        name="norm_rows",
    )(*slices, *gains, routes, route_weights, *after, *following)


def hidden_kernel(pieces, after, tile, first, steps, *refs):
    piece_refs = refs[:pieces]
    weight_refs = refs[pieces : pieces + 2]
    out_ref, rows_scr, route_scr, weight_scr, sems, weight_sems = refs[pieces + 2 + after :]
    full_width = weight_scr.shape[2]

    def fetch(i, act):
        slot = lax.rem(i, 2)
        columns = pl.ds(pl.multiple_of((first + i) * tile, tile), tile)
        for j in range(2):
            act(
                pltpu.make_async_copy(
                    weight_refs[j].at[0, :, columns],
                    weight_scr.at[j, slot],
                    weight_sems.at[j, slot],
                )
            )

    load_pieces(piece_refs, rows_scr, sems, lambda: fetch(0, lambda copy: copy.start()))
    small = rows_scr[:, full_width:].astype(jnp.float32)
    lane = lax.broadcasted_iota(jnp.int32, small.shape, 1)
    start = lax.axis_index("expert") * 3
    mine = (lane >= start) & (lane < start + 3)
    weight = jnp.sum(jnp.where(mine, small, 0.0), axis=1, keepdims=True)
    route_scr[...] = jnp.broadcast_to(0.5 * weight, route_scr.shape)

    @pl.loop(0, steps)
    def _(i):
        fetch(i, lambda copy: copy.wait())

        @pl.when(i + 1 < steps)
        def _():
            fetch(i + 1, lambda copy: copy.start())

        slot = lax.rem(i, 2)
        rows = rows_scr[:, :full_width]
        gate = jnp.dot(rows, weight_scr[0, slot], preferred_element_type=jnp.float32)
        up = jnp.dot(rows, weight_scr[1, slot], preferred_element_type=jnp.float32)
        hidden = gate * (1.0 + jnp.tanh(0.5 * gate)) * up * route_scr[:, :1]
        columns = pl.ds(pl.multiple_of(i * tile, tile), tile)
        out_ref[:, columns] = hidden.astype(jnp.bfloat16)


def tile_of(weight):
    hidden = weight.shape[2]
    return next(t for t in (256, 128, hidden) if hidden % t == 0)


def hidden_rows(pieces, w_gate, w_up, after, first, steps, tile):
    rows = sum(p.shape[0] for p in pieces)
    full_width = w_gate.shape[1]
    hidden = steps * tile
    return pl.pallas_call(
        functools.partial(hidden_kernel, len(pieces), len(after), tile, first, steps),
        out_shape=jax.ShapeDtypeStruct((rows, hidden), jnp.bfloat16),
        in_specs=[anywhere()] * (len(pieces) + 2 + len(after)),
        out_specs=whole(),
        scratch_shapes=[
            pltpu.VMEM((rows, full_width + LANES), jnp.bfloat16),
            pltpu.VMEM((rows, LANES), jnp.float32),
            pltpu.VMEM((2, 2, full_width, tile), jnp.bfloat16),
            pltpu.SemaphoreType.DMA((len(pieces),)),
            pltpu.SemaphoreType.DMA((2, 2)),
        ],
        compiler_params=params((14 + rows // 64) * MIB),
        cost_estimate=pl.CostEstimate(
            flops=4 * rows * full_width * hidden,
            bytes_accessed=4 * full_width * hidden + 2 * rows * (full_width + hidden),
            transcendentals=rows * hidden,
        ),
        name="hidden_rows",
    )(*pieces, w_gate, w_up, *after)


def down_kernel(start, count, *refs):
    hidden_refs, down_ref, out_ref = refs[:count], refs[count], refs[-1]
    full_width = out_ref.shape[1]
    tile = 512 if full_width % 512 == 0 else full_width

    @pl.loop(0, full_width // tile)
    def _(i):
        columns = pl.ds(pl.multiple_of(i * tile, tile), tile)
        out = None
        depth = 0
        for hidden_ref in hidden_refs:
            rows = hidden_ref[start : start + out_ref.shape[0], :]
            block = down_ref[0, depth : depth + rows.shape[1], columns]
            term = jnp.dot(rows, block, preferred_element_type=jnp.float32)
            out = term if out is None else out + term
            depth += rows.shape[1]
        out_ref[:, columns] = out.astype(jnp.bfloat16)


def down_rows(hidden, w_down, start, rows, after):
    depth, full_width = w_down.shape[1:]
    hidden = [pltpu.with_memory_space_constraint(part, pltpu.VMEM) for part in hidden]
    return pl.pallas_call(
        functools.partial(down_kernel, start, len(hidden)),
        out_shape=jax.ShapeDtypeStruct((rows, full_width), jnp.bfloat16),
        in_specs=[whole()] * (len(hidden) + 1) + [anywhere()] * len(after),
        out_specs=whole(),
        compiler_params=params((4 + rows // 64) * MIB),
        cost_estimate=pl.CostEstimate(
            flops=2 * rows * depth * full_width,
            bytes_accessed=2 * rows * (depth + full_width),
            transcendentals=0,
        ),
        name="down_rows",
    )(*hidden, w_down, *after)


def many_rows(pieces, w_gate, w_up, w_down):
    outs = []
    tile = tile_of(w_gate)
    steps = w_gate.shape[2] // tile
    while pieces:
        count = 1
        while count < len(pieces) and sum(p.shape[0] for p in pieces[: count + 1]) <= LARGEST:
            count += 1
        hidden = hidden_rows(pieces[:count], w_gate, w_up, [], 0, steps, tile)
        outs.append(down_rows([hidden], w_down, 0, hidden.shape[0], []))
        pieces = pieces[count:]
    return jnp.concatenate(outs)


def final_kernel(parts, gains_count, after, *refs):
    part_refs, gain_refs = refs[: parts + 1], refs[parts + 1 : parts + 1 + gains_count]
    out_ref, rows_scr, gains_scr, work, sems = refs[parts + 1 + gains_count + after :]
    width = gains_scr.shape[2]
    me = lax.axis_index("tensor")
    copies = [
        pltpu.make_async_copy(part_refs[i], rows_scr.at[i], sems.at[i]) for i in range(parts + 1)
    ]
    for d in range(gains_count):
        tail = gain_refs[d].at[pl.ds(gain_refs[d].shape[0] - 16, 16), :]
        copies.append(pltpu.make_async_copy(tail, gains_scr.at[d], sems.at[parts + 1 + d]))
    for copy in copies:
        copy.start()
    for copy in copies:
        copy.wait()
    mixed = rows_scr[0].astype(jnp.float32)
    for i in range(1, parts):
        mixed = mixed + rows_scr[i].astype(jnp.float32)
    residual = rows_scr[parts].astype(jnp.float32) + mixed
    residual = residual.astype(jnp.bfloat16).astype(jnp.float32)
    total = jnp.sum(residual * residual, axis=1, keepdims=True)
    scale = lax.rsqrt(total / residual.shape[1] + epsilon)
    work[...] = residual * scale
    for d in range(gains_count):
        columns = pl.ds(pl.multiple_of((me ^ d) * width, width), width)
        out_ref[:, columns] = (work[:, columns] * gain_row(gains_scr.at[d], 1)).astype(
            jnp.bfloat16
        )


def final_rows(parts, raw, gains, after):
    rows, full_width = raw.shape
    count = len(parts) + 1 + len(gains)
    return pl.pallas_call(
        functools.partial(final_kernel, len(parts), len(gains), len(after)),
        out_shape=jax.ShapeDtypeStruct((rows, full_width), jnp.bfloat16),
        in_specs=[anywhere()] * (count + len(after)),
        out_specs=whole(),
        scratch_shapes=[
            pltpu.VMEM((len(parts) + 1, rows, full_width), jnp.bfloat16),
            pltpu.VMEM((len(gains), 16, gains[0].shape[1]), jnp.bfloat16),
            pltpu.VMEM((rows, full_width), jnp.float32),
            pltpu.SemaphoreType.DMA((count,)),
        ],
        compiler_params=params(6 * MIB),
        cost_estimate=pl.CostEstimate(
            flops=8 * rows * full_width, bytes_accessed=12 * rows * full_width, transcendentals=rows
        ),
        name="final_rows",
    )(*parts, raw, *gains, *after)


def head_kernel(pieces, tile, sub, *refs):
    piece_refs = refs[:pieces]
    head_ref, target_ref, out_ref, rows_scr, head_scr, sems, head_sems = refs[pieces:]
    vocab_part = head_ref.shape[0]
    steps = vocab_part // tile
    my_expert, my_tensor = lax.axis_index("expert"), lax.axis_index("tensor")
    n_tensor = lax.axis_size("tensor")

    def fetch(i):
        return pltpu.make_async_copy(
            head_ref.at[pl.ds(pl.multiple_of(i * tile, tile), tile), :],
            head_scr.at[i],
            head_sems.at[i],
        )

    copies = []
    for piece_ref in piece_refs:
        for start in range(0, piece_ref.shape[0], sub):
            far_expert, far_tensor = divmod(len(copies), n_tensor)
            block = (my_expert ^ far_expert) * n_tensor + (my_tensor ^ far_tensor)
            copies.append(
                pltpu.make_async_copy(
                    piece_ref.at[pl.ds(start, sub), :],
                    rows_scr.at[pl.ds(pl.multiple_of(block * sub, sub), sub), :],
                    sems.at[len(copies)],
                )
            )
    for copy in copies:
        copy.start()
    fetch(0).start()
    for copy in copies:
        copy.wait()
    for i in range(1, steps):
        fetch(i).start()
    lane = lax.broadcasted_iota(jnp.int32, out_ref.shape, 0)
    out_ref[...] = jnp.where(lane == 0, -jnp.inf, 0.0)
    targets = target_ref[...] - (my_expert * n_tensor + my_tensor) * vocab_part

    @pl.loop(0, steps)
    def _(i):
        fetch(i).wait()
        logits = lax.dot_general(
            head_scr[i],
            rows_scr[...],
            (((1,), (1,)), ((), ())),
            preferred_element_type=jnp.float32,
        )
        word = lax.broadcasted_iota(jnp.int32, logits.shape, 0) + i * tile
        old_top, old_total = out_ref[0:1, :], out_ref[1:2, :]
        top = jnp.maximum(old_top, jnp.max(logits, axis=0, keepdims=True))
        out_ref[0:1, :] = top
        out_ref[1:2, :] = old_total * jnp.exp(old_top - top) + jnp.sum(
            jnp.exp(logits - top), axis=0, keepdims=True
        )
        hit = word == targets
        out_ref[2:3, :] += jnp.sum(jnp.where(hit, logits, 0.0), axis=0, keepdims=True)


def head_terms(pieces, head_rows, targets, sub):
    rows = sum(p.shape[0] for p in pieces)
    vocab_part, full_width = head_rows.shape
    tile = next(t for t in (400, 200, 80, 8, vocab_part) if vocab_part % t == 0)
    return pl.pallas_call(
        functools.partial(head_kernel, len(pieces), tile, sub),
        out_shape=jax.ShapeDtypeStruct((8, rows), jnp.float32),
        in_specs=[anywhere()] * (len(pieces) + 1) + [whole()],
        out_specs=whole(),
        scratch_shapes=[
            pltpu.VMEM((rows, full_width), jnp.bfloat16),
            pltpu.VMEM((vocab_part // tile, tile, full_width), jnp.bfloat16),
            pltpu.SemaphoreType.DMA((rows // sub,)),
            pltpu.SemaphoreType.DMA((vocab_part // tile,)),
        ],
        compiler_params=params((22 + rows // 64) * MIB),
        cost_estimate=pl.CostEstimate(
            flops=2 * rows * full_width * vocab_part,
            bytes_accessed=2 * full_width * (vocab_part + rows),
            transcendentals=rows * vocab_part,
        ),
        name="head_terms",
    )(*pieces, head_rows, targets)


def join_terms(parts):
    top = functools.reduce(jnp.maximum, [p[0] for p in parts])
    total = sum(p[1] * jnp.exp(p[0] - top) for p in parts)
    target = sum(p[2] for p in parts)
    return jnp.stack([top, total, target])


def join_axis(terms, axis, place, me):
    def of(d):
        return lax.dynamic_index_in_dim(terms, me ^ d, place, False)

    return join_terms([of(0)] + [swap(of(d), axis, d) for d in range(1, lax.axis_size(axis))])


def pack_kernel(kept_ref, got_ref, one_ref, two_ref, home_ref, side_ref):
    rows = home_ref.shape[0]
    half = rows // 2

    def both(d, first):
        block = slice(d * rows + first, d * rows + first + half)
        return kept_ref[block, :].astype(jnp.float32) + got_ref[block, :].astype(jnp.float32)

    one_ref[:half, :] = both(1, 0).astype(jnp.bfloat16)
    one_ref[half:, :] = both(3, 0).astype(jnp.bfloat16)
    two_ref[:half, :] = both(2, half).astype(jnp.bfloat16)
    two_ref[half:, :] = both(3, half).astype(jnp.bfloat16)
    home_ref[:half, :] = both(0, 0)
    home_ref[half:, :] = both(0, half)
    side_ref[0] = both(1, half)
    side_ref[1] = both(2, 0)


def pass_kernel(side_ref, one_ref, two_ref, *refs):
    pass_one_ref, pass_two_ref = refs[-2:]
    half = pass_one_ref.shape[0]
    pass_one_ref[...] = (side_ref[0] + two_ref[half:, :].astype(jnp.float32)).astype(jnp.bfloat16)
    pass_two_ref[...] = (side_ref[1] + one_ref[half:, :].astype(jnp.float32)).astype(jnp.bfloat16)


def total_kernel(count, home_ref, one_ref, two_ref, last_one_ref, last_two_ref, *refs):
    outs, work = refs[-count - 1 : -1], refs[-1]
    half = last_one_ref.shape[0]
    sub = outs[0].shape[0]
    me = lax.axis_index("tensor")
    upper = one_ref[:half, :].astype(jnp.float32) + last_two_ref[...].astype(jnp.float32)
    lower = two_ref[:half, :].astype(jnp.float32) + last_one_ref[...].astype(jnp.float32)
    work[:half, :] = home_ref[:half, :] + upper
    work[half:, :] = home_ref[half:, :] + lower
    for d in range(count):
        block = pl.ds(pl.multiple_of((me ^ d) * sub, sub), sub)
        outs[d][...] = work[block, :].astype(jnp.bfloat16)


def small_call(kernel, name, inputs, after, outs, scratch, limit):
    size = sum(x.size * x.dtype.itemsize for x in inputs)
    return pl.pallas_call(
        kernel,
        out_shape=tuple(jax.ShapeDtypeStruct(*out) for out in outs),
        in_specs=[whole()] * len(inputs) + [anywhere()] * len(after),
        out_specs=(whole(),) * len(outs),
        scratch_shapes=scratch,
        compiler_params=params(limit),
        cost_estimate=pl.CostEstimate(flops=size, bytes_accessed=2 * size, transcendentals=0),
        name=name,
    )(*inputs, *after)


def sum_plane(kept, got, rows, after_pass):
    f32, b16 = jnp.float32, jnp.bfloat16
    n_tensor = lax.axis_size("tensor")
    count, full_width = kept.shape[0] // rows, kept.shape[1]
    half = rows // 2
    sub = rows // n_tensor
    if count == 4 and half % 16 == 0 and sub % 16 == 0:
        one, two, home, side = small_call(
            pack_kernel,
            "pack",
            [kept, got],
            [],
            [((rows, full_width), b16)] * 2
            + [((rows, full_width), f32), ((2, half, full_width), f32)],
            [],
            10 * MIB,
        )
        from_one, from_two = swap(one, "expert", 1), swap(two, "expert", 2)
        pass_one, pass_two = small_call(
            pass_kernel,
            "pass_on",
            [side, from_one, from_two],
            after_pass,
            [((half, full_width), b16)] * 2,
            [],
            6 * MIB,
        )
        last_one, last_two = swap(pass_one, "expert", 1), swap(pass_two, "expert", 2)
        pieces = small_call(
            functools.partial(total_kernel, n_tensor),
            "total",
            [home, from_one, from_two, last_one, last_two],
            [],
            [((sub, full_width), b16)] * n_tensor,
            [pltpu.VMEM((rows, full_width), f32)],
            8 * MIB,
        )
        return list(pieces), [one, two], [pass_one, pass_two]
    both = (kept.astype(f32) + got.astype(f32)).reshape(count, rows, full_width)
    total = both[0]
    for d in range(1, count):
        total = total + swap(both[d].astype(b16), "expert", d).astype(f32)
    total = total.astype(b16).reshape(n_tensor, sub, full_width)
    me = lax.axis_index("tensor")
    pieces = [lax.dynamic_index_in_dim(total, me ^ d, 0, False) for d in range(n_tensor)]
    return pieces, [], []


def on_device(
    tokens, routes, route_weights, norm_gain, final_gain, w_gate, w_up, w_down, head_weight, targets
):
    tok_rows, width = tokens.shape
    n_expert = lax.axis_size("expert")
    n_tensor = lax.axis_size("tensor")
    my_expert = lax.axis_index("expert")
    my_tensor = lax.axis_index("tensor")
    full_width = width * n_tensor
    own = tok_rows // n_tensor
    splits = 2 if own % 32 == 0 else 1
    sub = own // splits
    rows = sub * n_tensor

    parts = tokens.reshape(n_tensor, splits, sub, width)
    rider = jnp.concatenate([split_three(norm_gain), split_three(final_gain)])
    rider = jnp.pad(rider, ((0, 16 - rider.shape[0]), (0, 0))).astype(jnp.bfloat16)
    blocks = [parts[:, h].reshape(rows, width) for h in range(splits)]
    gains = slices = gather_near(jnp.concatenate([blocks[0], rider]), "tensor")
    planes, raws = [], []
    after = []
    for h in range(splits):
        following = blocks[h + 1 : h + 2]
        normed, raw, *block = norm_rows(
            slices, gains, routes, route_weights, splits, h, rows, after, following
        )
        if block:
            slices = gather_near(block[0], "tensor")
        plane = gather_plane(normed, "expert", [])
        planes.append(plane)
        raws.append(raw)
        after = plane[3:]

    w_gate = pltpu.with_memory_space_constraint(w_gate, pltpu.HBM)
    w_up = pltpu.with_memory_space_constraint(w_up, pltpu.HBM)
    head_rows = pltpu.with_memory_space_constraint(head_weight.T, pltpu.HBM)
    target_rows = targets.reshape(n_expert, n_tensor, splits, sub)
    terms = []
    before = {}
    for h in range(splits):
        far = planes[h][3:]
        if before and len(far) == 2:
            far = [stack_rows(far, before["kept"])]
        away = [swap(p, "seq", 1) for p in planes[h][:3] + far]
        if 2 * n_expert * rows <= LARGEST:
            half = n_expert * rows
            everything = planes[h] + away
            tile = tile_of(w_gate)
            count = w_gate.shape[2] // tile
            cuts = [0, (count + 1) // 2, count - 1, count] if h else [0, count]
            ties = [before.get(key, []) for key in ("packed", "passed", "totals")]
            hidden = [
                hidden_rows(
                    everything, w_gate, w_up, ties[i], cuts[i], cuts[i + 1] - cuts[i], tile
                )
                for i in range(len(cuts) - 1)
            ]
            later = planes[h + 1][1:3] if h + 1 < splits else []
            other = down_rows(hidden, w_down, half, half, later + before.get("sums", []))
            kept = down_rows(hidden, w_down, 0, half, before.get("final", []))
        else:
            away = [swap(p, "seq", 1) for p in planes[h]]
            kept, other = many_rows(planes[h], w_gate, w_up, w_down), many_rows(
                away, w_gate, w_up, w_down
            )
        got = swap(other, "seq", 1)
        totals, packed, passed = sum_plane(kept, got, rows, before.get("column", []))
        sums = [swap(totals[d], "tensor", d) for d in range(1, n_tensor)]
        finals_near, finals_far = [], []
        if before:
            column = stack_rows([before["final"][0]] + before["column"], totals[:1])
            plane = gather_plane(column, "expert", [])
            finals_near, finals_far = plane[1:3], plane[3:]
            wanted = target_rows[:, :, h - 1].reshape(1, -1)
            terms.append(head_terms(plane, head_rows, wanted, sub))
        final = final_rows(totals[:1] + sums, raws[h], gains, finals_near)
        column = gather_near(final, "tensor")
        before = {
            "kept": [kept],
            "packed": packed,
            "passed": passed,
            "totals": totals,
            "sums": sums,
            "final": [final],
            "column": column[1:],
        }
    column = stack_rows(column, finals_far)
    plane = gather_plane(column, "expert", terms[-1:])
    wanted = target_rows[:, :, splits - 1].reshape(1, -1)
    terms.append(head_terms(plane, head_rows, wanted, sub))
    terms = [term[:3].reshape(3, n_expert, n_tensor, sub) for term in terms]
    terms = jnp.stack(terms, axis=3)
    joined = join_axis(terms, "tensor", 2, my_tensor)
    joined = join_axis(joined, "expert", 1, my_expert)
    return (joined[0] + jnp.log(joined[1]) - joined[2]).reshape(own)


def solution(mesh):
    return jax.shard_map(
        on_device,
        mesh=mesh,
        in_specs=(
            P(("seq", "expert"), "tensor"),
            P(("seq", "expert"), None),
            P(("seq", "expert"), None),
            P("tensor"),
            P("tensor"),
            P("expert", None, ("seq", "tensor")),
            P("expert", None, ("seq", "tensor")),
            P("expert", ("seq", "tensor"), None),
            P(None, ("expert", "tensor")),
            P("seq"),
        ),
        out_specs=P(("seq", "expert", "tensor")),
        check_vma=False,
    )
```

```python
import functools

import jax
import jax.numpy as jnp
from jax import lax
from jax.experimental import pallas as pl
from jax.experimental.pallas import tpu as pltpu
from jax.sharding import PartitionSpec as P

epsilon = 1e-05
LANES = 128
LARGEST = 512
MIB = 1024 * 1024
VMEM_BYTES = 56 * 1024 * 1024


def params(limit=VMEM_BYTES):
    return pltpu.CompilerParams(vmem_limit_bytes=limit)


def whole():
    return pl.BlockSpec(memory_space=pltpu.VMEM)


def anywhere():
    return pl.BlockSpec(memory_space=pl.ANY)


def swap(x, axis, distance):
    size = lax.axis_size(axis)
    return lax.ppermute(x, axis, [(i, i ^ distance) for i in range(size)])


def gather_near(x, axis):
    return [x] + [swap(x, axis, d) for d in range(1, lax.axis_size(axis))]


def gather_plane(x, axis, after):
    if lax.axis_size(axis) != 4:
        return gather_near(x, axis), []
    half = x.shape[0] // 2
    one, two = swap(x, axis, 1), swap(x, axis, 2)
    upper, lower = move_rows([two, one], [(0, 0, half, 0, 0), (1, half, half, 1, 0)], after)
    return [x, one, two, swap(upper, axis, 1), swap(lower, axis, 2)], [upper, lower]


def move_kernel(sources, targets, moves, *refs):
    out_refs, sems = refs[-targets - 1 : -1], refs[-1]
    copies = []
    for i, (source, start, count, target, place) in enumerate(moves):
        copies.append(
            pltpu.make_async_copy(
                refs[source].at[pl.ds(start, count), :],
                out_refs[target].at[pl.ds(place, count), :],
                sems.at[i],
            )
        )
    for copy in copies:
        copy.start()
    for copy in copies:
        copy.wait()


def move_rows(arrays, moves, after):
    targets = 1 + max(m[3] for m in moves)
    sizes = [sum(m[2] for m in moves if m[3] == t) for t in range(targets)]
    size = sum(sizes) * arrays[0].shape[1]
    return pl.pallas_call(
        functools.partial(move_kernel, len(arrays), targets, moves),
        out_shape=tuple(
            jax.ShapeDtypeStruct((rows, arrays[0].shape[1]), arrays[0].dtype) for rows in sizes
        ),
        in_specs=[anywhere()] * (len(arrays) + len(after)),
        out_specs=(anywhere(),) * targets,
        scratch_shapes=[pltpu.SemaphoreType.DMA((len(moves),))],
        compiler_params=params(MIB),
        cost_estimate=pl.CostEstimate(flops=0, bytes_accessed=4 * size, transcendentals=0),
        name="move_rows",
    )(*arrays, *after)


def stack_rows(arrays, after):
    moves = []
    place = 0
    for i, x in enumerate(arrays):
        moves.append((i, 0, x.shape[0], 0, place))
        place += x.shape[0]
    return move_rows(arrays, moves, after)[0]


def load_pieces(piece_refs, scratch, sems):
    copies = []
    start = 0
    for i in range(len(piece_refs)):
        count = piece_refs[i].shape[0]
        copies.append(
            pltpu.make_async_copy(piece_refs[i], scratch.at[pl.ds(start, count), :], sems.at[i])
        )
        start += count
    for copy in copies:
        copy.start()
    for copy in copies:
        copy.wait()


def begin_kernel(count, tokens_ref, norm_ref, final_ref, *block_refs):
    splits = len(block_refs)
    own_rows = tokens_ref.shape[0] // (count * splits)
    for i in range(count):
        for h in range(splits):
            start = (i * splits + h) * own_rows
            block_refs[h][i * own_rows : (i + 1) * own_rows, :] = tokens_ref[
                start : start + own_rows, :
            ]
    lines = []
    for gain_ref in (norm_ref, final_ref):
        gain = gain_ref[...]
        high = gain.astype(jnp.bfloat16).astype(jnp.float32)
        middle = (gain - high).astype(jnp.bfloat16).astype(jnp.float32)
        lines += [high, middle, gain - high - middle]
    lines.append(jnp.zeros((2, lines[0].shape[1]), jnp.float32))
    block_refs[0][count * own_rows :, :] = jnp.concatenate(lines).astype(jnp.bfloat16)


def begin(tokens, norm_gain, final_gain, count, splits):
    rows, width = tokens.shape
    sizes = [rows // splits + (0 if h else 8) for h in range(splits)]
    return small_call(
        functools.partial(begin_kernel, count),
        "begin",
        [tokens, norm_gain.reshape(1, width), final_gain.reshape(1, width)],
        [],
        [((size, width), jnp.bfloat16) for size in sizes],
        [],
        4 * MIB,
    )


def norm_kernel(splits, part, count, after, *refs):
    slices = refs[:count]
    routes_ref, weights_ref = refs[count : count + 2]
    rest = list(refs[count + 2 :])
    gains_in = rest.pop(0) if part else None
    rest = rest[after:]
    rows_ref, raw_ref = rest[:2]
    gains_ref = gains_in if part else rest[2]
    rows = rows_ref.shape[0]
    width = slices[0].shape[1]
    full_width = width * count
    own_rows = rows // count
    me = lax.axis_index("tensor")
    total = jnp.zeros((rows, 1), jnp.float32)
    for piece in slices:
        value = piece[:rows, :].astype(jnp.float32)
        total = total + jnp.sum(value * value, axis=1, keepdims=True)
    scale = lax.rsqrt(total / full_width + epsilon)
    start = pl.multiple_of(me * own_rows, own_rows)
    for d in range(count):
        columns = pl.ds(pl.multiple_of((me ^ d) * width, width), width)
        if not part:
            tail = slices[d][rows:, :].astype(jnp.float32)
            gains_ref[0:1, columns] = tail[0:1] + tail[1:2] + tail[2:3]
            gains_ref[1:2, columns] = tail[3:4] + tail[4:5] + tail[5:6]
        value = slices[d][:rows, :].astype(jnp.float32)
        rows_ref[:, columns] = (value * scale * gains_ref[0:1, columns]).astype(jnp.bfloat16)
        raw_ref[:, columns] = slices[d][pl.ds(start, own_rows), :]
    lane = lax.broadcasted_iota(jnp.int32, (own_rows, LANES), 1)
    expert = lane // 3
    kind = lane - expert * 3
    for i in range(count):
        block = pl.ds((i * splits + part) * own_rows, own_rows)
        weight = jnp.zeros((own_rows, LANES), jnp.float32)
        for j in range(routes_ref.shape[1]):
            named = routes_ref[block, j : j + 1] == expert
            weight = weight + jnp.where(named, weights_ref[block, j : j + 1], 0.0)
        high = weight.astype(jnp.bfloat16).astype(jnp.float32)
        middle = (weight - high).astype(jnp.bfloat16).astype(jnp.float32)
        low = weight - high - middle
        value = jnp.where(kind == 0, high, jnp.where(kind == 1, middle, low))
        rows_ref[i * own_rows : (i + 1) * own_rows, full_width:] = value.astype(jnp.bfloat16)


def norm_rows(slices, gains, routes, route_weights, splits, part, rows, after):
    width = slices[0].shape[1]
    count = len(slices)
    full_width = width * count
    gains = gains if part else []
    made = [] if part else [jax.ShapeDtypeStruct((8, full_width), jnp.float32)]
    return pl.pallas_call(
        functools.partial(norm_kernel, splits, part, count, len(after)),
        out_shape=(
            jax.ShapeDtypeStruct((rows, full_width + LANES), jnp.bfloat16),
            jax.ShapeDtypeStruct((rows // count, full_width), jnp.bfloat16),
            *made,
        ),
        in_specs=[whole()] * (count + 2 + len(gains)) + [anywhere()] * len(after),
        out_specs=(whole(),) * (2 + len(made)),
        compiler_params=params(6 * MIB),
        cost_estimate=pl.CostEstimate(
            flops=6 * rows * full_width, bytes_accessed=4 * rows * full_width, transcendentals=rows
        ),
        name="norm_rows",
    )(*slices, routes, route_weights, *gains, *after)


def hidden_kernel(pieces, after, tile, first, steps, *refs):
    piece_refs = refs[:pieces]
    weight_refs = refs[pieces : pieces + 2]
    out_ref, rows_scr, route_scr, weight_scr, work, sems, weight_sems = refs[pieces + 2 + after :]
    full_width = weight_scr.shape[2]

    def fetch(i, act):
        slot = lax.rem(i, 2)
        columns = pl.ds(pl.multiple_of((first + i) * tile, tile), tile)
        for j in range(2):
            act(
                pltpu.make_async_copy(
                    weight_refs[j].at[0, :, columns],
                    weight_scr.at[j, slot],
                    weight_sems.at[j, slot],
                )
            )

    def start(copy):
        copy.start()

    def wait(copy):
        copy.wait()

    def dots(i):
        rows = rows_scr[:, :full_width]
        slot = lax.rem(i, 2)
        for j in range(2):
            work[j] = jnp.dot(rows, weight_scr[j, slot], preferred_element_type=jnp.float32)

    def finish(i):
        gate, up = work[0], work[1]
        hidden = gate * (1.0 + jnp.tanh(0.5 * gate)) * up * route_scr[:, :1]
        columns = pl.ds(pl.multiple_of(i * tile, tile), tile)
        out_ref[:, columns] = hidden.astype(jnp.bfloat16)

    fetch(0, start)
    load_pieces(piece_refs, rows_scr, sems)
    small = rows_scr[:, full_width:].astype(jnp.float32)
    lane = lax.broadcasted_iota(jnp.int32, small.shape, 1)
    place = lax.axis_index("expert") * 3
    mine = (lane >= place) & (lane < place + 3)
    weight = jnp.sum(jnp.where(mine, small, 0.0), axis=1, keepdims=True)
    route_scr[...] = jnp.broadcast_to(0.5 * weight, route_scr.shape)
    fetch(0, wait)
    if steps > 1:
        fetch(1, start)
    dots(0)

    @pl.loop(1, steps)
    def _(i):
        fetch(i, wait)

        @pl.when(i + 1 < steps)
        def _():
            fetch(i + 1, start)

        finish(i - 1)
        dots(i)

    finish(steps - 1)


def tile_of(weight):
    hidden = weight.shape[2]
    return next(t for t in (256, 128, hidden) if hidden % t == 0)


def hidden_rows(pieces, w_gate, w_up, after, first, steps, tile):
    rows = sum(p.shape[0] for p in pieces)
    full_width = w_gate.shape[1]
    hidden = steps * tile
    return pl.pallas_call(
        functools.partial(hidden_kernel, len(pieces), len(after), tile, first, steps),
        out_shape=jax.ShapeDtypeStruct((rows, hidden), jnp.bfloat16),
        in_specs=[anywhere()] * (len(pieces) + 2 + len(after)),
        out_specs=whole(),
        scratch_shapes=[
            pltpu.VMEM((rows, full_width + LANES), jnp.bfloat16),
            pltpu.VMEM((rows, LANES), jnp.float32),
            pltpu.VMEM((2, 2, full_width, tile), jnp.bfloat16),
            pltpu.VMEM((2, rows, tile), jnp.float32),
            pltpu.SemaphoreType.DMA((len(pieces),)),
            pltpu.SemaphoreType.DMA((2, 2)),
        ],
        compiler_params=params((14 + rows // 64) * MIB),
        cost_estimate=pl.CostEstimate(
            flops=4 * rows * full_width * hidden,
            bytes_accessed=4 * full_width * hidden + 2 * rows * (full_width + hidden),
            transcendentals=rows * hidden,
        ),
        name="hidden_rows",
    )(*pieces, w_gate, w_up, *after)


def down_kernel(start, count, *refs):
    hidden_refs, down_ref, out_ref = refs[:count], refs[count], refs[-1]
    full_width = out_ref.shape[1]
    tile = 512 if full_width % 512 == 0 else full_width

    @pl.loop(0, full_width // tile, unroll=True)
    def _(i):
        columns = pl.ds(pl.multiple_of(i * tile, tile), tile)
        out = None
        depth = 0
        for hidden_ref in hidden_refs:
            rows = hidden_ref[start : start + out_ref.shape[0], :]
            block = down_ref[0, depth : depth + rows.shape[1], columns]
            term = jnp.dot(rows, block, preferred_element_type=jnp.float32)
            out = term if out is None else out + term
            depth += rows.shape[1]
        out_ref[:, columns] = out.astype(jnp.bfloat16)


def down_rows(hidden, w_down, start, rows, after):
    depth, full_width = w_down.shape[1:]
    hidden = [pltpu.with_memory_space_constraint(part, pltpu.VMEM) for part in hidden]
    return pl.pallas_call(
        functools.partial(down_kernel, start, len(hidden)),
        out_shape=jax.ShapeDtypeStruct((rows, full_width), jnp.bfloat16),
        in_specs=[whole()] * (len(hidden) + 1) + [anywhere()] * len(after),
        out_specs=whole(),
        compiler_params=params((4 + rows // 64) * MIB),
        cost_estimate=pl.CostEstimate(
            flops=2 * rows * depth * full_width,
            bytes_accessed=2 * rows * (depth + full_width),
            transcendentals=0,
        ),
        name="down_rows",
    )(*hidden, w_down, *after)


def many_rows(pieces, w_gate, w_up, w_down):
    outs = []
    tile = tile_of(w_gate)
    steps = w_gate.shape[2] // tile
    while pieces:
        count = 1
        while count < len(pieces) and sum(p.shape[0] for p in pieces[: count + 1]) <= LARGEST:
            count += 1
        hidden = hidden_rows(pieces[:count], w_gate, w_up, [], 0, steps, tile)
        outs.append(down_rows([hidden], w_down, 0, hidden.shape[0], []))
        pieces = pieces[count:]
    return jnp.concatenate(outs)


def final_kernel(parts, *refs):
    part_refs = refs[: parts + 2]
    out_ref, rows_scr, gains_scr, sems = refs[-4:]
    targets = [rows_scr.at[i] for i in range(parts + 1)] + [gains_scr]
    copies = [
        pltpu.make_async_copy(part_refs[i], targets[i], sems.at[i]) for i in range(parts + 2)
    ]
    for copy in copies:
        copy.start()
    for copy in copies:
        copy.wait()
    mixed = rows_scr[0].astype(jnp.float32)
    for i in range(1, parts):
        mixed = mixed + rows_scr[i].astype(jnp.float32)
    residual = rows_scr[parts].astype(jnp.float32) + mixed
    residual = residual.astype(jnp.bfloat16).astype(jnp.float32)
    total = jnp.sum(residual * residual, axis=1, keepdims=True)
    scale = lax.rsqrt(total / residual.shape[1] + epsilon)
    out_ref[...] = (residual * scale * gains_scr[1:2, :]).astype(jnp.bfloat16)


def final_rows(parts, raw, gains, after):
    rows, full_width = raw.shape
    return pl.pallas_call(
        functools.partial(final_kernel, len(parts)),
        out_shape=jax.ShapeDtypeStruct((rows, full_width), jnp.bfloat16),
        in_specs=[anywhere()] * (len(parts) + 2 + len(after)),
        out_specs=whole(),
        scratch_shapes=[
            pltpu.VMEM((len(parts) + 1, rows, full_width), jnp.bfloat16),
            pltpu.VMEM(gains.shape, jnp.float32),
            pltpu.SemaphoreType.DMA((len(parts) + 2,)),
        ],
        compiler_params=params(6 * MIB),
        cost_estimate=pl.CostEstimate(
            flops=8 * rows * full_width, bytes_accessed=12 * rows * full_width, transcendentals=rows
        ),
        name="final_rows",
    )(*parts, raw, gains, *after)


def head_kernel(pieces, tile, sub, *refs):
    piece_refs = refs[:pieces]
    head_ref, target_ref, out_ref, rows_scr, head_scr, sems, head_sems = refs[pieces:]
    vocab_part = head_ref.shape[0]
    steps = vocab_part // tile
    my_expert, my_tensor = lax.axis_index("expert"), lax.axis_index("tensor")
    n_tensor = lax.axis_size("tensor")

    def fetch(i):
        return pltpu.make_async_copy(
            head_ref.at[pl.ds(pl.multiple_of(i * tile, tile), tile), :],
            head_scr.at[i],
            head_sems.at[i],
        )

    copies = []
    for piece_ref in piece_refs:
        for start in range(0, piece_ref.shape[0], sub):
            far_expert, far_tensor = divmod(len(copies), n_tensor)
            block = (my_expert ^ far_expert) * n_tensor + (my_tensor ^ far_tensor)
            copies.append(
                pltpu.make_async_copy(
                    piece_ref.at[pl.ds(start, sub), :],
                    rows_scr.at[pl.ds(pl.multiple_of(block * sub, sub), sub), :],
                    sems.at[len(copies)],
                )
            )
    ahead = min(2, steps)
    for i in range(1):
        fetch(i).start()
    for copy in copies:
        copy.start()
    for i in range(1, ahead):
        fetch(i).start()
    for copy in copies:
        copy.wait()
    lane = lax.broadcasted_iota(jnp.int32, out_ref.shape, 0)
    out_ref[...] = jnp.where(lane == 0, -jnp.inf, 0.0)
    targets = target_ref[...] - (my_expert * n_tensor + my_tensor) * vocab_part

    @pl.loop(0, steps)
    def _(i):
        fetch(i).wait()

        @pl.when(i + ahead < steps)
        def _():
            fetch(i + ahead).start()

        logits = lax.dot_general(
            head_scr[i],
            rows_scr[...],
            (((1,), (1,)), ((), ())),
            preferred_element_type=jnp.float32,
        )
        word = lax.broadcasted_iota(jnp.int32, logits.shape, 0) + i * tile
        old_top, old_total = out_ref[0:1, :], out_ref[1:2, :]
        top = jnp.maximum(old_top, jnp.max(logits, axis=0, keepdims=True))
        out_ref[0:1, :] = top
        out_ref[1:2, :] = old_total * jnp.exp(old_top - top) + jnp.sum(
            jnp.exp(logits - top), axis=0, keepdims=True
        )
        hit = word == targets
        out_ref[2:3, :] += jnp.sum(jnp.where(hit, logits, 0.0), axis=0, keepdims=True)


def head_terms(pieces, head_rows, targets, sub):
    rows = sum(p.shape[0] for p in pieces)
    vocab_part, full_width = head_rows.shape
    tile = next(t for t in (400, 200, 80, 8, vocab_part) if vocab_part % t == 0)
    return pl.pallas_call(
        functools.partial(head_kernel, len(pieces), tile, sub),
        out_shape=jax.ShapeDtypeStruct((8, rows), jnp.float32),
        in_specs=[anywhere()] * (len(pieces) + 1) + [whole()],
        out_specs=whole(),
        scratch_shapes=[
            pltpu.VMEM((rows, full_width), jnp.bfloat16),
            pltpu.VMEM((vocab_part // tile, tile, full_width), jnp.bfloat16),
            pltpu.SemaphoreType.DMA((rows // sub,)),
            pltpu.SemaphoreType.DMA((vocab_part // tile,)),
        ],
        compiler_params=params((22 + rows // 64) * MIB),
        cost_estimate=pl.CostEstimate(
            flops=2 * rows * full_width * vocab_part,
            bytes_accessed=2 * full_width * (vocab_part + rows),
            transcendentals=rows * vocab_part,
        ),
        name="head_terms",
    )(*pieces, head_rows, targets)


def join_terms(parts):
    top = functools.reduce(jnp.maximum, [p[0] for p in parts])
    total = sum(p[1] * jnp.exp(p[0] - top) for p in parts)
    target = sum(p[2] for p in parts)
    return jnp.stack([top, total, target])


def join_axis(terms, axis, place, me):
    def of(d):
        return lax.dynamic_index_in_dim(terms, me ^ d, place, False)

    return join_terms([of(0)] + [swap(of(d), axis, d) for d in range(1, lax.axis_size(axis))])


def pack_kernel(kept_ref, got_ref, one_ref, two_ref, home_ref, side_ref):
    rows = home_ref.shape[0]
    half = rows // 2

    def both(d, first):
        block = slice(d * rows + first, d * rows + first + half)
        return kept_ref[block, :].astype(jnp.float32) + got_ref[block, :].astype(jnp.float32)

    one_ref[:half, :] = both(1, 0).astype(jnp.bfloat16)
    one_ref[half:, :] = both(3, 0).astype(jnp.bfloat16)
    two_ref[:half, :] = both(2, half).astype(jnp.bfloat16)
    two_ref[half:, :] = both(3, half).astype(jnp.bfloat16)
    home_ref[:half, :] = both(0, 0)
    home_ref[half:, :] = both(0, half)
    side_ref[0] = both(1, half)
    side_ref[1] = both(2, 0)


def pass_kernel(side_ref, one_ref, two_ref, *refs):
    pass_one_ref, pass_two_ref = refs[-2:]
    half = pass_one_ref.shape[0]
    pass_one_ref[...] = (side_ref[0] + two_ref[half:, :].astype(jnp.float32)).astype(jnp.bfloat16)
    pass_two_ref[...] = (side_ref[1] + one_ref[half:, :].astype(jnp.float32)).astype(jnp.bfloat16)


def total_kernel(count, home_ref, one_ref, two_ref, last_one_ref, last_two_ref, *refs):
    outs, work = refs[-count - 1 : -1], refs[-1]
    half = last_one_ref.shape[0]
    sub = outs[0].shape[0]
    me = lax.axis_index("tensor")
    upper = one_ref[:half, :].astype(jnp.float32) + last_two_ref[...].astype(jnp.float32)
    lower = two_ref[:half, :].astype(jnp.float32) + last_one_ref[...].astype(jnp.float32)
    work[:half, :] = home_ref[:half, :] + upper
    work[half:, :] = home_ref[half:, :] + lower
    for d in range(count):
        block = pl.ds(pl.multiple_of((me ^ d) * sub, sub), sub)
        outs[d][...] = work[block, :].astype(jnp.bfloat16)


def small_call(kernel, name, inputs, after, outs, scratch, limit):
    size = sum(x.size * x.dtype.itemsize for x in inputs)
    return pl.pallas_call(
        kernel,
        out_shape=tuple(jax.ShapeDtypeStruct(*out) for out in outs),
        in_specs=[whole()] * len(inputs) + [anywhere()] * len(after),
        out_specs=(whole(),) * len(outs),
        scratch_shapes=scratch,
        compiler_params=params(limit),
        cost_estimate=pl.CostEstimate(flops=size, bytes_accessed=2 * size, transcendentals=0),
        name=name,
    )(*inputs, *after)


def sum_plane(kept, got, rows, after_pass):
    f32, b16 = jnp.float32, jnp.bfloat16
    n_tensor = lax.axis_size("tensor")
    count, full_width = kept.shape[0] // rows, kept.shape[1]
    half = rows // 2
    sub = rows // n_tensor
    if count == 4 and half % 16 == 0 and sub % 16 == 0:
        one, two, home, side = small_call(
            pack_kernel,
            "pack",
            [kept, got],
            [],
            [((rows, full_width), b16)] * 2
            + [((rows, full_width), f32), ((2, half, full_width), f32)],
            [],
            10 * MIB,
        )
        from_one, from_two = swap(one, "expert", 1), swap(two, "expert", 2)
        pass_one, pass_two = small_call(
            pass_kernel,
            "pass_on",
            [side, from_one, from_two],
            after_pass,
            [((half, full_width), b16)] * 2,
            [],
            6 * MIB,
        )
        last_one, last_two = swap(pass_one, "expert", 1), swap(pass_two, "expert", 2)
        pieces = small_call(
            functools.partial(total_kernel, n_tensor),
            "total",
            [home, from_one, from_two, last_one, last_two],
            [],
            [((sub, full_width), b16)] * n_tensor,
            [pltpu.VMEM((rows, full_width), f32)],
            8 * MIB,
        )
        return list(pieces), [one, two], [pass_one, pass_two]
    both = (kept.astype(f32) + got.astype(f32)).reshape(count, rows, full_width)
    total = both[0]
    for d in range(1, count):
        total = total + swap(both[d].astype(b16), "expert", d).astype(f32)
    total = total.astype(b16).reshape(n_tensor, sub, full_width)
    me = lax.axis_index("tensor")
    pieces = [lax.dynamic_index_in_dim(total, me ^ d, 0, False) for d in range(n_tensor)]
    return pieces, [], []


def on_device(
    tokens, routes, route_weights, norm_gain, final_gain, w_gate, w_up, w_down, head_weight, targets
):
    tok_rows, width = tokens.shape
    n_expert = lax.axis_size("expert")
    n_tensor = lax.axis_size("tensor")
    my_expert = lax.axis_index("expert")
    my_tensor = lax.axis_index("tensor")
    full_width = width * n_tensor
    own = tok_rows // n_tensor
    splits = 2 if own % 32 == 0 else 1
    sub = own // splits
    rows = sub * n_tensor

    blocks = begin(tokens, norm_gain, final_gain, n_tensor, splits)
    slices = [gather_near(block, "tensor") for block in blocks]
    gains = None
    planes, raws = [], []
    after = []
    for h in range(splits):
        normed, raw, *made = norm_rows(
            slices[h], [gains], routes, route_weights, splits, h, rows, after
        )
        if made:
            gains = made[0]
        plane, _ = gather_plane(normed, "expert", [])
        planes.append(plane)
        raws.append(raw)
        after = plane[3:]

    w_gate = pltpu.with_memory_space_constraint(w_gate, pltpu.HBM)
    w_up = pltpu.with_memory_space_constraint(w_up, pltpu.HBM)
    head_rows = pltpu.with_memory_space_constraint(head_weight.T, pltpu.HBM)
    target_rows = targets.reshape(n_expert, n_tensor, splits, sub)
    terms = []
    before = {}
    for h in range(splits):
        if 2 * n_expert * rows <= LARGEST:
            nearer = stack_rows(planes[h][:3], [] if before else sum((p[1:] for p in slices[1:2]), []))
            away = [swap(nearer, "seq", 1)]
            if planes[h][3:]:
                away.append(swap(stack_rows(planes[h][3:], before.get("kept", [])), "seq", 1))
            half = n_expert * rows
            everything = planes[h] + away
            tile = tile_of(w_gate)
            count = w_gate.shape[2] // tile
            cuts = [0, (count + 1) // 2, count - 1, count] if h else [0, count]
            ties = [before.get(key, []) for key in ("packed", "passed", "totals")]
            hidden = [
                hidden_rows(
                    everything, w_gate, w_up, ties[i], cuts[i], cuts[i + 1] - cuts[i], tile
                )
                for i in range(len(cuts) - 1)
            ]
            later = planes[h + 1][1:3] if h + 1 < splits else []
            other = down_rows(hidden, w_down, half, half, later + before.get("sums", []))
            kept = down_rows(hidden, w_down, 0, half, before.get("final", []))
        else:
            away = [swap(p, "seq", 1) for p in planes[h]]
            kept, other = many_rows(planes[h], w_gate, w_up, w_down), many_rows(
                away, w_gate, w_up, w_down
            )
        got = swap(other, "seq", 1)
        totals, packed, passed = sum_plane(kept, got, rows, before.get("column", []))
        sums = [swap(totals[d], "tensor", d) for d in range(1, n_tensor)]
        cut = []
        if before:
            column = stack_rows([before["final"][0]] + before["column"], totals[:1])
            plane, cut = gather_plane(column, "expert", [])
            wanted = target_rows[:, :, h - 1].reshape(1, -1)
            terms.append(head_terms(plane, head_rows, wanted, sub))
        final = final_rows(totals[:1] + sums, raws[h], gains, [])
        column = gather_near(final, "tensor")
        before = {
            "kept": [kept],
            "packed": packed,
            "passed": passed,
            "totals": totals,
            "sums": sums,
            "final": [final],
            "column": column[1:],
        }
    column = stack_rows(column, cut)
    plane, _ = gather_plane(column, "expert", terms[-1:])
    wanted = target_rows[:, :, splits - 1].reshape(1, -1)
    terms.append(head_terms(plane, head_rows, wanted, sub))
    terms = [term[:3].reshape(3, n_expert, n_tensor, sub) for term in terms]
    terms = jnp.stack(terms, axis=3)
    joined = join_axis(terms, "tensor", 2, my_tensor)
    joined = join_axis(joined, "expert", 1, my_expert)
    return (joined[0] + jnp.log(joined[1]) - joined[2]).reshape(own)


def solution(mesh):
    return jax.shard_map(
        on_device,
        mesh=mesh,
        in_specs=(
            P(("seq", "expert"), "tensor"),
            P(("seq", "expert"), None),
            P(("seq", "expert"), None),
            P("tensor"),
            P("tensor"),
            P("expert", None, ("seq", "tensor")),
            P("expert", None, ("seq", "tensor")),
            P("expert", ("seq", "tensor"), None),
            P(None, ("expert", "tensor")),
            P("seq"),
        ),
        out_specs=P(("seq", "expert", "tensor")),
        check_vma=False,
    )
```

```python
import functools

import jax
import jax.numpy as jnp
from jax import lax
from jax.experimental import pallas as pl
from jax.experimental.pallas import tpu as pltpu
from jax.sharding import PartitionSpec as P

epsilon = 1e-05
LANES = 128
LARGEST = 512
MIB = 1024 * 1024
VMEM_BYTES = 56 * 1024 * 1024


def params(limit=VMEM_BYTES):
    return pltpu.CompilerParams(vmem_limit_bytes=limit)


def whole():
    return pl.BlockSpec(memory_space=pltpu.VMEM)


def anywhere():
    return pl.BlockSpec(memory_space=pl.ANY)


def swap(x, axis, distance):
    size = lax.axis_size(axis)
    return lax.ppermute(x, axis, [(i, i ^ distance) for i in range(size)])


def gather_near(x, axis):
    return [x] + swap_each([x] * (lax.axis_size(axis) - 1), axis)


def swap_each(pieces, axis):
    return [swap(piece, axis, d + 1) for d, piece in enumerate(pieces)]


def far_first(pieces):
    return pieces[:1] + pieces[1:][::-1]


def gather_plane(x, axis, after):
    if lax.axis_size(axis) != 4:
        return gather_near(x, axis), []
    half = x.shape[0] // 2
    one, two = swap(x, axis, 1), swap(x, axis, 2)
    upper, lower = move_rows([two, one], [(0, 0, half, 0, 0), (1, half, half, 1, 0)], after)
    return [x, one, two, swap(upper, axis, 1), swap(lower, axis, 2)], [upper, lower]


def move_kernel(sources, targets, moves, *refs):
    out_refs, sems = refs[-targets - 1 : -1], refs[-1]
    copies = []
    for i, (source, start, count, target, place) in enumerate(moves):
        copies.append(
            pltpu.make_async_copy(
                refs[source].at[pl.ds(start, count), :],
                out_refs[target].at[pl.ds(place, count), :],
                sems.at[i],
            )
        )
    for copy in copies:
        copy.start()
    for copy in copies:
        copy.wait()


def move_rows(arrays, moves, after):
    targets = 1 + max(m[3] for m in moves)
    sizes = [sum(m[2] for m in moves if m[3] == t) for t in range(targets)]
    size = sum(sizes) * arrays[0].shape[1]
    return pl.pallas_call(
        functools.partial(move_kernel, len(arrays), targets, moves),
        out_shape=tuple(
            jax.ShapeDtypeStruct((rows, arrays[0].shape[1]), arrays[0].dtype) for rows in sizes
        ),
        in_specs=[anywhere()] * (len(arrays) + len(after)),
        out_specs=(anywhere(),) * targets,
        scratch_shapes=[pltpu.SemaphoreType.DMA((len(moves),))],
        compiler_params=params(MIB),
        cost_estimate=pl.CostEstimate(flops=0, bytes_accessed=4 * size, transcendentals=0),
        name="move_rows",
    )(*arrays, *after)


def stack_rows(arrays, after):
    moves = []
    place = 0
    for i, x in enumerate(arrays):
        moves.append((i, 0, x.shape[0], 0, place))
        place += x.shape[0]
    return move_rows(arrays, moves, after)[0]


def stack_line(pieces, after):
    count, size = len(pieces), pieces[0].shape[0]
    moves = [(i, 0, size, 0, (count - i if i else 0) * size) for i in range(count)]
    return move_rows(far_first(pieces), moves, after)[0]


def load_pieces(piece_refs, scratch, sems):
    copies = []
    start = 0
    for i in range(len(piece_refs)):
        count = piece_refs[i].shape[0]
        copies.append(
            pltpu.make_async_copy(piece_refs[i], scratch.at[pl.ds(start, count), :], sems.at[i])
        )
        start += count
    for copy in copies:
        copy.start()
    for copy in copies:
        copy.wait()


def begin_kernel(count, splits, *refs):
    block_refs, (tokens_scr, gains_scr, sems) = refs[3 : 3 + splits], refs[3 + splits :]
    targets = [tokens_scr, gains_scr.at[0], gains_scr.at[1]]
    copies = [pltpu.make_async_copy(refs[i], targets[i], sems.at[i]) for i in range(3)]
    for copy in copies:
        copy.start()
    for copy in copies:
        copy.wait()
    own_rows = tokens_scr.shape[0] // (count * splits)
    for i in range(count):
        for h in range(splits):
            start = (i * splits + h) * own_rows
            block_refs[h][i * own_rows : (i + 1) * own_rows, :] = tokens_scr[
                start : start + own_rows, :
            ]
    lines = []
    for i in range(2):
        gain = gains_scr[i]
        high = gain.astype(jnp.bfloat16).astype(jnp.float32)
        middle = (gain - high).astype(jnp.bfloat16).astype(jnp.float32)
        lines += [high, middle, gain - high - middle]
    lines.append(jnp.zeros((2, lines[0].shape[1]), jnp.float32))
    block_refs[0][count * own_rows :, :] = jnp.concatenate(lines).astype(jnp.bfloat16)


def begin(tokens, norm_gain, final_gain, count, splits):
    rows, width = tokens.shape
    sizes = [rows // splits + (0 if h else 8) for h in range(splits)]
    return pl.pallas_call(
        functools.partial(begin_kernel, count, splits),
        out_shape=tuple(jax.ShapeDtypeStruct((size, width), jnp.bfloat16) for size in sizes),
        in_specs=[anywhere()] * 3,
        out_specs=(whole(),) * splits,
        scratch_shapes=[
            pltpu.VMEM((rows, width), jnp.bfloat16),
            pltpu.VMEM((2, 1, width), jnp.float32),
            pltpu.SemaphoreType.DMA((3,)),
        ],
        compiler_params=params(4 * MIB),
        name="begin",
    )(
        pltpu.with_memory_space_constraint(tokens, pltpu.HBM),
        pltpu.with_memory_space_constraint(norm_gain.reshape(1, width), pltpu.HBM),
        pltpu.with_memory_space_constraint(final_gain.reshape(1, width), pltpu.HBM),
    )


def norm_kernel(splits, part, count, after, *refs):
    slices = refs[:1] + refs[1:count][::-1]
    routes_ref, weights_ref = refs[count : count + 2]
    rest = list(refs[count + 2 :])
    gains_in = rest.pop(0) if part else None
    rest = rest[after:]
    rows_ref, raw_ref = rest[:2]
    gains_ref = gains_in if part else rest[2]
    rows = rows_ref.shape[0]
    width = slices[0].shape[1]
    full_width = width * count
    own_rows = rows // count
    me = lax.axis_index("tensor")
    total = jnp.zeros((rows, 1), jnp.float32)
    for piece in slices:
        value = piece[:rows, :].astype(jnp.float32)
        total = total + jnp.sum(value * value, axis=1, keepdims=True)
    scale = lax.rsqrt(total / full_width + epsilon)
    start = pl.multiple_of(me * own_rows, own_rows)
    for d in range(count):
        columns = pl.ds(pl.multiple_of((me ^ d) * width, width), width)
        if not part:
            tail = slices[d][rows:, :].astype(jnp.float32)
            gains_ref[0:1, columns] = tail[0:1] + tail[1:2] + tail[2:3]
            gains_ref[1:2, columns] = tail[3:4] + tail[4:5] + tail[5:6]
        value = slices[d][:rows, :].astype(jnp.float32)
        rows_ref[:, columns] = (value * scale * gains_ref[0:1, columns]).astype(jnp.bfloat16)
        raw_ref[:, columns] = slices[d][pl.ds(start, own_rows), :]
    lane = lax.broadcasted_iota(jnp.int32, (own_rows, LANES), 1)
    expert = lane // 3
    kind = lane - expert * 3
    for i in range(count):
        block = pl.ds((i * splits + part) * own_rows, own_rows)
        weight = jnp.zeros((own_rows, LANES), jnp.float32)
        for j in range(routes_ref.shape[1]):
            named = routes_ref[block, j : j + 1] == expert
            weight = weight + jnp.where(named, weights_ref[block, j : j + 1], 0.0)
        high = weight.astype(jnp.bfloat16).astype(jnp.float32)
        middle = (weight - high).astype(jnp.bfloat16).astype(jnp.float32)
        low = weight - high - middle
        value = jnp.where(kind == 0, high, jnp.where(kind == 1, middle, low))
        rows_ref[i * own_rows : (i + 1) * own_rows, full_width:] = value.astype(jnp.bfloat16)


def norm_rows(slices, gains, routes, route_weights, splits, part, rows, after):
    width = slices[0].shape[1]
    count = len(slices)
    full_width = width * count
    gains = gains if part else []
    made = [] if part else [jax.ShapeDtypeStruct((8, full_width), jnp.float32)]
    return pl.pallas_call(
        functools.partial(norm_kernel, splits, part, count, len(after)),
        out_shape=(
            jax.ShapeDtypeStruct((rows, full_width + LANES), jnp.bfloat16),
            jax.ShapeDtypeStruct((rows // count, full_width), jnp.bfloat16),
            *made,
        ),
        in_specs=[whole()] * (count + 2 + len(gains)) + [anywhere()] * len(after),
        out_specs=(whole(),) * (2 + len(made)),
        compiler_params=params(6 * MIB),
        cost_estimate=pl.CostEstimate(
            flops=6 * rows * full_width, bytes_accessed=4 * rows * full_width, transcendentals=rows
        ),
        name="norm_rows",
    )(*far_first(slices), routes, route_weights, *gains, *after)


def hidden_kernel(pieces, after, tile, first, steps, *refs):
    piece_refs = refs[:pieces]
    weight_refs = refs[pieces : pieces + 2]
    out_ref, rows_scr, route_scr, weight_scr, sems, weight_sems = refs[pieces + 2 + after :]
    full_width = weight_scr.shape[2]

    def fetch(i, act):
        columns = pl.ds((first + i) * tile, tile)
        for j in range(2):
            act(
                pltpu.make_async_copy(
                    weight_refs[j].at[0, :, columns],
                    weight_scr.at[j, i % 2],
                    weight_sems.at[j, i % 2],
                )
            )

    def start(copy):
        copy.start()

    def wait(copy):
        copy.wait()

    fetch(0, start)
    load_pieces(piece_refs, rows_scr, sems)
    small = rows_scr[:, full_width:].astype(jnp.float32)
    lane = lax.broadcasted_iota(jnp.int32, small.shape, 1)
    place = lax.axis_index("expert") * 3
    mine = (lane >= place) & (lane < place + 3)
    weight = jnp.sum(jnp.where(mine, small, 0.0), axis=1, keepdims=True)
    route_scr[...] = jnp.broadcast_to(0.5 * weight, route_scr.shape)
    for i in range(steps):
        fetch(i, wait)
        if i + 1 < steps:
            fetch(i + 1, start)
        rows = rows_scr[:, :full_width]
        gate = jnp.dot(rows, weight_scr[0, i % 2], preferred_element_type=jnp.float32)
        up = jnp.dot(rows, weight_scr[1, i % 2], preferred_element_type=jnp.float32)
        hidden = gate * (1.0 + jnp.tanh(0.5 * gate)) * up * route_scr[:, :1]
        out_ref[:, i * tile : (i + 1) * tile] = hidden.astype(jnp.bfloat16)


def tile_of(weight):
    hidden = weight.shape[2]
    return next(t for t in (256, 128, hidden) if hidden % t == 0)


def hidden_rows(pieces, w_gate, w_up, after, first, steps, tile):
    rows = sum(p.shape[0] for p in pieces)
    full_width = w_gate.shape[1]
    hidden = steps * tile
    return pl.pallas_call(
        functools.partial(hidden_kernel, len(pieces), len(after), tile, first, steps),
        out_shape=jax.ShapeDtypeStruct((rows, hidden), jnp.bfloat16),
        in_specs=[anywhere()] * (len(pieces) + 2 + len(after)),
        out_specs=whole(),
        scratch_shapes=[
            pltpu.VMEM((rows, full_width + LANES), jnp.bfloat16),
            pltpu.VMEM((rows, LANES), jnp.float32),
            pltpu.VMEM((2, 2, full_width, tile), jnp.bfloat16),
            pltpu.SemaphoreType.DMA((len(pieces),)),
            pltpu.SemaphoreType.DMA((2, 2)),
        ],
        compiler_params=params((14 + rows // 64) * MIB),
        cost_estimate=pl.CostEstimate(
            flops=4 * rows * full_width * hidden,
            bytes_accessed=4 * full_width * hidden + 2 * rows * (full_width + hidden),
            transcendentals=rows * hidden,
        ),
        name="hidden_rows",
    )(*pieces, w_gate, w_up, *after)


def down_kernel(start, count, *refs):
    hidden_refs, down_ref, out_ref = refs[:count], refs[count], refs[-1]
    full_width = out_ref.shape[1]
    tile = 512 if full_width % 512 == 0 else full_width

    @pl.loop(0, full_width // tile, unroll=True)
    def _(i):
        columns = pl.ds(pl.multiple_of(i * tile, tile), tile)
        out = None
        depth = 0
        for hidden_ref in hidden_refs:
            rows = hidden_ref[start : start + out_ref.shape[0], :]
            block = down_ref[0, depth : depth + rows.shape[1], columns]
            term = jnp.dot(rows, block, preferred_element_type=jnp.float32)
            out = term if out is None else out + term
            depth += rows.shape[1]
        out_ref[:, columns] = out.astype(jnp.bfloat16)


def down_rows(hidden, w_down, start, rows, after):
    depth, full_width = w_down.shape[1:]
    hidden = [pltpu.with_memory_space_constraint(part, pltpu.VMEM) for part in hidden]
    return pl.pallas_call(
        functools.partial(down_kernel, start, len(hidden)),
        out_shape=jax.ShapeDtypeStruct((rows, full_width), jnp.bfloat16),
        in_specs=[whole()] * (len(hidden) + 1) + [anywhere()] * len(after),
        out_specs=whole(),
        compiler_params=params((4 + rows // 64) * MIB),
        cost_estimate=pl.CostEstimate(
            flops=2 * rows * depth * full_width,
            bytes_accessed=2 * rows * (depth + full_width),
            transcendentals=0,
        ),
        name="down_rows",
    )(*hidden, w_down, *after)


def many_rows(pieces, w_gate, w_up, w_down):
    outs = []
    tile = tile_of(w_gate)
    steps = w_gate.shape[2] // tile
    while pieces:
        count = 1
        while count < len(pieces) and sum(p.shape[0] for p in pieces[: count + 1]) <= LARGEST:
            count += 1
        hidden = hidden_rows(pieces[:count], w_gate, w_up, [], 0, steps, tile)
        outs.append(down_rows([hidden], w_down, 0, hidden.shape[0], []))
        pieces = pieces[count:]
    return jnp.concatenate(outs)


def final_kernel(parts, *refs):
    part_refs = refs[: parts + 2]
    out_ref, rows_scr, gains_scr, sems = refs[-4:]
    targets = [rows_scr.at[i] for i in range(parts + 1)] + [gains_scr]
    copies = [
        pltpu.make_async_copy(part_refs[i], targets[i], sems.at[i]) for i in range(parts + 2)
    ]
    for copy in copies:
        copy.start()
    for copy in copies:
        copy.wait()
    mixed = rows_scr[0].astype(jnp.float32)
    for i in range(1, parts):
        mixed = mixed + rows_scr[i].astype(jnp.float32)
    residual = rows_scr[parts].astype(jnp.float32) + mixed
    residual = residual.astype(jnp.bfloat16).astype(jnp.float32)
    total = jnp.sum(residual * residual, axis=1, keepdims=True)
    scale = lax.rsqrt(total / residual.shape[1] + epsilon)
    out_ref[...] = (residual * scale * gains_scr[1:2, :]).astype(jnp.bfloat16)


def final_rows(parts, raw, gains, after):
    rows, full_width = raw.shape
    return pl.pallas_call(
        functools.partial(final_kernel, len(parts)),
        out_shape=jax.ShapeDtypeStruct((rows, full_width), jnp.bfloat16),
        in_specs=[anywhere()] * (len(parts) + 2 + len(after)),
        out_specs=whole(),
        scratch_shapes=[
            pltpu.VMEM((len(parts) + 1, rows, full_width), jnp.bfloat16),
            pltpu.VMEM(gains.shape, jnp.float32),
            pltpu.SemaphoreType.DMA((len(parts) + 2,)),
        ],
        compiler_params=params(6 * MIB),
        cost_estimate=pl.CostEstimate(
            flops=8 * rows * full_width, bytes_accessed=12 * rows * full_width, transcendentals=rows
        ),
        name="final_rows",
    )(*parts, raw, gains, *after)


def head_kernel(pieces, tile, sub, *refs):
    piece_refs = refs[:pieces]
    head_ref, target_ref, out_ref, rows_scr, head_scr, sems, head_sems = refs[pieces:]
    vocab_part = head_ref.shape[0]
    steps = vocab_part // tile
    my_expert, my_tensor = lax.axis_index("expert"), lax.axis_index("tensor")
    n_tensor = lax.axis_size("tensor")

    def fetch(i):
        return pltpu.make_async_copy(
            head_ref.at[pl.ds(i * tile, tile), :],
            head_scr.at[i],
            head_sems.at[i],
        )

    copies = []
    for piece_ref in piece_refs:
        for start in range(0, piece_ref.shape[0], sub):
            far_expert, far_tensor = divmod(len(copies), n_tensor)
            block = (my_expert ^ far_expert) * n_tensor + (my_tensor ^ far_tensor)
            copies.append(
                pltpu.make_async_copy(
                    piece_ref.at[pl.ds(start, sub), :],
                    rows_scr.at[pl.ds(pl.multiple_of(block * sub, sub), sub), :],
                    sems.at[len(copies)],
                )
            )
    ahead = min(2, steps)
    fetch(0).start()
    for copy in copies:
        copy.start()
    for i in range(1, ahead):
        fetch(i).start()
    for copy in copies:
        copy.wait()
    lane = lax.broadcasted_iota(jnp.int32, out_ref.shape, 0)
    out_ref[...] = jnp.where(lane == 0, -jnp.inf, 0.0)
    targets = target_ref[...] - (my_expert * n_tensor + my_tensor) * vocab_part

    for i in range(steps):
        fetch(i).wait()
        if i + ahead < steps:
            fetch(i + ahead).start()
        logits = lax.dot_general(
            head_scr[i],
            rows_scr[...],
            (((1,), (1,)), ((), ())),
            preferred_element_type=jnp.float32,
        )
        word = lax.broadcasted_iota(jnp.int32, logits.shape, 0) + i * tile
        old_top, old_total = out_ref[0:1, :], out_ref[1:2, :]
        top = jnp.maximum(old_top, jnp.max(logits, axis=0, keepdims=True))
        out_ref[0:1, :] = top
        out_ref[1:2, :] = old_total * jnp.exp(old_top - top) + jnp.sum(
            jnp.exp(logits - top), axis=0, keepdims=True
        )
        hit = word == targets
        out_ref[2:3, :] += jnp.sum(jnp.where(hit, logits, 0.0), axis=0, keepdims=True)


def head_terms(pieces, head_rows, targets, sub):
    rows = sum(p.shape[0] for p in pieces)
    vocab_part, full_width = head_rows.shape
    tile = next(t for t in (400, 200, 80, 8, vocab_part) if vocab_part % t == 0)
    return pl.pallas_call(
        functools.partial(head_kernel, len(pieces), tile, sub),
        out_shape=jax.ShapeDtypeStruct((8, rows), jnp.float32),
        in_specs=[anywhere()] * (len(pieces) + 1) + [whole()],
        out_specs=whole(),
        scratch_shapes=[
            pltpu.VMEM((rows, full_width), jnp.bfloat16),
            pltpu.VMEM((vocab_part // tile, tile, full_width), jnp.bfloat16),
            pltpu.SemaphoreType.DMA((rows // sub,)),
            pltpu.SemaphoreType.DMA((vocab_part // tile,)),
        ],
        compiler_params=params((22 + rows // 64) * MIB),
        cost_estimate=pl.CostEstimate(
            flops=2 * rows * full_width * vocab_part,
            bytes_accessed=2 * full_width * (vocab_part + rows),
            transcendentals=rows * vocab_part,
        ),
        name="head_terms",
    )(*pieces, head_rows, targets)


def join_terms(parts):
    top = functools.reduce(jnp.maximum, [p[0] for p in parts])
    total = sum(p[1] * jnp.exp(p[0] - top) for p in parts)
    target = sum(p[2] for p in parts)
    return jnp.stack([top, total, target])


def join_axis(terms, axis, place, me):
    def of(d):
        return lax.dynamic_index_in_dim(terms, me ^ d, place, False)

    return join_terms([of(0)] + [swap(of(d), axis, d) for d in range(1, lax.axis_size(axis))])


def pack_kernel(kept_ref, got_ref, one_ref, two_ref, home_ref, side_ref):
    rows = home_ref.shape[0]
    half = rows // 2

    def both(d, first):
        block = slice(d * rows + first, d * rows + first + half)
        return kept_ref[block, :].astype(jnp.float32) + got_ref[block, :].astype(jnp.float32)

    one_ref[:half, :] = both(1, 0).astype(jnp.bfloat16)
    one_ref[half:, :] = both(3, 0).astype(jnp.bfloat16)
    two_ref[:half, :] = both(2, half).astype(jnp.bfloat16)
    two_ref[half:, :] = both(3, half).astype(jnp.bfloat16)
    home_ref[:half, :] = both(0, 0)
    home_ref[half:, :] = both(0, half)
    side_ref[0] = both(1, half)
    side_ref[1] = both(2, 0)


def pass_kernel(side_ref, one_ref, two_ref, *refs):
    pass_one_ref, pass_two_ref = refs[-2:]
    half = pass_one_ref.shape[0]
    pass_one_ref[...] = (side_ref[0] + two_ref[half:, :].astype(jnp.float32)).astype(jnp.bfloat16)
    pass_two_ref[...] = (side_ref[1] + one_ref[half:, :].astype(jnp.float32)).astype(jnp.bfloat16)


def total_kernel(count, home_ref, one_ref, two_ref, last_one_ref, last_two_ref, *refs):
    outs, work = refs[-count - 1 : -1], refs[-1]
    half = last_one_ref.shape[0]
    sub = outs[0].shape[0]
    me = lax.axis_index("tensor")
    upper = one_ref[:half, :].astype(jnp.float32) + last_two_ref[...].astype(jnp.float32)
    lower = two_ref[:half, :].astype(jnp.float32) + last_one_ref[...].astype(jnp.float32)
    work[:half, :] = home_ref[:half, :] + upper
    work[half:, :] = home_ref[half:, :] + lower
    for d in range(count):
        block = pl.ds(pl.multiple_of((me ^ d) * sub, sub), sub)
        outs[d][...] = work[block, :].astype(jnp.bfloat16)


def small_call(kernel, name, inputs, after, outs, scratch, limit):
    size = sum(x.size * x.dtype.itemsize for x in inputs)
    return pl.pallas_call(
        kernel,
        out_shape=tuple(jax.ShapeDtypeStruct(*out) for out in outs),
        in_specs=[whole()] * len(inputs) + [anywhere()] * len(after),
        out_specs=(whole(),) * len(outs),
        scratch_shapes=scratch,
        compiler_params=params(limit),
        cost_estimate=pl.CostEstimate(flops=size, bytes_accessed=2 * size, transcendentals=0),
        name=name,
    )(*inputs, *after)


def sum_plane(kept, got, rows, after_pass):
    f32, b16 = jnp.float32, jnp.bfloat16
    n_tensor = lax.axis_size("tensor")
    count, full_width = kept.shape[0] // rows, kept.shape[1]
    half = rows // 2
    sub = rows // n_tensor
    if count == 4 and half % 16 == 0 and sub % 16 == 0:
        one, two, home, side = small_call(
            pack_kernel,
            "pack",
            [kept, got],
            [],
            [((rows, full_width), b16)] * 2
            + [((rows, full_width), f32), ((2, half, full_width), f32)],
            [],
            10 * MIB,
        )
        from_one, from_two = swap(one, "expert", 1), swap(two, "expert", 2)
        pass_one, pass_two = small_call(
            pass_kernel,
            "pass_on",
            [side, from_one, from_two],
            after_pass,
            [((half, full_width), b16)] * 2,
            [],
            6 * MIB,
        )
        last_one, last_two = swap(pass_one, "expert", 1), swap(pass_two, "expert", 2)
        pieces = small_call(
            functools.partial(total_kernel, n_tensor),
            "total",
            [home, from_one, from_two, last_one, last_two],
            [],
            [((sub, full_width), b16)] * n_tensor,
            [pltpu.VMEM((rows, full_width), f32)],
            8 * MIB,
        )
        return list(pieces), [one, two], [pass_one, pass_two]
    both = (kept.astype(f32) + got.astype(f32)).reshape(count, rows, full_width)
    total = both[0]
    for d in range(1, count):
        total = total + swap(both[d].astype(b16), "expert", d).astype(f32)
    total = total.astype(b16).reshape(n_tensor, sub, full_width)
    me = lax.axis_index("tensor")
    pieces = [lax.dynamic_index_in_dim(total, me ^ d, 0, False) for d in range(n_tensor)]
    return pieces, [], []


def on_device(
    tokens, routes, route_weights, norm_gain, final_gain, w_gate, w_up, w_down, head_weight, targets
):
    tok_rows, width = tokens.shape
    n_expert = lax.axis_size("expert")
    n_tensor = lax.axis_size("tensor")
    my_expert = lax.axis_index("expert")
    my_tensor = lax.axis_index("tensor")
    full_width = width * n_tensor
    own = tok_rows // n_tensor
    splits = 2 if own % 32 == 0 else 1
    sub = own // splits
    rows = sub * n_tensor

    blocks = begin(tokens, norm_gain, final_gain, n_tensor, splits)
    slices = [gather_near(block, "tensor") for block in blocks]
    gains = None
    planes, raws = [], []
    after = []
    for h in range(splits):
        normed, raw, *made = norm_rows(
            slices[h], [gains], routes, route_weights, splits, h, rows, after
        )
        if made:
            gains = made[0]
        plane, _ = gather_plane(normed, "expert", [])
        planes.append(plane)
        raws.append(raw)
        after = plane[3:]

    w_gate = pltpu.with_memory_space_constraint(w_gate, pltpu.HBM)
    w_up = pltpu.with_memory_space_constraint(w_up, pltpu.HBM)
    head_rows = pltpu.with_memory_space_constraint(head_weight.T, pltpu.HBM)
    target_rows = targets.reshape(n_expert, n_tensor, splits, sub)
    terms = []
    before = {}
    for h in range(splits):
        if 2 * n_expert * rows <= LARGEST:
            nearer = stack_rows(planes[h][:3], [] if before else sum((p[:0:-1] for p in slices[1:2]), []))
            away = [swap(nearer, "seq", 1)]
            if planes[h][3:]:
                away.append(swap(stack_rows(planes[h][3:], before.get("kept", [])), "seq", 1))
            half = n_expert * rows
            everything = planes[h] + away
            tile = tile_of(w_gate)
            count = w_gate.shape[2] // tile
            cuts = [0, (count + 1) // 2, count - 1, count] if h else [0, count]
            ties = [before.get(key, []) for key in ("packed", "passed", "totals")]
            hidden = [
                hidden_rows(
                    everything, w_gate, w_up, ties[i], cuts[i], cuts[i + 1] - cuts[i], tile
                )
                for i in range(len(cuts) - 1)
            ]
            later = planes[h + 1][1:3] if h + 1 < splits else []
            other = down_rows(hidden, w_down, half, half, later + before.get("sums", [])[::-1])
            kept = down_rows(hidden, w_down, 0, half, before.get("final", []))
        else:
            away = [swap(p, "seq", 1) for p in planes[h]]
            kept, other = many_rows(planes[h], w_gate, w_up, w_down), many_rows(
                away, w_gate, w_up, w_down
            )
        got = swap(other, "seq", 1)
        totals, packed, passed = sum_plane(kept, got, rows, before.get("column", [])[::-1])
        sums = swap_each(totals[1:], "tensor")
        cut = []
        if before:
            column = stack_line(before["final"] + before["column"], totals[:1])
            plane, cut = gather_plane(column, "expert", [])
            wanted = target_rows[:, :, h - 1].reshape(1, -1)
            terms.append(head_terms(plane, head_rows, wanted, sub))
        final = final_rows(far_first(totals[:1] + sums), raws[h], gains, [])
        column = gather_near(final, "tensor")
        before = {
            "kept": [kept],
            "packed": packed,
            "passed": passed,
            "totals": totals,
            "sums": sums,
            "final": [final],
            "column": column[1:],
        }
    column = stack_line(column, cut)
    plane, _ = gather_plane(column, "expert", terms[-1:])
    wanted = target_rows[:, :, splits - 1].reshape(1, -1)
    terms.append(head_terms(plane, head_rows, wanted, sub))
    terms = [term[:3].reshape(3, n_expert, n_tensor, sub) for term in terms]
    terms = jnp.stack(terms, axis=3)
    joined = join_axis(terms, "tensor", 2, my_tensor)
    joined = join_axis(joined, "expert", 1, my_expert)
    return (joined[0] + jnp.log(joined[1]) - joined[2]).reshape(own)


def solution(mesh):
    return jax.shard_map(
        on_device,
        mesh=mesh,
        in_specs=(
            P(("seq", "expert"), "tensor"),
            P(("seq", "expert"), None),
            P(("seq", "expert"), None),
            P("tensor"),
            P("tensor"),
            P("expert", None, ("seq", "tensor")),
            P("expert", None, ("seq", "tensor")),
            P("expert", ("seq", "tensor"), None),
            P(None, ("expert", "tensor")),
            P("seq"),
        ),
        out_specs=P(("seq", "expert", "tensor")),
        check_vma=False,
    )
```

```python
import functools

import jax
import jax.numpy as jnp
from jax import lax
from jax.experimental import pallas as pl
from jax.experimental.pallas import tpu as pltpu
from jax.sharding import PartitionSpec as P

epsilon = 1e-05
LANES = 128
SLOTS = 3
LARGEST = 512
MIB = 1024 * 1024
VMEM_BYTES = 56 * 1024 * 1024


def params(limit=VMEM_BYTES):
    return pltpu.CompilerParams(vmem_limit_bytes=limit)


def whole():
    return pl.BlockSpec(memory_space=pltpu.VMEM)


def anywhere():
    return pl.BlockSpec(memory_space=pl.ANY)


def swap(x, axis, distance):
    size = lax.axis_size(axis)
    return lax.ppermute(x, axis, [(i, i ^ distance) for i in range(size)])


def gather_near(x, axis):
    return [x] + swap_each([x] * (lax.axis_size(axis) - 1), axis)


def swap_each(pieces, axis):
    return [swap(piece, axis, d + 1) for d, piece in enumerate(pieces)]


def far_first(pieces):
    return pieces[:1] + pieces[1:][::-1]


def gather_plane(x, axis, after):
    if lax.axis_size(axis) != 4:
        return gather_near(x, axis), []
    half = x.shape[0] // 2
    one, two = swap(x, axis, 1), swap(x, axis, 2)
    upper, lower = move_rows([two, one], [(0, 0, half, 0, 0), (1, half, half, 1, 0)], after)
    return [x, one, two, swap(upper, axis, 1), swap(lower, axis, 2)], [upper, lower]


def move_kernel(sources, targets, moves, *refs):
    out_refs, sems = refs[-targets - 1 : -1], refs[-1]
    copies = []
    for i, (source, start, count, target, place) in enumerate(moves):
        copies.append(
            pltpu.make_async_copy(
                refs[source].at[pl.ds(start, count), :],
                out_refs[target].at[pl.ds(place, count), :],
                sems.at[i],
            )
        )
    for copy in copies:
        copy.start()
    for copy in copies:
        copy.wait()


def move_rows(arrays, moves, after):
    targets = 1 + max(m[3] for m in moves)
    sizes = [sum(m[2] for m in moves if m[3] == t) for t in range(targets)]
    size = sum(sizes) * arrays[0].shape[1]
    return pl.pallas_call(
        functools.partial(move_kernel, len(arrays), targets, moves),
        out_shape=tuple(
            jax.ShapeDtypeStruct((rows, arrays[0].shape[1]), arrays[0].dtype) for rows in sizes
        ),
        in_specs=[anywhere()] * (len(arrays) + len(after)),
        out_specs=(anywhere(),) * targets,
        scratch_shapes=[pltpu.SemaphoreType.DMA((len(moves),))],
        compiler_params=params(MIB),
        cost_estimate=pl.CostEstimate(flops=0, bytes_accessed=4 * size, transcendentals=0),
        name="move_rows",
    )(*arrays, *after)


def stack_rows(arrays, after):
    moves = []
    place = 0
    for i, x in enumerate(arrays):
        moves.append((i, 0, x.shape[0], 0, place))
        place += x.shape[0]
    return move_rows(arrays, moves, after)[0]


def stack_line(pieces, after):
    count, size = len(pieces), pieces[0].shape[0]
    moves = [(i, 0, size, 0, (count - i if i else 0) * size) for i in range(count)]
    return move_rows(far_first(pieces), moves, after)[0]


def load_pieces(piece_refs, scratch, sems):
    copies = []
    start = 0
    for i in range(len(piece_refs)):
        count = piece_refs[i].shape[0]
        copies.append(
            pltpu.make_async_copy(piece_refs[i], scratch.at[pl.ds(start, count), :], sems.at[i])
        )
        start += count
    for copy in copies:
        copy.start()
    for copy in copies:
        copy.wait()


def begin_kernel(count, splits, *refs):
    block_refs, (tokens_scr, gains_scr, sems) = refs[3 : 3 + splits], refs[3 + splits :]
    targets = [tokens_scr, gains_scr.at[0], gains_scr.at[1]]
    copies = [pltpu.make_async_copy(refs[i], targets[i], sems.at[i]) for i in range(3)]
    for copy in copies:
        copy.start()
    for copy in copies:
        copy.wait()
    own_rows = tokens_scr.shape[0] // (count * splits)
    for i in range(count):
        for h in range(splits):
            start = (i * splits + h) * own_rows
            block_refs[h][i * own_rows : (i + 1) * own_rows, :] = tokens_scr[
                start : start + own_rows, :
            ]
    lines = []
    for i in range(2):
        gain = gains_scr[i]
        high = gain.astype(jnp.bfloat16).astype(jnp.float32)
        middle = (gain - high).astype(jnp.bfloat16).astype(jnp.float32)
        lines += [high, middle, gain - high - middle]
    lines.append(jnp.zeros((2, lines[0].shape[1]), jnp.float32))
    block_refs[0][count * own_rows :, :] = jnp.concatenate(lines).astype(jnp.bfloat16)


def begin(tokens, norm_gain, final_gain, count, splits):
    rows, width = tokens.shape
    sizes = [rows // splits + (0 if h else 8) for h in range(splits)]
    return pl.pallas_call(
        functools.partial(begin_kernel, count, splits),
        out_shape=tuple(jax.ShapeDtypeStruct((size, width), jnp.bfloat16) for size in sizes),
        in_specs=[anywhere()] * 3,
        out_specs=(whole(),) * splits,
        scratch_shapes=[
            pltpu.VMEM((rows, width), jnp.bfloat16),
            pltpu.VMEM((2, 1, width), jnp.float32),
            pltpu.SemaphoreType.DMA((3,)),
        ],
        compiler_params=params(4 * MIB),
        name="begin",
    )(
        pltpu.with_memory_space_constraint(tokens, pltpu.HBM),
        pltpu.with_memory_space_constraint(norm_gain.reshape(1, width), pltpu.HBM),
        pltpu.with_memory_space_constraint(final_gain.reshape(1, width), pltpu.HBM),
    )


def norm_kernel(splits, part, count, after, *refs):
    slices = refs[:1] + refs[1:count][::-1]
    routes_ref, weights_ref = refs[count : count + 2]
    rest = list(refs[count + 2 :])
    gains_in = rest.pop(0) if part else None
    rest = rest[after:]
    rows_ref, raw_ref = rest[:2]
    gains_ref = gains_in if part else rest[2]
    rows = rows_ref.shape[0]
    width = slices[0].shape[1]
    full_width = width * count
    own_rows = rows // count
    me = lax.axis_index("tensor")
    total = jnp.zeros((rows, 1), jnp.float32)
    for piece in slices:
        value = piece[:rows, :].astype(jnp.float32)
        total = total + jnp.sum(value * value, axis=1, keepdims=True)
    scale = lax.rsqrt(total / full_width + epsilon)
    start = pl.multiple_of(me * own_rows, own_rows)
    for d in range(count):
        columns = pl.ds(pl.multiple_of((me ^ d) * width, width), width)
        if not part:
            tail = slices[d][rows:, :].astype(jnp.float32)
            gains_ref[0:1, columns] = tail[0:1] + tail[1:2] + tail[2:3]
            gains_ref[1:2, columns] = tail[3:4] + tail[4:5] + tail[5:6]
        value = slices[d][:rows, :].astype(jnp.float32)
        rows_ref[:, columns] = (value * scale * gains_ref[0:1, columns]).astype(jnp.bfloat16)
        raw_ref[:, columns] = slices[d][pl.ds(start, own_rows), :]
    lane = lax.broadcasted_iota(jnp.int32, (own_rows, LANES), 1)
    expert = lane // 3
    kind = lane - expert * 3
    for i in range(count):
        block = pl.ds((i * splits + part) * own_rows, own_rows)
        weight = jnp.zeros((own_rows, LANES), jnp.float32)
        for j in range(routes_ref.shape[1]):
            named = routes_ref[block, j : j + 1] == expert
            weight = weight + jnp.where(named, weights_ref[block, j : j + 1], 0.0)
        high = weight.astype(jnp.bfloat16).astype(jnp.float32)
        middle = (weight - high).astype(jnp.bfloat16).astype(jnp.float32)
        low = weight - high - middle
        value = jnp.where(kind == 0, high, jnp.where(kind == 1, middle, low))
        rows_ref[i * own_rows : (i + 1) * own_rows, full_width:] = value.astype(jnp.bfloat16)


def norm_rows(slices, gains, routes, route_weights, splits, part, rows, after):
    width = slices[0].shape[1]
    count = len(slices)
    full_width = width * count
    gains = gains if part else []
    made = [] if part else [jax.ShapeDtypeStruct((8, full_width), jnp.float32)]
    return pl.pallas_call(
        functools.partial(norm_kernel, splits, part, count, len(after)),
        out_shape=(
            jax.ShapeDtypeStruct((rows, full_width + LANES), jnp.bfloat16),
            jax.ShapeDtypeStruct((rows // count, full_width), jnp.bfloat16),
            *made,
        ),
        in_specs=[whole()] * (count + 2 + len(gains)) + [anywhere()] * len(after),
        out_specs=(whole(),) * (2 + len(made)),
        compiler_params=params(6 * MIB),
        cost_estimate=pl.CostEstimate(
            flops=6 * rows * full_width, bytes_accessed=4 * rows * full_width, transcendentals=rows
        ),
        name="norm_rows",
    )(*far_first(slices), routes, route_weights, *gains, *after)


def hidden_kernel(pieces, after, tile, first, steps, *refs):
    piece_refs = refs[:pieces]
    weight_refs = refs[pieces : pieces + 2]
    out_ref, rows_scr, route_scr, weight_scr, sems, weight_sems = refs[pieces + 2 + after :]
    full_width = weight_scr.shape[2]

    def fetch(i, act):
        columns = pl.ds((first + i) * tile, tile)
        for j in range(2):
            act(
                pltpu.make_async_copy(
                    weight_refs[j].at[0, :, columns],
                    weight_scr.at[j, i % SLOTS],
                    weight_sems.at[j, i % SLOTS],
                )
            )

    def start(copy):
        copy.start()

    def wait(copy):
        copy.wait()

    fetch(0, start)
    load_pieces(piece_refs, rows_scr, sems)
    for i in range(1, min(SLOTS - 1, steps)):
        fetch(i, start)
    small = rows_scr[:, full_width:].astype(jnp.float32)
    lane = lax.broadcasted_iota(jnp.int32, small.shape, 1)
    place = lax.axis_index("expert") * 3
    mine = (lane >= place) & (lane < place + 3)
    weight = jnp.sum(jnp.where(mine, small, 0.0), axis=1, keepdims=True)
    route_scr[...] = jnp.broadcast_to(0.5 * weight, route_scr.shape)
    for i in range(steps):
        fetch(i, wait)
        if i + SLOTS - 1 < steps:
            fetch(i + SLOTS - 1, start)
        rows = rows_scr[:, :full_width]
        gate = jnp.dot(rows, weight_scr[0, i % SLOTS], preferred_element_type=jnp.float32)
        up = jnp.dot(rows, weight_scr[1, i % SLOTS], preferred_element_type=jnp.float32)
        hidden = gate * (1.0 + jnp.tanh(0.5 * gate)) * up * route_scr[:, :1]
        out_ref[:, i * tile : (i + 1) * tile] = hidden.astype(jnp.bfloat16)


def tile_of(weight):
    hidden = weight.shape[2]
    return next(t for t in (256, 128, hidden) if hidden % t == 0)


def hidden_rows(pieces, w_gate, w_up, after, first, steps, tile):
    rows = sum(p.shape[0] for p in pieces)
    full_width = w_gate.shape[1]
    hidden = steps * tile
    return pl.pallas_call(
        functools.partial(hidden_kernel, len(pieces), len(after), tile, first, steps),
        out_shape=jax.ShapeDtypeStruct((rows, hidden), jnp.bfloat16),
        in_specs=[anywhere()] * (len(pieces) + 2 + len(after)),
        out_specs=whole(),
        scratch_shapes=[
            pltpu.VMEM((rows, full_width + LANES), jnp.bfloat16),
            pltpu.VMEM((rows, LANES), jnp.float32),
            pltpu.VMEM((2, SLOTS, full_width, tile), jnp.bfloat16),
            pltpu.SemaphoreType.DMA((len(pieces),)),
            pltpu.SemaphoreType.DMA((2, SLOTS)),
        ],
        compiler_params=params((18 + rows // 64) * MIB),
        cost_estimate=pl.CostEstimate(
            flops=4 * rows * full_width * hidden,
            bytes_accessed=4 * full_width * hidden + 2 * rows * (full_width + hidden),
            transcendentals=rows * hidden,
        ),
        name="hidden_rows",
    )(*pieces, w_gate, w_up, *after)


def down_kernel(start, count, *refs):
    hidden_refs, down_ref, out_ref = refs[:count], refs[count], refs[-1]
    full_width = out_ref.shape[1]
    tile = 512 if full_width % 512 == 0 else full_width

    @pl.loop(0, full_width // tile, unroll=True)
    def _(i):
        columns = pl.ds(pl.multiple_of(i * tile, tile), tile)
        out = None
        depth = 0
        for hidden_ref in hidden_refs:
            rows = hidden_ref[start : start + out_ref.shape[0], :]
            block = down_ref[0, depth : depth + rows.shape[1], columns]
            term = jnp.dot(rows, block, preferred_element_type=jnp.float32)
            out = term if out is None else out + term
            depth += rows.shape[1]
        out_ref[:, columns] = out.astype(jnp.bfloat16)


def down_rows(hidden, w_down, start, rows, after):
    depth, full_width = w_down.shape[1:]
    hidden = [pltpu.with_memory_space_constraint(part, pltpu.VMEM) for part in hidden]
    return pl.pallas_call(
        functools.partial(down_kernel, start, len(hidden)),
        out_shape=jax.ShapeDtypeStruct((rows, full_width), jnp.bfloat16),
        in_specs=[whole()] * (len(hidden) + 1) + [anywhere()] * len(after),
        out_specs=whole(),
        compiler_params=params((4 + rows // 64) * MIB),
        cost_estimate=pl.CostEstimate(
            flops=2 * rows * depth * full_width,
            bytes_accessed=2 * rows * (depth + full_width),
            transcendentals=0,
        ),
        name="down_rows",
    )(*hidden, w_down, *after)


def many_rows(pieces, w_gate, w_up, w_down):
    outs = []
    tile = tile_of(w_gate)
    steps = w_gate.shape[2] // tile
    while pieces:
        count = 1
        while count < len(pieces) and sum(p.shape[0] for p in pieces[: count + 1]) <= LARGEST:
            count += 1
        hidden = hidden_rows(pieces[:count], w_gate, w_up, [], 0, steps, tile)
        outs.append(down_rows([hidden], w_down, 0, hidden.shape[0], []))
        pieces = pieces[count:]
    return jnp.concatenate(outs)


def final_kernel(parts, *refs):
    part_refs = refs[: parts + 2]
    out_ref, rows_scr, gains_scr, sems = refs[-4:]
    targets = [rows_scr.at[i] for i in range(parts + 1)] + [gains_scr]
    copies = [
        pltpu.make_async_copy(part_refs[i], targets[i], sems.at[i]) for i in range(parts + 2)
    ]
    for copy in copies:
        copy.start()
    for copy in copies:
        copy.wait()
    mixed = rows_scr[0].astype(jnp.float32)
    for i in range(1, parts):
        mixed = mixed + rows_scr[i].astype(jnp.float32)
    residual = rows_scr[parts].astype(jnp.float32) + mixed
    residual = residual.astype(jnp.bfloat16).astype(jnp.float32)
    total = jnp.sum(residual * residual, axis=1, keepdims=True)
    scale = lax.rsqrt(total / residual.shape[1] + epsilon)
    out_ref[...] = (residual * scale * gains_scr[1:2, :]).astype(jnp.bfloat16)


def final_rows(parts, raw, gains, after):
    rows, full_width = raw.shape
    return pl.pallas_call(
        functools.partial(final_kernel, len(parts)),
        out_shape=jax.ShapeDtypeStruct((rows, full_width), jnp.bfloat16),
        in_specs=[anywhere()] * (len(parts) + 2 + len(after)),
        out_specs=whole(),
        scratch_shapes=[
            pltpu.VMEM((len(parts) + 1, rows, full_width), jnp.bfloat16),
            pltpu.VMEM(gains.shape, jnp.float32),
            pltpu.SemaphoreType.DMA((len(parts) + 2,)),
        ],
        compiler_params=params(6 * MIB),
        cost_estimate=pl.CostEstimate(
            flops=8 * rows * full_width, bytes_accessed=12 * rows * full_width, transcendentals=rows
        ),
        name="final_rows",
    )(*parts, raw, gains, *after)


def head_kernel(pieces, tile, sub, *refs):
    piece_refs = refs[:pieces]
    head_ref, target_ref, out_ref, rows_scr, head_scr, sems, head_sems = refs[pieces:]
    vocab_part = head_ref.shape[0]
    steps = vocab_part // tile
    my_expert, my_tensor = lax.axis_index("expert"), lax.axis_index("tensor")
    n_tensor = lax.axis_size("tensor")

    def fetch(i):
        return pltpu.make_async_copy(
            head_ref.at[pl.ds(pl.multiple_of(i * tile, tile), tile), :],
            head_scr.at[i],
            head_sems.at[i],
        )

    copies = []
    for piece_ref in piece_refs:
        for start in range(0, piece_ref.shape[0], sub):
            far_expert, far_tensor = divmod(len(copies), n_tensor)
            block = (my_expert ^ far_expert) * n_tensor + (my_tensor ^ far_tensor)
            copies.append(
                pltpu.make_async_copy(
                    piece_ref.at[pl.ds(start, sub), :],
                    rows_scr.at[pl.ds(pl.multiple_of(block * sub, sub), sub), :],
                    sems.at[len(copies)],
                )
            )
    for copy in copies:
        copy.start()
    for i in range(steps):
        fetch(i).start()
    for copy in copies:
        copy.wait()
    lane = lax.broadcasted_iota(jnp.int32, out_ref.shape, 0)
    out_ref[...] = jnp.where(lane == 0, -jnp.inf, 0.0)
    targets = target_ref[...] - (my_expert * n_tensor + my_tensor) * vocab_part

    @pl.loop(0, steps)
    def _(i):
        fetch(i).wait()
        logits = lax.dot_general(
            head_scr[i],
            rows_scr[...],
            (((1,), (1,)), ((), ())),
            preferred_element_type=jnp.float32,
        )
        word = lax.broadcasted_iota(jnp.int32, logits.shape, 0) + i * tile
        old_top, old_total = out_ref[0:1, :], out_ref[1:2, :]
        top = jnp.maximum(old_top, jnp.max(logits, axis=0, keepdims=True))
        out_ref[0:1, :] = top
        out_ref[1:2, :] = old_total * jnp.exp(old_top - top) + jnp.sum(
            jnp.exp(logits - top), axis=0, keepdims=True
        )
        hit = word == targets
        out_ref[2:3, :] += jnp.sum(jnp.where(hit, logits, 0.0), axis=0, keepdims=True)


def head_terms(pieces, head_rows, targets, sub):
    rows = sum(p.shape[0] for p in pieces)
    vocab_part, full_width = head_rows.shape
    tile = next(t for t in (400, 200, 80, 8, vocab_part) if vocab_part % t == 0)
    return pl.pallas_call(
        functools.partial(head_kernel, len(pieces), tile, sub),
        out_shape=jax.ShapeDtypeStruct((8, rows), jnp.float32),
        in_specs=[anywhere()] * (len(pieces) + 1) + [whole()],
        out_specs=whole(),
        scratch_shapes=[
            pltpu.VMEM((rows, full_width), jnp.bfloat16),
            pltpu.VMEM((vocab_part // tile, tile, full_width), jnp.bfloat16),
            pltpu.SemaphoreType.DMA((rows // sub,)),
            pltpu.SemaphoreType.DMA((vocab_part // tile,)),
        ],
        compiler_params=params((22 + rows // 64) * MIB),
        cost_estimate=pl.CostEstimate(
            flops=2 * rows * full_width * vocab_part,
            bytes_accessed=2 * full_width * (vocab_part + rows),
            transcendentals=rows * vocab_part,
        ),
        name="head_terms",
    )(*pieces, head_rows, targets)


def join_terms(parts):
    top = functools.reduce(jnp.maximum, [p[0] for p in parts])
    total = sum(p[1] * jnp.exp(p[0] - top) for p in parts)
    target = sum(p[2] for p in parts)
    return jnp.stack([top, total, target])


def join_axis(terms, axis, place, me):
    def of(d):
        return lax.dynamic_index_in_dim(terms, me ^ d, place, False)

    return join_terms([of(0)] + [swap(of(d), axis, d) for d in range(1, lax.axis_size(axis))])


def pack_kernel(kept_ref, got_ref, one_ref, two_ref, home_ref, side_ref):
    rows = home_ref.shape[0]
    half = rows // 2

    def both(d, first):
        block = slice(d * rows + first, d * rows + first + half)
        return kept_ref[block, :].astype(jnp.float32) + got_ref[block, :].astype(jnp.float32)

    one_ref[:half, :] = both(1, 0).astype(jnp.bfloat16)
    one_ref[half:, :] = both(3, 0).astype(jnp.bfloat16)
    two_ref[:half, :] = both(2, half).astype(jnp.bfloat16)
    two_ref[half:, :] = both(3, half).astype(jnp.bfloat16)
    home_ref[:half, :] = both(0, 0)
    home_ref[half:, :] = both(0, half)
    side_ref[0] = both(1, half)
    side_ref[1] = both(2, 0)


def pass_kernel(side_ref, one_ref, two_ref, *refs):
    pass_one_ref, pass_two_ref = refs[-2:]
    half = pass_one_ref.shape[0]
    pass_one_ref[...] = (side_ref[0] + two_ref[half:, :].astype(jnp.float32)).astype(jnp.bfloat16)
    pass_two_ref[...] = (side_ref[1] + one_ref[half:, :].astype(jnp.float32)).astype(jnp.bfloat16)


def total_kernel(count, home_ref, one_ref, two_ref, last_one_ref, last_two_ref, *refs):
    outs, work = refs[-count - 1 : -1], refs[-1]
    half = last_one_ref.shape[0]
    sub = outs[0].shape[0]
    me = lax.axis_index("tensor")
    upper = one_ref[:half, :].astype(jnp.float32) + last_two_ref[...].astype(jnp.float32)
    lower = two_ref[:half, :].astype(jnp.float32) + last_one_ref[...].astype(jnp.float32)
    work[:half, :] = home_ref[:half, :] + upper
    work[half:, :] = home_ref[half:, :] + lower
    for d in range(count):
        block = pl.ds(pl.multiple_of((me ^ d) * sub, sub), sub)
        outs[d][...] = work[block, :].astype(jnp.bfloat16)


def small_call(kernel, name, inputs, after, outs, scratch, limit):
    size = sum(x.size * x.dtype.itemsize for x in inputs)
    return pl.pallas_call(
        kernel,
        out_shape=tuple(jax.ShapeDtypeStruct(*out) for out in outs),
        in_specs=[whole()] * len(inputs) + [anywhere()] * len(after),
        out_specs=(whole(),) * len(outs),
        scratch_shapes=scratch,
        compiler_params=params(limit),
        cost_estimate=pl.CostEstimate(flops=size, bytes_accessed=2 * size, transcendentals=0),
        name=name,
    )(*inputs, *after)


def sum_plane(kept, got, rows, after_pass):
    f32, b16 = jnp.float32, jnp.bfloat16
    n_tensor = lax.axis_size("tensor")
    count, full_width = kept.shape[0] // rows, kept.shape[1]
    half = rows // 2
    sub = rows // n_tensor
    if count == 4 and half % 16 == 0 and sub % 16 == 0:
        one, two, home, side = small_call(
            pack_kernel,
            "pack",
            [kept, got],
            [],
            [((rows, full_width), b16)] * 2
            + [((rows, full_width), f32), ((2, half, full_width), f32)],
            [],
            10 * MIB,
        )
        from_one, from_two = swap(one, "expert", 1), swap(two, "expert", 2)
        pass_one, pass_two = small_call(
            pass_kernel,
            "pass_on",
            [side, from_one, from_two],
            after_pass,
            [((half, full_width), b16)] * 2,
            [],
            6 * MIB,
        )
        last_one, last_two = swap(pass_one, "expert", 1), swap(pass_two, "expert", 2)
        pieces = small_call(
            functools.partial(total_kernel, n_tensor),
            "total",
            [home, from_one, from_two, last_one, last_two],
            [],
            [((sub, full_width), b16)] * n_tensor,
            [pltpu.VMEM((rows, full_width), f32)],
            8 * MIB,
        )
        return list(pieces), [one, two], [pass_one, pass_two]
    both = (kept.astype(f32) + got.astype(f32)).reshape(count, rows, full_width)
    total = both[0]
    for d in range(1, count):
        total = total + swap(both[d].astype(b16), "expert", d).astype(f32)
    total = total.astype(b16).reshape(n_tensor, sub, full_width)
    me = lax.axis_index("tensor")
    pieces = [lax.dynamic_index_in_dim(total, me ^ d, 0, False) for d in range(n_tensor)]
    return pieces, [], []


def on_device(
    tokens, routes, route_weights, norm_gain, final_gain, w_gate, w_up, w_down, head_weight, targets
):
    tok_rows, width = tokens.shape
    n_expert = lax.axis_size("expert")
    n_tensor = lax.axis_size("tensor")
    my_expert = lax.axis_index("expert")
    my_tensor = lax.axis_index("tensor")
    full_width = width * n_tensor
    own = tok_rows // n_tensor
    splits = 2 if own % 32 == 0 else 1
    sub = own // splits
    rows = sub * n_tensor

    blocks = begin(tokens, norm_gain, final_gain, n_tensor, splits)
    slices = [gather_near(block, "tensor") for block in blocks]
    gains = None
    planes, raws = [], []
    after = []
    for h in range(splits):
        normed, raw, *made = norm_rows(
            slices[h], [gains], routes, route_weights, splits, h, rows, after
        )
        if made:
            gains = made[0]
        plane, _ = gather_plane(normed, "expert", [])
        planes.append(plane)
        raws.append(raw)
        after = plane[3:]

    w_gate = pltpu.with_memory_space_constraint(w_gate, pltpu.HBM)
    w_up = pltpu.with_memory_space_constraint(w_up, pltpu.HBM)
    head_rows = pltpu.with_memory_space_constraint(head_weight.T, pltpu.HBM)
    target_rows = targets.reshape(n_expert, n_tensor, splits, sub)
    terms = []
    before = {}
    for h in range(splits):
        if 2 * n_expert * rows <= LARGEST:
            nearer = stack_rows(planes[h][:3], [] if before else sum((p[:0:-1] for p in slices[1:2]), []))
            away = [swap(nearer, "seq", 1)]
            if planes[h][3:]:
                away.append(swap(stack_rows(planes[h][3:], before.get("kept", [])), "seq", 1))
            half = n_expert * rows
            everything = planes[h] + away
            tile = tile_of(w_gate)
            count = w_gate.shape[2] // tile
            cuts = [0, (count + 1) // 2, count - 1, count] if h else [0, count]
            ties = [before.get(key, []) for key in ("packed", "passed", "totals")]
            hidden = [
                hidden_rows(
                    everything, w_gate, w_up, ties[i], cuts[i], cuts[i + 1] - cuts[i], tile
                )
                for i in range(len(cuts) - 1)
            ]
            later = planes[h + 1][1:3] if h + 1 < splits else []
            other = down_rows(hidden, w_down, half, half, later + before.get("sums", [])[::-1])
            kept = down_rows(hidden, w_down, 0, half, before.get("final", []))
        else:
            away = [swap(p, "seq", 1) for p in planes[h]]
            kept, other = many_rows(planes[h], w_gate, w_up, w_down), many_rows(
                away, w_gate, w_up, w_down
            )
        got = swap(other, "seq", 1)
        totals, packed, passed = sum_plane(kept, got, rows, before.get("column", [])[::-1])
        sums = swap_each(totals[1:], "tensor")
        cut = []
        if before:
            column = stack_line(before["final"] + before["column"], totals[:1])
            plane, cut = gather_plane(column, "expert", [])
            wanted = target_rows[:, :, h - 1].reshape(1, -1)
            terms.append(head_terms(plane, head_rows, wanted, sub))
        final = final_rows(far_first(totals[:1] + sums), raws[h], gains, [])
        column = gather_near(final, "tensor")
        before = {
            "kept": [kept],
            "packed": packed,
            "passed": passed,
            "totals": totals,
            "sums": sums,
            "final": [final],
            "column": column[1:],
        }
    column = stack_line(column, cut)
    plane, _ = gather_plane(column, "expert", terms[-1:])
    wanted = target_rows[:, :, splits - 1].reshape(1, -1)
    terms.append(head_terms(plane, head_rows, wanted, sub))
    terms = [term[:3].reshape(3, n_expert, n_tensor, sub) for term in terms]
    terms = jnp.stack(terms, axis=3)
    joined = join_axis(terms, "tensor", 2, my_tensor)
    joined = join_axis(joined, "expert", 1, my_expert)
    return (joined[0] + jnp.log(joined[1]) - joined[2]).reshape(own)


def solution(mesh):
    return jax.shard_map(
        on_device,
        mesh=mesh,
        in_specs=(
            P(("seq", "expert"), "tensor"),
            P(("seq", "expert"), None),
            P(("seq", "expert"), None),
            P("tensor"),
            P("tensor"),
            P("expert", None, ("seq", "tensor")),
            P("expert", None, ("seq", "tensor")),
            P("expert", ("seq", "tensor"), None),
            P(None, ("expert", "tensor")),
            P("seq"),
        ),
        out_specs=P(("seq", "expert", "tensor")),
        check_vma=False,
    )
```

```python
import functools

import jax
import jax.numpy as jnp
from jax import lax
from jax.experimental import pallas as pl
from jax.experimental.pallas import tpu as pltpu
from jax.sharding import PartitionSpec as P

epsilon = 1e-05
LANES = 128
SLOTS = 3
LARGEST = 512
MIB = 1024 * 1024
VMEM_BYTES = 56 * 1024 * 1024


def params(limit=VMEM_BYTES):
    return pltpu.CompilerParams(vmem_limit_bytes=limit)


def whole():
    return pl.BlockSpec(memory_space=pltpu.VMEM)


def anywhere():
    return pl.BlockSpec(memory_space=pl.ANY)


def swap(x, axis, distance):
    size = lax.axis_size(axis)
    return lax.ppermute(x, axis, [(i, i ^ distance) for i in range(size)])


def gather_near(x, axis):
    return [x] + swap_each([x] * (lax.axis_size(axis) - 1), axis)


def swap_each(pieces, axis):
    return [swap(piece, axis, d + 1) for d, piece in enumerate(pieces)]


def far_first(pieces):
    return pieces[:1] + pieces[1:][::-1]


def gather_plane(x, axis, after):
    if lax.axis_size(axis) != 4:
        return gather_near(x, axis), []
    half = x.shape[0] // 2
    one, two = swap(x, axis, 1), swap(x, axis, 2)
    upper, lower = move_rows([two, one], [(0, 0, half, 0, 0), (1, half, half, 1, 0)], after)
    return [x, one, two, swap(upper, axis, 1), swap(lower, axis, 2)], [upper, lower]


def move_kernel(sources, targets, moves, *refs):
    out_refs, sems = refs[-targets - 1 : -1], refs[-1]
    copies = []
    for i, (source, start, count, target, place) in enumerate(moves):
        copies.append(
            pltpu.make_async_copy(
                refs[source].at[pl.ds(start, count), :],
                out_refs[target].at[pl.ds(place, count), :],
                sems.at[i],
            )
        )
    for copy in copies:
        copy.start()
    for copy in copies:
        copy.wait()


def move_rows(arrays, moves, after):
    targets = 1 + max(m[3] for m in moves)
    sizes = [sum(m[2] for m in moves if m[3] == t) for t in range(targets)]
    size = sum(sizes) * arrays[0].shape[1]
    return pl.pallas_call(
        functools.partial(move_kernel, len(arrays), targets, moves),
        out_shape=tuple(
            jax.ShapeDtypeStruct((rows, arrays[0].shape[1]), arrays[0].dtype) for rows in sizes
        ),
        in_specs=[anywhere()] * (len(arrays) + len(after)),
        out_specs=(anywhere(),) * targets,
        scratch_shapes=[pltpu.SemaphoreType.DMA((len(moves),))],
        compiler_params=params(MIB),
        cost_estimate=pl.CostEstimate(flops=0, bytes_accessed=4 * size, transcendentals=0),
        name="move_rows",
    )(*arrays, *after)


def stack_rows(arrays, after):
    moves = []
    place = 0
    for i, x in enumerate(arrays):
        moves.append((i, 0, x.shape[0], 0, place))
        place += x.shape[0]
    return move_rows(arrays, moves, after)[0]


def stack_line(pieces, after):
    count, size = len(pieces), pieces[0].shape[0]
    moves = [(i, 0, size, 0, (count - i if i else 0) * size) for i in range(count)]
    return move_rows(far_first(pieces), moves, after)[0]


def load_pieces(piece_refs, scratch, sems):
    copies = []
    start = 0
    for i in range(len(piece_refs)):
        count = piece_refs[i].shape[0]
        copies.append(
            pltpu.make_async_copy(piece_refs[i], scratch.at[pl.ds(start, count), :], sems.at[i])
        )
        start += count
    for copy in copies:
        copy.start()
    for copy in copies:
        copy.wait()


def begin_kernel(count, splits, *refs):
    block_refs, (tokens_scr, gains_scr, sems) = refs[3 : 3 + splits], refs[3 + splits :]
    targets = [tokens_scr, gains_scr.at[0], gains_scr.at[1]]
    copies = [pltpu.make_async_copy(refs[i], targets[i], sems.at[i]) for i in range(3)]
    for copy in copies:
        copy.start()
    for copy in copies:
        copy.wait()
    own_rows = tokens_scr.shape[0] // (count * splits)
    for i in range(count):
        for h in range(splits):
            start = (i * splits + h) * own_rows
            block_refs[h][i * own_rows : (i + 1) * own_rows, :] = tokens_scr[
                start : start + own_rows, :
            ]
    lines = []
    for i in range(2):
        gain = gains_scr[i]
        high = gain.astype(jnp.bfloat16).astype(jnp.float32)
        middle = (gain - high).astype(jnp.bfloat16).astype(jnp.float32)
        lines += [high, middle, gain - high - middle]
    lines.append(jnp.zeros((2, lines[0].shape[1]), jnp.float32))
    block_refs[0][count * own_rows :, :] = jnp.concatenate(lines).astype(jnp.bfloat16)


def begin(tokens, norm_gain, final_gain, count, splits):
    rows, width = tokens.shape
    sizes = [rows // splits + (0 if h else 8) for h in range(splits)]
    return pl.pallas_call(
        functools.partial(begin_kernel, count, splits),
        out_shape=tuple(jax.ShapeDtypeStruct((size, width), jnp.bfloat16) for size in sizes),
        in_specs=[anywhere()] * 3,
        out_specs=(whole(),) * splits,
        scratch_shapes=[
            pltpu.VMEM((rows, width), jnp.bfloat16),
            pltpu.VMEM((2, 1, width), jnp.float32),
            pltpu.SemaphoreType.DMA((3,)),
        ],
        compiler_params=params(4 * MIB),
        name="begin",
    )(
        pltpu.with_memory_space_constraint(tokens, pltpu.HBM),
        pltpu.with_memory_space_constraint(norm_gain.reshape(1, width), pltpu.HBM),
        pltpu.with_memory_space_constraint(final_gain.reshape(1, width), pltpu.HBM),
    )


def norm_kernel(splits, part, count, after, *refs):
    slices = refs[:1] + refs[1:count][::-1]
    routes_ref, weights_ref = refs[count : count + 2]
    rest = list(refs[count + 2 :])
    gains_in = rest.pop(0) if part else None
    rest = rest[after:]
    rows_ref, raw_ref = rest[:2]
    gains_ref = gains_in if part else rest[2]
    rows = rows_ref.shape[0]
    width = slices[0].shape[1]
    full_width = width * count
    own_rows = rows // count
    me = lax.axis_index("tensor")
    total = jnp.zeros((rows, 1), jnp.float32)
    for piece in slices:
        value = piece[:rows, :].astype(jnp.float32)
        total = total + jnp.sum(value * value, axis=1, keepdims=True)
    scale = lax.rsqrt(total / full_width + epsilon)
    start = pl.multiple_of(me * own_rows, own_rows)
    for d in range(count):
        columns = pl.ds(pl.multiple_of((me ^ d) * width, width), width)
        if not part:
            tail = slices[d][rows:, :].astype(jnp.float32)
            gains_ref[0:1, columns] = tail[0:1] + tail[1:2] + tail[2:3]
            gains_ref[1:2, columns] = tail[3:4] + tail[4:5] + tail[5:6]
        value = slices[d][:rows, :].astype(jnp.float32)
        rows_ref[:, columns] = (value * scale * gains_ref[0:1, columns]).astype(jnp.bfloat16)
        raw_ref[:, columns] = slices[d][pl.ds(start, own_rows), :]
    lane = lax.broadcasted_iota(jnp.int32, (own_rows, LANES), 1)
    expert = lane // 3
    kind = lane - expert * 3
    for i in range(count):
        block = pl.ds((i * splits + part) * own_rows, own_rows)
        weight = jnp.zeros((own_rows, LANES), jnp.float32)
        for j in range(routes_ref.shape[1]):
            named = routes_ref[block, j : j + 1] == expert
            weight = weight + jnp.where(named, weights_ref[block, j : j + 1], 0.0)
        high = weight.astype(jnp.bfloat16).astype(jnp.float32)
        middle = (weight - high).astype(jnp.bfloat16).astype(jnp.float32)
        low = weight - high - middle
        value = jnp.where(kind == 0, high, jnp.where(kind == 1, middle, low))
        rows_ref[i * own_rows : (i + 1) * own_rows, full_width:] = value.astype(jnp.bfloat16)


def norm_rows(slices, gains, routes, route_weights, splits, part, rows, after):
    width = slices[0].shape[1]
    count = len(slices)
    full_width = width * count
    gains = gains if part else []
    made = [] if part else [jax.ShapeDtypeStruct((8, full_width), jnp.float32)]
    return pl.pallas_call(
        functools.partial(norm_kernel, splits, part, count, len(after)),
        out_shape=(
            jax.ShapeDtypeStruct((rows, full_width + LANES), jnp.bfloat16),
            jax.ShapeDtypeStruct((rows // count, full_width), jnp.bfloat16),
            *made,
        ),
        in_specs=[whole()] * (count + 2 + len(gains)) + [anywhere()] * len(after),
        out_specs=(whole(),) * (2 + len(made)),
        compiler_params=params(6 * MIB),
        cost_estimate=pl.CostEstimate(
            flops=6 * rows * full_width, bytes_accessed=4 * rows * full_width, transcendentals=rows
        ),
        name="norm_rows",
    )(*far_first(slices), routes, route_weights, *gains, *after)


def hidden_kernel(pieces, after, tile, first, steps, *refs):
    piece_refs = refs[:pieces]
    weight_refs = refs[pieces : pieces + 2]
    out_ref, rows_scr, route_scr, weight_scr, sems, weight_sems = refs[pieces + 2 + after :]
    full_width = weight_scr.shape[2]

    def fetch(i, act):
        columns = pl.ds((first + i) * tile, tile)
        for j in range(2):
            act(
                pltpu.make_async_copy(
                    weight_refs[j].at[0, :, columns],
                    weight_scr.at[j, i % SLOTS],
                    weight_sems.at[j, i % SLOTS],
                )
            )

    def start(copy):
        copy.start()

    def wait(copy):
        copy.wait()

    fetch(0, start)
    load_pieces(piece_refs, rows_scr, sems)
    for i in range(1, min(SLOTS - 1, steps)):
        fetch(i, start)
    small = rows_scr[:, full_width:].astype(jnp.float32)
    lane = lax.broadcasted_iota(jnp.int32, small.shape, 1)
    place = lax.axis_index("expert") * 3
    mine = (lane >= place) & (lane < place + 3)
    weight = jnp.sum(jnp.where(mine, small, 0.0), axis=1, keepdims=True)
    route_scr[...] = jnp.broadcast_to(0.5 * weight, route_scr.shape)
    for i in range(steps):
        fetch(i, wait)
        if i + SLOTS - 1 < steps:
            fetch(i + SLOTS - 1, start)
        rows = rows_scr[:, :full_width]
        gate = jnp.dot(rows, weight_scr[0, i % SLOTS], preferred_element_type=jnp.float32)
        up = jnp.dot(rows, weight_scr[1, i % SLOTS], preferred_element_type=jnp.float32)
        hidden = gate * (1.0 + jnp.tanh(0.5 * gate)) * up * route_scr[:, :1]
        out_ref[:, i * tile : (i + 1) * tile] = hidden.astype(jnp.bfloat16)


def tile_of(weight):
    hidden = weight.shape[2]
    return next(t for t in (256, 128, hidden) if hidden % t == 0)


def hidden_rows(pieces, w_gate, w_up, after, first, steps, tile):
    rows = sum(p.shape[0] for p in pieces)
    full_width = w_gate.shape[1]
    hidden = steps * tile
    return pl.pallas_call(
        functools.partial(hidden_kernel, len(pieces), len(after), tile, first, steps),
        out_shape=jax.ShapeDtypeStruct((rows, hidden), jnp.bfloat16),
        in_specs=[anywhere()] * (len(pieces) + 2 + len(after)),
        out_specs=whole(),
        scratch_shapes=[
            pltpu.VMEM((rows, full_width + LANES), jnp.bfloat16),
            pltpu.VMEM((rows, LANES), jnp.float32),
            pltpu.VMEM((2, SLOTS, full_width, tile), jnp.bfloat16),
            pltpu.SemaphoreType.DMA((len(pieces),)),
            pltpu.SemaphoreType.DMA((2, SLOTS)),
        ],
        compiler_params=params((18 + rows // 64) * MIB),
        cost_estimate=pl.CostEstimate(
            flops=4 * rows * full_width * hidden,
            bytes_accessed=4 * full_width * hidden + 2 * rows * (full_width + hidden),
            transcendentals=rows * hidden,
        ),
        name="hidden_rows",
    )(*pieces, w_gate, w_up, *after)


def down_kernel(start, count, *refs):
    hidden_refs, down_ref, out_ref = refs[:count], refs[count], refs[-1]
    full_width = out_ref.shape[1]
    tile = 512 if full_width % 512 == 0 else full_width

    @pl.loop(0, full_width // tile, unroll=True)
    def _(i):
        columns = pl.ds(pl.multiple_of(i * tile, tile), tile)
        out = None
        depth = 0
        for hidden_ref in hidden_refs:
            rows = hidden_ref[start : start + out_ref.shape[0], :]
            block = down_ref[0, depth : depth + rows.shape[1], columns]
            term = jnp.dot(rows, block, preferred_element_type=jnp.float32)
            out = term if out is None else out + term
            depth += rows.shape[1]
        out_ref[:, columns] = out.astype(jnp.bfloat16)


def down_rows(hidden, w_down, start, rows, after):
    depth, full_width = w_down.shape[1:]
    hidden = [pltpu.with_memory_space_constraint(part, pltpu.VMEM) for part in hidden]
    return pl.pallas_call(
        functools.partial(down_kernel, start, len(hidden)),
        out_shape=jax.ShapeDtypeStruct((rows, full_width), jnp.bfloat16),
        in_specs=[whole()] * (len(hidden) + 1) + [anywhere()] * len(after),
        out_specs=whole(),
        compiler_params=params((4 + rows // 64) * MIB),
        cost_estimate=pl.CostEstimate(
            flops=2 * rows * depth * full_width,
            bytes_accessed=2 * rows * (depth + full_width),
            transcendentals=0,
        ),
        name="down_rows",
    )(*hidden, w_down, *after)


def many_rows(pieces, w_gate, w_up, w_down):
    outs = []
    tile = tile_of(w_gate)
    steps = w_gate.shape[2] // tile
    while pieces:
        count = 1
        while count < len(pieces) and sum(p.shape[0] for p in pieces[: count + 1]) <= LARGEST:
            count += 1
        hidden = hidden_rows(pieces[:count], w_gate, w_up, [], 0, steps, tile)
        outs.append(down_rows([hidden], w_down, 0, hidden.shape[0], []))
        pieces = pieces[count:]
    return jnp.concatenate(outs)


def final_kernel(parts, *refs):
    part_refs = refs[: parts + 2]
    out_ref, rows_scr, gains_scr, sems = refs[-4:]
    targets = [rows_scr.at[i] for i in range(parts + 1)] + [gains_scr]
    copies = [
        pltpu.make_async_copy(part_refs[i], targets[i], sems.at[i]) for i in range(parts + 2)
    ]
    for copy in copies:
        copy.start()
    for copy in copies:
        copy.wait()
    mixed = rows_scr[0].astype(jnp.float32)
    for i in range(1, parts):
        mixed = mixed + rows_scr[i].astype(jnp.float32)
    residual = rows_scr[parts].astype(jnp.float32) + mixed
    residual = residual.astype(jnp.bfloat16).astype(jnp.float32)
    total = jnp.sum(residual * residual, axis=1, keepdims=True)
    scale = lax.rsqrt(total / residual.shape[1] + epsilon)
    out_ref[...] = (residual * scale * gains_scr[1:2, :]).astype(jnp.bfloat16)


def final_rows(parts, raw, gains, after):
    rows, full_width = raw.shape
    return pl.pallas_call(
        functools.partial(final_kernel, len(parts)),
        out_shape=jax.ShapeDtypeStruct((rows, full_width), jnp.bfloat16),
        in_specs=[anywhere()] * (len(parts) + 2 + len(after)),
        out_specs=whole(),
        scratch_shapes=[
            pltpu.VMEM((len(parts) + 1, rows, full_width), jnp.bfloat16),
            pltpu.VMEM(gains.shape, jnp.float32),
            pltpu.SemaphoreType.DMA((len(parts) + 2,)),
        ],
        compiler_params=params(6 * MIB),
        cost_estimate=pl.CostEstimate(
            flops=8 * rows * full_width, bytes_accessed=12 * rows * full_width, transcendentals=rows
        ),
        name="final_rows",
    )(*parts, raw, gains, *after)


def head_kernel(pieces, tile, sub, earlier, *refs):
    piece_refs = refs[:pieces]
    head_ref, target_ref = refs[pieces : pieces + 2]
    earlier_refs = refs[pieces + 2 : pieces + 2 + earlier]
    out_refs, rows_scr, head_scr, sems, head_sems = refs[pieces + 2 + earlier :]
    for earlier_ref in earlier_refs:
        out_refs[: earlier_ref.shape[0], :] = earlier_ref[...]
    out_ref = out_refs.at[pl.ds(out_refs.shape[0] - 8, 8), :]
    vocab_part = head_ref.shape[0]
    steps = vocab_part // tile
    my_expert, my_tensor = lax.axis_index("expert"), lax.axis_index("tensor")
    n_tensor = lax.axis_size("tensor")

    def fetch(i):
        return pltpu.make_async_copy(
            head_ref.at[pl.ds(pl.multiple_of(i * tile, tile), tile), :],
            head_scr.at[i],
            head_sems.at[i],
        )

    copies = []
    for piece_ref in piece_refs:
        for start in range(0, piece_ref.shape[0], sub):
            far_expert, far_tensor = divmod(len(copies), n_tensor)
            block = (my_expert ^ far_expert) * n_tensor + (my_tensor ^ far_tensor)
            copies.append(
                pltpu.make_async_copy(
                    piece_ref.at[pl.ds(start, sub), :],
                    rows_scr.at[pl.ds(pl.multiple_of(block * sub, sub), sub), :],
                    sems.at[len(copies)],
                )
            )
    ahead = min(2, steps)
    fetch(0).start()
    for copy in copies:
        copy.start()
    for i in range(1, ahead):
        fetch(i).start()
    for copy in copies:
        copy.wait()
    lane = lax.broadcasted_iota(jnp.int32, out_ref.shape, 0)
    out_ref[...] = jnp.where(lane == 0, -jnp.inf, 0.0)
    targets = target_ref[...] - (my_expert * n_tensor + my_tensor) * vocab_part

    @pl.loop(0, steps)
    def _(i):
        fetch(i).wait()

        @pl.when(i + ahead < steps)
        def _():
            fetch(i + ahead).start()

        logits = lax.dot_general(
            head_scr[i],
            rows_scr[...],
            (((1,), (1,)), ((), ())),
            preferred_element_type=jnp.float32,
        )
        word = lax.broadcasted_iota(jnp.int32, logits.shape, 0) + i * tile
        old_top, old_total = out_ref[0:1, :], out_ref[1:2, :]
        top = jnp.maximum(old_top, jnp.max(logits, axis=0, keepdims=True))
        out_ref[0:1, :] = top
        out_ref[1:2, :] = old_total * jnp.exp(old_top - top) + jnp.sum(
            jnp.exp(logits - top), axis=0, keepdims=True
        )
        hit = word == targets
        out_ref[2:3, :] += jnp.sum(jnp.where(hit, logits, 0.0), axis=0, keepdims=True)


def head_terms(pieces, head_rows, targets, sub, earlier):
    rows = sum(p.shape[0] for p in pieces)
    vocab_part, full_width = head_rows.shape
    tile = next(t for t in (400, 200, 80, 8, vocab_part) if vocab_part % t == 0)
    return pl.pallas_call(
        functools.partial(head_kernel, len(pieces), tile, sub, len(earlier)),
        out_shape=jax.ShapeDtypeStruct((8 + sum(e.shape[0] for e in earlier), rows), jnp.float32),
        in_specs=[anywhere()] * (len(pieces) + 1) + [whole()] * (1 + len(earlier)),
        out_specs=whole(),
        scratch_shapes=[
            pltpu.VMEM((rows, full_width), jnp.bfloat16),
            pltpu.VMEM((vocab_part // tile, tile, full_width), jnp.bfloat16),
            pltpu.SemaphoreType.DMA((rows // sub,)),
            pltpu.SemaphoreType.DMA((vocab_part // tile,)),
        ],
        compiler_params=params((22 + rows // 64) * MIB),
        cost_estimate=pl.CostEstimate(
            flops=2 * rows * full_width * vocab_part,
            bytes_accessed=2 * full_width * (vocab_part + rows),
            transcendentals=rows * vocab_part,
        ),
        name="head_terms",
    )(*pieces, head_rows, targets, *earlier)


def join_kernel(last, mine_ref, got_ref, out_ref):
    for line in range(0, mine_ref.shape[0], 8):
        top_one, top_two = mine_ref[line : line + 1, :], got_ref[line : line + 1, :]
        top = jnp.maximum(top_one, top_two)
        total = mine_ref[line + 1 : line + 2, :] * jnp.exp(top_one - top)
        total = total + got_ref[line + 1 : line + 2, :] * jnp.exp(top_two - top)
        target = mine_ref[line + 2 : line + 3, :] + got_ref[line + 2 : line + 3, :]
        if last:
            out_ref[line : line + 1, :] = top + jnp.log(total) - target
        else:
            out_ref[line : line + 1, :] = top
            out_ref[line + 1 : line + 2, :] = total
            out_ref[line + 2 : line + 3, :] = target


def join_all(terms):
    hops = []
    for axis in ("tensor", "expert"):
        distance = 1
        while distance < lax.axis_size(axis):
            hops.append((axis, distance))
            distance *= 2
    for i, (axis, distance) in enumerate(hops):
        (terms,) = small_call(
            functools.partial(join_kernel, i == len(hops) - 1),
            "join",
            [terms, swap(terms, axis, distance)],
            [],
            [(terms.shape, jnp.float32)],
            [],
            2 * MIB,
        )
    return terms


def pack_kernel(kept_ref, got_ref, one_ref, two_ref, home_ref, side_ref):
    rows = home_ref.shape[0]
    half = rows // 2

    def both(d, first):
        block = slice(d * rows + first, d * rows + first + half)
        return kept_ref[block, :].astype(jnp.float32) + got_ref[block, :].astype(jnp.float32)

    one_ref[:half, :] = both(1, 0).astype(jnp.bfloat16)
    one_ref[half:, :] = both(3, 0).astype(jnp.bfloat16)
    two_ref[:half, :] = both(2, half).astype(jnp.bfloat16)
    two_ref[half:, :] = both(3, half).astype(jnp.bfloat16)
    home_ref[:half, :] = both(0, 0)
    home_ref[half:, :] = both(0, half)
    side_ref[0] = both(1, half)
    side_ref[1] = both(2, 0)


def pass_kernel(side_ref, one_ref, two_ref, *refs):
    pass_one_ref, pass_two_ref = refs[-2:]
    half = pass_one_ref.shape[0]
    pass_one_ref[...] = (side_ref[0] + two_ref[half:, :].astype(jnp.float32)).astype(jnp.bfloat16)
    pass_two_ref[...] = (side_ref[1] + one_ref[half:, :].astype(jnp.float32)).astype(jnp.bfloat16)


def total_kernel(count, column, *refs):
    home_ref, one_ref, two_ref, last_one_ref, last_two_ref = refs[:5]
    column_refs = refs[5 : 5 + column]
    outs = refs[5 + column : 5 + column + count]
    work, sems = refs[-2:]
    half = last_one_ref.shape[0]
    sub = outs[0].shape[0]
    me = lax.axis_index("tensor")
    copies = [
        pltpu.make_async_copy(
            column_refs[i], refs[-3].at[pl.ds(i * sub, sub), :], sems.at[i]
        )
        for i in range(column)
    ]
    for copy in copies:
        copy.start()
    upper = one_ref[:half, :].astype(jnp.float32) + last_two_ref[...].astype(jnp.float32)
    lower = two_ref[:half, :].astype(jnp.float32) + last_one_ref[...].astype(jnp.float32)
    work[:half, :] = home_ref[:half, :] + upper
    work[half:, :] = home_ref[half:, :] + lower
    for d in range(count):
        block = pl.ds(pl.multiple_of((me ^ d) * sub, sub), sub)
        outs[d][...] = work[block, :].astype(jnp.bfloat16)
    for copy in copies:
        copy.wait()


def totals_of(home, ones, lasts, count, sub, column):
    rows, full_width = home.shape
    piece = jax.ShapeDtypeStruct((sub, full_width), jnp.bfloat16)
    stacked = jax.ShapeDtypeStruct((sub * len(column), full_width), jnp.bfloat16)
    outs = pl.pallas_call(
        functools.partial(total_kernel, count, len(column)),
        out_shape=(piece,) * count + ((stacked,) if column else ()),
        in_specs=[whole()] * 5 + [anywhere()] * len(column),
        out_specs=(whole(),) * count + ((anywhere(),) if column else ()),
        scratch_shapes=[
            pltpu.VMEM((rows, full_width), jnp.float32),
            pltpu.SemaphoreType.DMA((max(1, len(column)),)),
        ],
        compiler_params=params(8 * MIB),
        cost_estimate=pl.CostEstimate(
            flops=4 * home.size, bytes_accessed=20 * home.size, transcendentals=0
        ),
        name="total",
    )(home, *ones, *lasts, *column)
    return list(outs[:count]), list(outs[count:])


def small_call(kernel, name, inputs, after, outs, scratch, limit):
    size = sum(x.size * x.dtype.itemsize for x in inputs)
    return pl.pallas_call(
        kernel,
        out_shape=tuple(jax.ShapeDtypeStruct(*out) for out in outs),
        in_specs=[whole()] * len(inputs) + [anywhere()] * len(after),
        out_specs=(whole(),) * len(outs),
        scratch_shapes=scratch,
        compiler_params=params(limit),
        cost_estimate=pl.CostEstimate(flops=size, bytes_accessed=2 * size, transcendentals=0),
        name=name,
    )(*inputs, *after)


def sum_plane(kept, got, rows, column):
    f32, b16 = jnp.float32, jnp.bfloat16
    n_tensor = lax.axis_size("tensor")
    count, full_width = kept.shape[0] // rows, kept.shape[1]
    half = rows // 2
    sub = rows // n_tensor
    if count == 4 and half % 16 == 0 and sub % 16 == 0:
        one, two, home, side = small_call(
            pack_kernel,
            "pack",
            [kept, got],
            [],
            [((rows, full_width), b16)] * 2
            + [((rows, full_width), f32), ((2, half, full_width), f32)],
            [],
            10 * MIB,
        )
        from_one, from_two = swap(one, "expert", 1), swap(two, "expert", 2)
        pass_one, pass_two = small_call(
            pass_kernel,
            "pass_on",
            [side, from_one, from_two],
            column[:0:-1],
            [((half, full_width), b16)] * 2,
            [],
            6 * MIB,
        )
        last_one, last_two = swap(pass_one, "expert", 1), swap(pass_two, "expert", 2)
        pieces, stacked = totals_of(
            home, [from_one, from_two], [last_one, last_two], n_tensor, sub, column
        )
        return pieces, [one, two], [pass_one, pass_two], stacked
    both = (kept.astype(f32) + got.astype(f32)).reshape(count, rows, full_width)
    total = both[0]
    for d in range(1, count):
        total = total + swap(both[d].astype(b16), "expert", d).astype(f32)
    total = total.astype(b16).reshape(n_tensor, sub, full_width)
    me = lax.axis_index("tensor")
    pieces = [lax.dynamic_index_in_dim(total, me ^ d, 0, False) for d in range(n_tensor)]
    return pieces, [], [], []


def on_device(
    tokens, routes, route_weights, norm_gain, final_gain, w_gate, w_up, w_down, head_weight, targets
):
    tok_rows, width = tokens.shape
    n_expert = lax.axis_size("expert")
    n_tensor = lax.axis_size("tensor")
    my_expert = lax.axis_index("expert")
    my_tensor = lax.axis_index("tensor")
    full_width = width * n_tensor
    own = tok_rows // n_tensor
    splits = 2 if own % 32 == 0 else 1
    sub = own // splits
    rows = sub * n_tensor

    blocks = begin(tokens, norm_gain, final_gain, n_tensor, splits)
    slices = [gather_near(block, "tensor") for block in blocks]
    gains = None
    planes, raws = [], []
    after = []
    for h in range(splits):
        normed, raw, *made = norm_rows(
            slices[h], [gains], routes, route_weights, splits, h, rows, after
        )
        if made:
            gains = made[0]
        plane, _ = gather_plane(normed, "expert", [])
        planes.append(plane)
        raws.append(raw)
        after = plane[3:]

    w_gate = pltpu.with_memory_space_constraint(w_gate, pltpu.HBM)
    w_up = pltpu.with_memory_space_constraint(w_up, pltpu.HBM)
    head_rows = pltpu.with_memory_space_constraint(head_weight.T, pltpu.HBM)
    target_rows = targets.reshape(n_expert, n_tensor, splits, sub)
    terms = []
    before = {}
    for h in range(splits):
        if 2 * n_expert * rows <= LARGEST:
            nearer = stack_rows(planes[h][:3], [] if before else sum((p[:0:-1] for p in slices[1:2]), []))
            away = [swap(nearer, "seq", 1)]
            if planes[h][3:]:
                away.append(swap(stack_rows(planes[h][3:], before.get("kept", [])), "seq", 1))
            half = n_expert * rows
            everything = planes[h] + away
            tile = tile_of(w_gate)
            count = w_gate.shape[2] // tile
            cuts = [0, (count + 1) // 2, count - 1, count] if h else [0, count]
            ties = [before.get(key, []) for key in ("packed", "passed", "totals")]
            hidden = [
                hidden_rows(
                    everything, w_gate, w_up, ties[i], cuts[i], cuts[i + 1] - cuts[i], tile
                )
                for i in range(len(cuts) - 1)
            ]
            later = planes[h + 1][1:3] if h + 1 < splits else []
            other = down_rows(hidden, w_down, half, half, later + before.get("sums", [])[::-1])
            kept = down_rows(hidden, w_down, 0, half, before.get("final", []))
        else:
            away = [swap(p, "seq", 1) for p in planes[h]]
            kept, other = many_rows(planes[h], w_gate, w_up, w_down), many_rows(
                away, w_gate, w_up, w_down
            )
        got = swap(other, "seq", 1)
        totals, packed, passed, stacked = sum_plane(kept, got, rows, before.get("column", []))
        sums = swap_each(totals[1:], "tensor")
        cut = []
        if before:
            plane, cut = gather_plane(stacked[0], "expert", [])
            wanted = target_rows[:, :, h - 1].reshape(1, -1)
            terms = [head_terms(plane, head_rows, wanted, sub, terms)]
        final = final_rows(far_first(totals[:1] + sums), raws[h], gains, [])
        column = gather_near(final, "tensor")
        before = {
            "kept": [kept],
            "packed": packed,
            "passed": passed,
            "totals": totals,
            "sums": sums,
            "final": [final],
            "column": column,
        }
    column = stack_line(column, cut)
    plane, _ = gather_plane(column, "expert", terms)
    wanted = target_rows[:, :, splits - 1].reshape(1, -1)
    terms = [head_terms(plane, head_rows, wanted, sub, terms)]
    losses = join_all(terms[0])[::8]
    start = (my_expert * n_tensor + my_tensor) * sub
    return lax.dynamic_slice_in_dim(losses, start, sub, 1).reshape(own)


def solution(mesh):
    return jax.shard_map(
        on_device,
        mesh=mesh,
        in_specs=(
            P(("seq", "expert"), "tensor"),
            P(("seq", "expert"), None),
            P(("seq", "expert"), None),
            P("tensor"),
            P("tensor"),
            P("expert", None, ("seq", "tensor")),
            P("expert", None, ("seq", "tensor")),
            P("expert", ("seq", "tensor"), None),
            P(None, ("expert", "tensor")),
            P("seq"),
        ),
        out_specs=P(("seq", "expert", "tensor")),
        check_vma=False,
    )
```

```python
import functools

import jax
import jax.numpy as jnp
from jax import lax
from jax.experimental import pallas as pl
from jax.experimental.pallas import tpu as pltpu
from jax.sharding import PartitionSpec as P

epsilon = 1e-05
LANES = 128
SLOTS = 3
LARGEST = 512
MIB = 1024 * 1024
VMEM_BYTES = 56 * 1024 * 1024


def params(limit=VMEM_BYTES):
    return pltpu.CompilerParams(vmem_limit_bytes=limit)


def whole():
    return pl.BlockSpec(memory_space=pltpu.VMEM)


def anywhere():
    return pl.BlockSpec(memory_space=pl.ANY)


def swap(x, axis, distance):
    size = lax.axis_size(axis)
    return lax.ppermute(x, axis, [(i, i ^ distance) for i in range(size)])


def gather_near(x, axis):
    return [x] + swap_each([x] * (lax.axis_size(axis) - 1), axis)


def swap_each(pieces, axis):
    return [swap(piece, axis, d + 1) for d, piece in enumerate(pieces)]


def far_first(pieces):
    return pieces[:1] + pieces[1:][::-1]


def gather_plane(x, axis, after):
    if lax.axis_size(axis) != 4:
        return gather_near(x, axis), []
    half = x.shape[0] // 2
    one, two = swap(x, axis, 1), swap(x, axis, 2)
    upper, lower = move_rows([two, one], [(0, 0, half, 0, 0), (1, half, half, 1, 0)], after)
    return [x, one, two, swap(upper, axis, 1), swap(lower, axis, 2)], [upper, lower]


def move_kernel(sources, targets, moves, *refs):
    out_refs, sems = refs[-targets - 1 : -1], refs[-1]
    copies = []
    for i, (source, start, count, target, place) in enumerate(moves):
        copies.append(
            pltpu.make_async_copy(
                refs[source].at[pl.ds(start, count), :],
                out_refs[target].at[pl.ds(place, count), :],
                sems.at[i],
            )
        )
    for copy in copies:
        copy.start()
    for copy in copies:
        copy.wait()


def move_rows(arrays, moves, after):
    targets = 1 + max(m[3] for m in moves)
    sizes = [sum(m[2] for m in moves if m[3] == t) for t in range(targets)]
    size = sum(sizes) * arrays[0].shape[1]
    return pl.pallas_call(
        functools.partial(move_kernel, len(arrays), targets, moves),
        out_shape=tuple(
            jax.ShapeDtypeStruct((rows, arrays[0].shape[1]), arrays[0].dtype) for rows in sizes
        ),
        in_specs=[anywhere()] * (len(arrays) + len(after)),
        out_specs=(anywhere(),) * targets,
        scratch_shapes=[pltpu.SemaphoreType.DMA((len(moves),))],
        compiler_params=params(MIB),
        cost_estimate=pl.CostEstimate(flops=0, bytes_accessed=4 * size, transcendentals=0),
        name="move_rows",
    )(*arrays, *after)


def stack_rows(arrays, after):
    moves = []
    place = 0
    for i, x in enumerate(arrays):
        moves.append((i, 0, x.shape[0], 0, place))
        place += x.shape[0]
    return move_rows(arrays, moves, after)[0]


def stack_line(pieces, after):
    count, size = len(pieces), pieces[0].shape[0]
    moves = [(i, 0, size, 0, (count - i if i else 0) * size) for i in range(count)]
    return move_rows(far_first(pieces), moves, after)[0]


def load_pieces(piece_refs, scratch, sems):
    copies = []
    start = 0
    for i in range(len(piece_refs)):
        count = piece_refs[i].shape[0]
        copies.append(
            pltpu.make_async_copy(piece_refs[i], scratch.at[pl.ds(start, count), :], sems.at[i])
        )
        start += count
    for copy in copies:
        copy.start()
    for copy in copies:
        copy.wait()


def begin_kernel(count, splits, *refs):
    block_refs, (tokens_scr, gains_scr, sems) = refs[3 : 3 + splits], refs[3 + splits :]
    targets = [tokens_scr, gains_scr.at[0], gains_scr.at[1]]
    copies = [pltpu.make_async_copy(refs[i], targets[i], sems.at[i]) for i in range(3)]
    for copy in copies:
        copy.start()
    for copy in copies:
        copy.wait()
    own_rows = tokens_scr.shape[0] // (count * splits)
    for i in range(count):
        for h in range(splits):
            start = (i * splits + h) * own_rows
            block_refs[h][i * own_rows : (i + 1) * own_rows, :] = tokens_scr[
                start : start + own_rows, :
            ]
    lines = []
    for i in range(2):
        gain = gains_scr[i]
        high = gain.astype(jnp.bfloat16).astype(jnp.float32)
        middle = (gain - high).astype(jnp.bfloat16).astype(jnp.float32)
        lines += [high, middle, gain - high - middle]
    lines.append(jnp.zeros((2, lines[0].shape[1]), jnp.float32))
    block_refs[0][count * own_rows :, :] = jnp.concatenate(lines).astype(jnp.bfloat16)


def begin(tokens, norm_gain, final_gain, count, splits):
    rows, width = tokens.shape
    sizes = [rows // splits + (0 if h else 8) for h in range(splits)]
    return pl.pallas_call(
        functools.partial(begin_kernel, count, splits),
        out_shape=tuple(jax.ShapeDtypeStruct((size, width), jnp.bfloat16) for size in sizes),
        in_specs=[anywhere()] * 3,
        out_specs=(whole(),) * splits,
        scratch_shapes=[
            pltpu.VMEM((rows, width), jnp.bfloat16),
            pltpu.VMEM((2, 1, width), jnp.float32),
            pltpu.SemaphoreType.DMA((3,)),
        ],
        compiler_params=params(4 * MIB),
        name="begin",
    )(
        pltpu.with_memory_space_constraint(tokens, pltpu.HBM),
        pltpu.with_memory_space_constraint(norm_gain.reshape(1, width), pltpu.HBM),
        pltpu.with_memory_space_constraint(final_gain.reshape(1, width), pltpu.HBM),
    )


def norm_kernel(splits, part, count, after, *refs):
    slices = refs[:1] + refs[1:count][::-1]
    routes_ref, weights_ref = refs[count : count + 2]
    rest = list(refs[count + 2 :])
    gains_in = rest.pop(0) if part else None
    rest = rest[after:]
    rows_ref, raw_ref = rest[:2]
    gains_ref = gains_in if part else rest[2]
    rows = rows_ref.shape[0]
    width = slices[0].shape[1]
    full_width = width * count
    own_rows = rows // count
    me = lax.axis_index("tensor")
    total = jnp.zeros((rows, 1), jnp.float32)
    for piece in slices:
        value = piece[:rows, :].astype(jnp.float32)
        total = total + jnp.sum(value * value, axis=1, keepdims=True)
    scale = lax.rsqrt(total / full_width + epsilon)
    start = pl.multiple_of(me * own_rows, own_rows)
    for d in range(count):
        columns = pl.ds(pl.multiple_of((me ^ d) * width, width), width)
        if not part:
            tail = slices[d][rows:, :].astype(jnp.float32)
            gains_ref[0:1, columns] = tail[0:1] + tail[1:2] + tail[2:3]
            gains_ref[1:2, columns] = tail[3:4] + tail[4:5] + tail[5:6]
        value = slices[d][:rows, :].astype(jnp.float32)
        rows_ref[:, columns] = (value * scale * gains_ref[0:1, columns]).astype(jnp.bfloat16)
        raw_ref[:, columns] = slices[d][pl.ds(start, own_rows), :]
    lane = lax.broadcasted_iota(jnp.int32, (own_rows, LANES), 1)
    expert = lane // 3
    kind = lane - expert * 3
    for i in range(count):
        block = pl.ds((i * splits + part) * own_rows, own_rows)
        weight = jnp.zeros((own_rows, LANES), jnp.float32)
        for j in range(routes_ref.shape[1]):
            named = routes_ref[block, j : j + 1] == expert
            weight = weight + jnp.where(named, weights_ref[block, j : j + 1], 0.0)
        high = weight.astype(jnp.bfloat16).astype(jnp.float32)
        middle = (weight - high).astype(jnp.bfloat16).astype(jnp.float32)
        low = weight - high - middle
        value = jnp.where(kind == 0, high, jnp.where(kind == 1, middle, low))
        rows_ref[i * own_rows : (i + 1) * own_rows, full_width:] = value.astype(jnp.bfloat16)


def norm_rows(slices, gains, routes, route_weights, splits, part, rows, after):
    width = slices[0].shape[1]
    count = len(slices)
    full_width = width * count
    gains = gains if part else []
    made = [] if part else [jax.ShapeDtypeStruct((8, full_width), jnp.float32)]
    return pl.pallas_call(
        functools.partial(norm_kernel, splits, part, count, len(after)),
        out_shape=(
            jax.ShapeDtypeStruct((rows, full_width + LANES), jnp.bfloat16),
            jax.ShapeDtypeStruct((rows // count, full_width), jnp.bfloat16),
            *made,
        ),
        in_specs=[whole()] * (count + 2 + len(gains)) + [anywhere()] * len(after),
        out_specs=(whole(),) * (2 + len(made)),
        compiler_params=params(6 * MIB),
        cost_estimate=pl.CostEstimate(
            flops=6 * rows * full_width, bytes_accessed=4 * rows * full_width, transcendentals=rows
        ),
        name="norm_rows",
    )(*far_first(slices), routes, route_weights, *gains, *after)


def hidden_kernel(pieces, after, tile, first, steps, *refs):
    piece_refs = refs[:pieces]
    weight_refs = refs[pieces : pieces + 2]
    out_ref, rows_scr, route_scr, weight_scr, sems, weight_sems = refs[pieces + 2 + after :]
    full_width = weight_scr.shape[2]

    def fetch(i, act):
        columns = pl.ds((first + i) * tile, tile)
        for j in range(2):
            act(
                pltpu.make_async_copy(
                    weight_refs[j].at[0, :, columns],
                    weight_scr.at[j, i % SLOTS],
                    weight_sems.at[j, i % SLOTS],
                )
            )

    def start(copy):
        copy.start()

    def wait(copy):
        copy.wait()

    fetch(0, start)
    load_pieces(piece_refs, rows_scr, sems)
    for i in range(1, min(SLOTS - 1, steps)):
        fetch(i, start)
    small = rows_scr[:, full_width:].astype(jnp.float32)
    lane = lax.broadcasted_iota(jnp.int32, small.shape, 1)
    place = lax.axis_index("expert") * 3
    mine = (lane >= place) & (lane < place + 3)
    weight = jnp.sum(jnp.where(mine, small, 0.0), axis=1, keepdims=True)
    route_scr[...] = jnp.broadcast_to(0.5 * weight, route_scr.shape)
    for i in range(steps):
        fetch(i, wait)
        if i + SLOTS - 1 < steps:
            fetch(i + SLOTS - 1, start)
        rows = rows_scr[:, :full_width]
        gate = jnp.dot(rows, weight_scr[0, i % SLOTS], preferred_element_type=jnp.float32)
        up = jnp.dot(rows, weight_scr[1, i % SLOTS], preferred_element_type=jnp.float32)
        hidden = gate * (1.0 + jnp.tanh(0.5 * gate)) * up * route_scr[:, :1]
        out_ref[:, i * tile : (i + 1) * tile] = hidden.astype(jnp.bfloat16)


def tile_of(weight):
    hidden = weight.shape[2]
    return next(t for t in (256, 128, hidden) if hidden % t == 0)


def hidden_rows(pieces, w_gate, w_up, after, first, steps, tile):
    rows = sum(p.shape[0] for p in pieces)
    full_width = w_gate.shape[1]
    hidden = steps * tile
    return pl.pallas_call(
        functools.partial(hidden_kernel, len(pieces), len(after), tile, first, steps),
        out_shape=jax.ShapeDtypeStruct((rows, hidden), jnp.bfloat16),
        in_specs=[anywhere()] * (len(pieces) + 2 + len(after)),
        out_specs=whole(),
        scratch_shapes=[
            pltpu.VMEM((rows, full_width + LANES), jnp.bfloat16),
            pltpu.VMEM((rows, LANES), jnp.float32),
            pltpu.VMEM((2, SLOTS, full_width, tile), jnp.bfloat16),
            pltpu.SemaphoreType.DMA((len(pieces),)),
            pltpu.SemaphoreType.DMA((2, SLOTS)),
        ],
        compiler_params=params((18 + rows // 64) * MIB),
        cost_estimate=pl.CostEstimate(
            flops=4 * rows * full_width * hidden,
            bytes_accessed=4 * full_width * hidden + 2 * rows * (full_width + hidden),
            transcendentals=rows * hidden,
        ),
        name="hidden_rows",
    )(*pieces, w_gate, w_up, *after)


def down_kernel(start, count, *refs):
    hidden_refs, down_ref, out_ref = refs[:count], refs[count], refs[-1]
    full_width = out_ref.shape[1]
    tile = 512 if full_width % 512 == 0 else full_width

    @pl.loop(0, full_width // tile, unroll=True)
    def _(i):
        columns = pl.ds(pl.multiple_of(i * tile, tile), tile)
        out = None
        depth = 0
        for hidden_ref in hidden_refs:
            rows = hidden_ref[start : start + out_ref.shape[0], :]
            block = down_ref[0, depth : depth + rows.shape[1], columns]
            term = jnp.dot(rows, block, preferred_element_type=jnp.float32)
            out = term if out is None else out + term
            depth += rows.shape[1]
        out_ref[:, columns] = out.astype(jnp.bfloat16)


def down_rows(hidden, w_down, start, rows, after):
    depth, full_width = w_down.shape[1:]
    hidden = [pltpu.with_memory_space_constraint(part, pltpu.VMEM) for part in hidden]
    return pl.pallas_call(
        functools.partial(down_kernel, start, len(hidden)),
        out_shape=jax.ShapeDtypeStruct((rows, full_width), jnp.bfloat16),
        in_specs=[whole()] * (len(hidden) + 1) + [anywhere()] * len(after),
        out_specs=whole(),
        compiler_params=params((4 + rows // 64) * MIB),
        cost_estimate=pl.CostEstimate(
            flops=2 * rows * depth * full_width,
            bytes_accessed=2 * rows * (depth + full_width),
            transcendentals=0,
        ),
        name="down_rows",
    )(*hidden, w_down, *after)


def many_rows(pieces, w_gate, w_up, w_down):
    outs = []
    tile = tile_of(w_gate)
    steps = w_gate.shape[2] // tile
    while pieces:
        count = 1
        while count < len(pieces) and sum(p.shape[0] for p in pieces[: count + 1]) <= LARGEST:
            count += 1
        hidden = hidden_rows(pieces[:count], w_gate, w_up, [], 0, steps, tile)
        outs.append(down_rows([hidden], w_down, 0, hidden.shape[0], []))
        pieces = pieces[count:]
    return jnp.concatenate(outs)


def final_kernel(parts, *refs):
    part_refs = refs[: parts + 2]
    out_ref, rows_scr, gains_scr, sems = refs[-4:]
    targets = [rows_scr.at[i] for i in range(parts + 1)] + [gains_scr]
    copies = [
        pltpu.make_async_copy(part_refs[i], targets[i], sems.at[i]) for i in range(parts + 2)
    ]
    for copy in copies:
        copy.start()
    for copy in copies:
        copy.wait()
    mixed = rows_scr[0].astype(jnp.float32)
    for i in range(1, parts):
        mixed = mixed + rows_scr[i].astype(jnp.float32)
    residual = rows_scr[parts].astype(jnp.float32) + mixed
    residual = residual.astype(jnp.bfloat16).astype(jnp.float32)
    total = jnp.sum(residual * residual, axis=1, keepdims=True)
    scale = lax.rsqrt(total / residual.shape[1] + epsilon)
    out_ref[...] = (residual * scale * gains_scr[1:2, :]).astype(jnp.bfloat16)


def final_rows(parts, raw, gains, after):
    rows, full_width = raw.shape
    return pl.pallas_call(
        functools.partial(final_kernel, len(parts)),
        out_shape=jax.ShapeDtypeStruct((rows, full_width), jnp.bfloat16),
        in_specs=[anywhere()] * (len(parts) + 2 + len(after)),
        out_specs=whole(),
        scratch_shapes=[
            pltpu.VMEM((len(parts) + 1, rows, full_width), jnp.bfloat16),
            pltpu.VMEM(gains.shape, jnp.float32),
            pltpu.SemaphoreType.DMA((len(parts) + 2,)),
        ],
        compiler_params=params(6 * MIB),
        cost_estimate=pl.CostEstimate(
            flops=8 * rows * full_width, bytes_accessed=12 * rows * full_width, transcendentals=rows
        ),
        name="final_rows",
    )(*parts, raw, gains, *after)


def head_kernel(pieces, tile, sub, earlier, *refs):
    piece_refs = refs[:pieces]
    head_ref, target_ref = refs[pieces : pieces + 2]
    earlier_refs = refs[pieces + 2 : pieces + 2 + earlier]
    out_refs, rows_scr, head_scr, sems, head_sems = refs[pieces + 2 + earlier :]
    for earlier_ref in earlier_refs:
        out_refs[: earlier_ref.shape[0], :] = earlier_ref[...]
    out_ref = out_refs.at[pl.ds(out_refs.shape[0] - 8, 8), :]
    vocab_part = head_ref.shape[0]
    steps = vocab_part // tile
    my_expert, my_tensor = lax.axis_index("expert"), lax.axis_index("tensor")
    n_tensor = lax.axis_size("tensor")

    def fetch(i):
        return pltpu.make_async_copy(
            head_ref.at[pl.ds(pl.multiple_of(i * tile, tile), tile), :],
            head_scr.at[i],
            head_sems.at[i],
        )

    copies = []
    for piece_ref in piece_refs:
        for start in range(0, piece_ref.shape[0], sub):
            far_expert, far_tensor = divmod(len(copies), n_tensor)
            block = (my_expert ^ far_expert) * n_tensor + (my_tensor ^ far_tensor)
            copies.append(
                pltpu.make_async_copy(
                    piece_ref.at[pl.ds(start, sub), :],
                    rows_scr.at[pl.ds(pl.multiple_of(block * sub, sub), sub), :],
                    sems.at[len(copies)],
                )
            )
    ahead = min(2, steps)
    fetch(0).start()
    for copy in copies:
        copy.start()
    for i in range(1, ahead):
        fetch(i).start()
    for copy in copies:
        copy.wait()
    lane = lax.broadcasted_iota(jnp.int32, out_ref.shape, 0)
    out_ref[...] = jnp.where(lane == 0, -jnp.inf, 0.0)
    targets = target_ref[...] - (my_expert * n_tensor + my_tensor) * vocab_part

    @pl.loop(0, steps)
    def _(i):
        fetch(i).wait()

        @pl.when(i + ahead < steps)
        def _():
            fetch(i + ahead).start()

        logits = lax.dot_general(
            head_scr[i],
            rows_scr[...],
            (((1,), (1,)), ((), ())),
            preferred_element_type=jnp.float32,
        )
        word = lax.broadcasted_iota(jnp.int32, logits.shape, 0) + i * tile
        old_top, old_total = out_ref[0:1, :], out_ref[1:2, :]
        top = jnp.maximum(old_top, jnp.max(logits, axis=0, keepdims=True))
        out_ref[0:1, :] = top
        out_ref[1:2, :] = old_total * jnp.exp(old_top - top) + jnp.sum(
            jnp.exp(logits - top), axis=0, keepdims=True
        )
        hit = word == targets
        out_ref[2:3, :] += jnp.sum(jnp.where(hit, logits, 0.0), axis=0, keepdims=True)


def head_terms(pieces, head_rows, targets, sub, earlier):
    rows = sum(p.shape[0] for p in pieces)
    vocab_part, full_width = head_rows.shape
    tile = next(t for t in (400, 200, 80, 8, vocab_part) if vocab_part % t == 0)
    return pl.pallas_call(
        functools.partial(head_kernel, len(pieces), tile, sub, len(earlier)),
        out_shape=jax.ShapeDtypeStruct((8 + sum(e.shape[0] for e in earlier), rows), jnp.float32),
        in_specs=[anywhere()] * (len(pieces) + 1) + [whole()] * (1 + len(earlier)),
        out_specs=whole(),
        scratch_shapes=[
            pltpu.VMEM((rows, full_width), jnp.bfloat16),
            pltpu.VMEM((vocab_part // tile, tile, full_width), jnp.bfloat16),
            pltpu.SemaphoreType.DMA((rows // sub,)),
            pltpu.SemaphoreType.DMA((vocab_part // tile,)),
        ],
        compiler_params=params((22 + rows // 64) * MIB),
        cost_estimate=pl.CostEstimate(
            flops=2 * rows * full_width * vocab_part,
            bytes_accessed=2 * full_width * (vocab_part + rows),
            transcendentals=rows * vocab_part,
        ),
        name="head_terms",
    )(*pieces, head_rows, targets, *earlier)


def join_kernel(last, *refs):
    out_ref = refs[-1]
    for line in range(0, out_ref.shape[0], 8):

        def each(offset):
            return [ref[line + offset : line + offset + 1, :] for ref in refs[:-1]]

        tops = each(0)
        top = functools.reduce(jnp.maximum, tops)
        total = sum(t * jnp.exp(m - top) for m, t in zip(tops, each(1)))
        target = sum(each(2))
        if last:
            out_ref[line : line + 1, :] = top + jnp.log(total) - target
        else:
            out_ref[line : line + 1, :] = top
            out_ref[line + 1 : line + 2, :] = total
            out_ref[line + 2 : line + 3, :] = target


def join_all(terms):
    for axis in ("tensor", "expert"):
        (terms,) = small_call(
            functools.partial(join_kernel, axis == "expert"),
            "join",
            far_first(gather_near(terms, axis)),
            [],
            [(terms.shape, jnp.float32)],
            [],
            2 * MIB,
        )
    return terms


def pack_kernel(kept_ref, got_ref, one_ref, two_ref, home_ref, side_ref):
    rows = home_ref.shape[0]
    half = rows // 2

    def both(d, first):
        block = slice(d * rows + first, d * rows + first + half)
        return kept_ref[block, :].astype(jnp.float32) + got_ref[block, :].astype(jnp.float32)

    one_ref[:half, :] = both(1, 0).astype(jnp.bfloat16)
    one_ref[half:, :] = both(3, 0).astype(jnp.bfloat16)
    two_ref[:half, :] = both(2, half).astype(jnp.bfloat16)
    two_ref[half:, :] = both(3, half).astype(jnp.bfloat16)
    home_ref[:half, :] = both(0, 0)
    home_ref[half:, :] = both(0, half)
    side_ref[0] = both(1, half)
    side_ref[1] = both(2, 0)


def pass_kernel(side_ref, one_ref, two_ref, *refs):
    pass_one_ref, pass_two_ref = refs[-2:]
    half = pass_one_ref.shape[0]
    pass_one_ref[...] = (side_ref[0] + two_ref[half:, :].astype(jnp.float32)).astype(jnp.bfloat16)
    pass_two_ref[...] = (side_ref[1] + one_ref[half:, :].astype(jnp.float32)).astype(jnp.bfloat16)


def total_kernel(count, column, *refs):
    home_ref, one_ref, two_ref, last_one_ref, last_two_ref = refs[:5]
    column_refs = refs[5 : 5 + column]
    outs = refs[5 + column : 5 + column + count]
    work, sems = refs[-2:]
    half = last_one_ref.shape[0]
    sub = outs[0].shape[0]
    me = lax.axis_index("tensor")
    copies = [
        pltpu.make_async_copy(
            column_refs[i], refs[-3].at[pl.ds(i * sub, sub), :], sems.at[i]
        )
        for i in range(column)
    ]
    for copy in copies:
        copy.start()
    upper = one_ref[:half, :].astype(jnp.float32) + last_two_ref[...].astype(jnp.float32)
    lower = two_ref[:half, :].astype(jnp.float32) + last_one_ref[...].astype(jnp.float32)
    work[:half, :] = home_ref[:half, :] + upper
    work[half:, :] = home_ref[half:, :] + lower
    for d in range(count):
        block = pl.ds(pl.multiple_of((me ^ d) * sub, sub), sub)
        outs[d][...] = work[block, :].astype(jnp.bfloat16)
    for copy in copies:
        copy.wait()


def totals_of(home, ones, lasts, count, sub, column):
    rows, full_width = home.shape
    piece = jax.ShapeDtypeStruct((sub, full_width), jnp.bfloat16)
    stacked = jax.ShapeDtypeStruct((sub * len(column), full_width), jnp.bfloat16)
    outs = pl.pallas_call(
        functools.partial(total_kernel, count, len(column)),
        out_shape=(piece,) * count + ((stacked,) if column else ()),
        in_specs=[whole()] * 5 + [anywhere()] * len(column),
        out_specs=(whole(),) * count + ((anywhere(),) if column else ()),
        scratch_shapes=[
            pltpu.VMEM((rows, full_width), jnp.float32),
            pltpu.SemaphoreType.DMA((max(1, len(column)),)),
        ],
        compiler_params=params(8 * MIB),
        cost_estimate=pl.CostEstimate(
            flops=4 * home.size, bytes_accessed=20 * home.size, transcendentals=0
        ),
        name="total",
    )(home, *ones, *lasts, *column)
    return list(outs[:count]), list(outs[count:])


def small_call(kernel, name, inputs, after, outs, scratch, limit):
    size = sum(x.size * x.dtype.itemsize for x in inputs)
    return pl.pallas_call(
        kernel,
        out_shape=tuple(jax.ShapeDtypeStruct(*out) for out in outs),
        in_specs=[whole()] * len(inputs) + [anywhere()] * len(after),
        out_specs=(whole(),) * len(outs),
        scratch_shapes=scratch,
        compiler_params=params(limit),
        cost_estimate=pl.CostEstimate(flops=size, bytes_accessed=2 * size, transcendentals=0),
        name=name,
    )(*inputs, *after)


def sum_plane(kept, got, rows, column):
    f32, b16 = jnp.float32, jnp.bfloat16
    n_tensor = lax.axis_size("tensor")
    count, full_width = kept.shape[0] // rows, kept.shape[1]
    half = rows // 2
    sub = rows // n_tensor
    if count == 4 and half % 16 == 0 and sub % 16 == 0:
        one, two, home, side = small_call(
            pack_kernel,
            "pack",
            [kept, got],
            [],
            [((rows, full_width), b16)] * 2
            + [((rows, full_width), f32), ((2, half, full_width), f32)],
            [],
            10 * MIB,
        )
        from_one, from_two = swap(one, "expert", 1), swap(two, "expert", 2)
        pass_one, pass_two = small_call(
            pass_kernel,
            "pass_on",
            [side, from_one, from_two],
            column[:0:-1],
            [((half, full_width), b16)] * 2,
            [],
            6 * MIB,
        )
        last_one, last_two = swap(pass_one, "expert", 1), swap(pass_two, "expert", 2)
        pieces, stacked = totals_of(
            home, [from_one, from_two], [last_one, last_two], n_tensor, sub, column
        )
        return pieces, [one, two], [pass_one, pass_two], stacked
    both = (kept.astype(f32) + got.astype(f32)).reshape(count, rows, full_width)
    total = both[0]
    for d in range(1, count):
        total = total + swap(both[d].astype(b16), "expert", d).astype(f32)
    total = total.astype(b16).reshape(n_tensor, sub, full_width)
    me = lax.axis_index("tensor")
    pieces = [lax.dynamic_index_in_dim(total, me ^ d, 0, False) for d in range(n_tensor)]
    return pieces, [], [], []


def on_device(
    tokens, routes, route_weights, norm_gain, final_gain, w_gate, w_up, w_down, head_weight, targets
):
    tok_rows, width = tokens.shape
    n_expert = lax.axis_size("expert")
    n_tensor = lax.axis_size("tensor")
    my_expert = lax.axis_index("expert")
    my_tensor = lax.axis_index("tensor")
    full_width = width * n_tensor
    own = tok_rows // n_tensor
    splits = 2 if own % 32 == 0 else 1
    sub = own // splits
    rows = sub * n_tensor

    blocks = begin(tokens, norm_gain, final_gain, n_tensor, splits)
    slices = [gather_near(block, "tensor") for block in blocks]
    gains = None
    planes, raws = [], []
    after = []
    for h in range(splits):
        normed, raw, *made = norm_rows(
            slices[h], [gains], routes, route_weights, splits, h, rows, after
        )
        if made:
            gains = made[0]
        plane, _ = gather_plane(normed, "expert", [])
        planes.append(plane)
        raws.append(raw)
        after = plane[3:]

    w_gate = pltpu.with_memory_space_constraint(w_gate, pltpu.HBM)
    w_up = pltpu.with_memory_space_constraint(w_up, pltpu.HBM)
    head_rows = pltpu.with_memory_space_constraint(head_weight.T, pltpu.HBM)
    target_rows = targets.reshape(n_expert, n_tensor, splits, sub)
    terms = []
    before = {}
    for h in range(splits):
        if 2 * n_expert * rows <= LARGEST:
            nearer = stack_rows(planes[h][:3], [] if before else sum((p[:0:-1] for p in slices[1:2]), []))
            away = [swap(nearer, "seq", 1)]
            if planes[h][3:]:
                away.append(swap(stack_rows(planes[h][3:], before.get("kept", [])), "seq", 1))
            half = n_expert * rows
            everything = planes[h] + away
            tile = tile_of(w_gate)
            count = w_gate.shape[2] // tile
            cuts = [0, (count + 1) // 2, count - 1, count] if h else [0, count]
            ties = [before.get(key, []) for key in ("packed", "passed", "totals")]
            hidden = [
                hidden_rows(
                    everything, w_gate, w_up, ties[i], cuts[i], cuts[i + 1] - cuts[i], tile
                )
                for i in range(len(cuts) - 1)
            ]
            later = planes[h + 1][1:3] if h + 1 < splits else []
            other = down_rows(hidden, w_down, half, half, later + before.get("sums", [])[::-1])
            kept = down_rows(hidden, w_down, 0, half, before.get("final", []))
        else:
            away = [swap(p, "seq", 1) for p in planes[h]]
            kept, other = many_rows(planes[h], w_gate, w_up, w_down), many_rows(
                away, w_gate, w_up, w_down
            )
        got = swap(other, "seq", 1)
        totals, packed, passed, stacked = sum_plane(kept, got, rows, before.get("column", []))
        sums = swap_each(totals[1:], "tensor")
        cut = []
        if before:
            plane, cut = gather_plane(stacked[0], "expert", [])
            wanted = target_rows[:, :, h - 1].reshape(1, -1)
            terms = [head_terms(plane, head_rows, wanted, sub, terms)]
        final = final_rows(far_first(totals[:1] + sums), raws[h], gains, [])
        column = gather_near(final, "tensor")
        before = {
            "kept": [kept],
            "packed": packed,
            "passed": passed,
            "totals": totals,
            "sums": sums,
            "final": [final],
            "column": column,
        }
    column = stack_line(column, cut)
    plane, _ = gather_plane(column, "expert", terms)
    wanted = target_rows[:, :, splits - 1].reshape(1, -1)
    terms = [head_terms(plane, head_rows, wanted, sub, terms)]
    losses = join_all(terms[0])[::8]
    start = (my_expert * n_tensor + my_tensor) * sub
    return lax.dynamic_slice_in_dim(losses, start, sub, 1).reshape(own)


def solution(mesh):
    return jax.shard_map(
        on_device,
        mesh=mesh,
        in_specs=(
            P(("seq", "expert"), "tensor"),
            P(("seq", "expert"), None),
            P(("seq", "expert"), None),
            P("tensor"),
            P("tensor"),
            P("expert", None, ("seq", "tensor")),
            P("expert", None, ("seq", "tensor")),
            P("expert", ("seq", "tensor"), None),
            P(None, ("expert", "tensor")),
            P("seq"),
        ),
        out_specs=P(("seq", "expert", "tensor")),
        check_vma=False,
    )
```

```python
import functools

import jax
import jax.numpy as jnp
from jax import lax
from jax.experimental import pallas as pl
from jax.experimental.pallas import tpu as pltpu
from jax.sharding import PartitionSpec as P

epsilon = 1e-05
LANES = 128
SLOTS = 3
LARGEST = 512
MIB = 1024 * 1024
VMEM_BYTES = 56 * 1024 * 1024


def params(limit=VMEM_BYTES):
    return pltpu.CompilerParams(vmem_limit_bytes=limit)


def whole():
    return pl.BlockSpec(memory_space=pltpu.VMEM)


def anywhere():
    return pl.BlockSpec(memory_space=pl.ANY)


def swap(x, axis, distance):
    size = lax.axis_size(axis)
    return lax.ppermute(x, axis, [(i, i ^ distance) for i in range(size)])


def gather_near(x, axis):
    return [x] + swap_each([x] * (lax.axis_size(axis) - 1), axis)


def swap_each(pieces, axis):
    return [swap(piece, axis, d + 1) for d, piece in enumerate(pieces)]


def far_first(pieces):
    return pieces[:1] + pieces[1:][::-1]


def gather_plane(x, axis, after):
    if lax.axis_size(axis) != 4:
        return gather_near(x, axis), []
    half = x.shape[0] // 2
    one, two = swap(x, axis, 1), swap(x, axis, 2)
    upper, lower = move_rows([two, one], [(0, 0, half, 0, 0), (1, half, half, 1, 0)], after)
    return [x, one, two, swap(upper, axis, 1), swap(lower, axis, 2)], [upper, lower]


def move_kernel(sources, targets, moves, *refs):
    out_refs, sems = refs[-targets - 1 : -1], refs[-1]
    copies = []
    for i, (source, start, count, target, place) in enumerate(moves):
        copies.append(
            pltpu.make_async_copy(
                refs[source].at[pl.ds(start, count), :],
                out_refs[target].at[pl.ds(place, count), :],
                sems.at[i],
            )
        )
    for copy in copies:
        copy.start()
    for copy in copies:
        copy.wait()


def move_rows(arrays, moves, after):
    targets = 1 + max(m[3] for m in moves)
    sizes = [sum(m[2] for m in moves if m[3] == t) for t in range(targets)]
    size = sum(sizes) * arrays[0].shape[1]
    return pl.pallas_call(
        functools.partial(move_kernel, len(arrays), targets, moves),
        out_shape=tuple(
            jax.ShapeDtypeStruct((rows, arrays[0].shape[1]), arrays[0].dtype) for rows in sizes
        ),
        in_specs=[anywhere()] * (len(arrays) + len(after)),
        out_specs=(anywhere(),) * targets,
        scratch_shapes=[pltpu.SemaphoreType.DMA((len(moves),))],
        compiler_params=params(MIB),
        cost_estimate=pl.CostEstimate(flops=0, bytes_accessed=4 * size, transcendentals=0),
        name="move_rows",
    )(*arrays, *after)


def stack_rows(arrays, after):
    moves = []
    place = 0
    for i, x in enumerate(arrays):
        moves.append((i, 0, x.shape[0], 0, place))
        place += x.shape[0]
    return move_rows(arrays, moves, after)[0]


def stack_line(pieces, after):
    count, size = len(pieces), pieces[0].shape[0]
    moves = [(i, 0, size, 0, (count - i if i else 0) * size) for i in range(count)]
    return move_rows(far_first(pieces), moves, after)[0]


def begin_kernel(count, splits, *refs):
    block_refs, (tokens_scr, gains_scr, sems) = refs[3 : 3 + splits], refs[3 + splits :]
    targets = [tokens_scr, gains_scr.at[0], gains_scr.at[1]]
    copies = [pltpu.make_async_copy(refs[i], targets[i], sems.at[i]) for i in range(3)]
    for copy in copies:
        copy.start()
    for copy in copies:
        copy.wait()
    own_rows = tokens_scr.shape[0] // (count * splits)
    for i in range(count):
        for h in range(splits):
            start = (i * splits + h) * own_rows
            block_refs[h][i * own_rows : (i + 1) * own_rows, :] = tokens_scr[
                start : start + own_rows, :
            ]
    lines = []
    for i in range(2):
        gain = gains_scr[i]
        high = gain.astype(jnp.bfloat16).astype(jnp.float32)
        middle = (gain - high).astype(jnp.bfloat16).astype(jnp.float32)
        lines += [high, middle, gain - high - middle]
    lines.append(jnp.zeros((2, lines[0].shape[1]), jnp.float32))
    block_refs[0][count * own_rows :, :] = jnp.concatenate(lines).astype(jnp.bfloat16)


def begin(tokens, norm_gain, final_gain, count, splits):
    rows, width = tokens.shape
    sizes = [rows // splits + (0 if h else 8) for h in range(splits)]
    return pl.pallas_call(
        functools.partial(begin_kernel, count, splits),
        out_shape=tuple(jax.ShapeDtypeStruct((size, width), jnp.bfloat16) for size in sizes),
        in_specs=[anywhere()] * 3,
        out_specs=(whole(),) * splits,
        scratch_shapes=[
            pltpu.VMEM((rows, width), jnp.bfloat16),
            pltpu.VMEM((2, 1, width), jnp.float32),
            pltpu.SemaphoreType.DMA((3,)),
        ],
        compiler_params=params(4 * MIB),
        name="begin",
    )(
        pltpu.with_memory_space_constraint(tokens, pltpu.HBM),
        pltpu.with_memory_space_constraint(norm_gain.reshape(1, width), pltpu.HBM),
        pltpu.with_memory_space_constraint(final_gain.reshape(1, width), pltpu.HBM),
    )


def norm_kernel(splits, part, count, after, *refs):
    slices = refs[:1] + refs[1:count][::-1]
    routes_ref, weights_ref = refs[count : count + 2]
    rest = list(refs[count + 2 :])
    gains_in = rest.pop(0) if part else None
    rest = rest[after:]
    rows_ref, raw_ref = rest[:2]
    gains_ref = gains_in if part else rest[2]
    rows = rows_ref.shape[0]
    width = slices[0].shape[1]
    full_width = width * count
    own_rows = rows // count
    me = lax.axis_index("tensor")
    total = jnp.zeros((rows, 1), jnp.float32)
    for piece in slices:
        value = piece[:rows, :].astype(jnp.float32)
        total = total + jnp.sum(value * value, axis=1, keepdims=True)
    scale = lax.rsqrt(total / full_width + epsilon)
    start = pl.multiple_of(me * own_rows, own_rows)
    for d in range(count):
        columns = pl.ds(pl.multiple_of((me ^ d) * width, width), width)
        if not part:
            tail = slices[d][rows:, :].astype(jnp.float32)
            gains_ref[0:1, columns] = tail[0:1] + tail[1:2] + tail[2:3]
            gains_ref[1:2, columns] = tail[3:4] + tail[4:5] + tail[5:6]
        value = slices[d][:rows, :].astype(jnp.float32)
        rows_ref[:, columns] = (value * scale * gains_ref[0:1, columns]).astype(jnp.bfloat16)
        raw_ref[:, columns] = slices[d][pl.ds(start, own_rows), :]
    lane = lax.broadcasted_iota(jnp.int32, (own_rows, LANES), 1)
    expert = lane // 3
    kind = lane - expert * 3
    for i in range(count):
        block = pl.ds((i * splits + part) * own_rows, own_rows)
        weight = jnp.zeros((own_rows, LANES), jnp.float32)
        for j in range(routes_ref.shape[1]):
            named = routes_ref[block, j : j + 1] == expert
            weight = weight + jnp.where(named, weights_ref[block, j : j + 1], 0.0)
        high = weight.astype(jnp.bfloat16).astype(jnp.float32)
        middle = (weight - high).astype(jnp.bfloat16).astype(jnp.float32)
        low = weight - high - middle
        value = jnp.where(kind == 0, high, jnp.where(kind == 1, middle, low))
        rows_ref[i * own_rows : (i + 1) * own_rows, full_width:] = value.astype(jnp.bfloat16)


def norm_rows(slices, gains, routes, route_weights, splits, part, rows, after):
    width = slices[0].shape[1]
    count = len(slices)
    full_width = width * count
    gains = gains if part else []
    made = [] if part else [jax.ShapeDtypeStruct((8, full_width), jnp.float32)]
    return pl.pallas_call(
        functools.partial(norm_kernel, splits, part, count, len(after)),
        out_shape=(
            jax.ShapeDtypeStruct((rows, full_width + LANES), jnp.bfloat16),
            jax.ShapeDtypeStruct((rows // count, full_width), jnp.bfloat16),
            *made,
        ),
        in_specs=[whole()] * (count + 2 + len(gains)) + [anywhere()] * len(after),
        out_specs=(whole(),) * (2 + len(made)),
        compiler_params=params(6 * MIB),
        cost_estimate=pl.CostEstimate(
            flops=6 * rows * full_width, bytes_accessed=4 * rows * full_width, transcendentals=rows
        ),
        name="norm_rows",
    )(*far_first(slices), routes, route_weights, *gains, *after)


def hidden_kernel(pieces, after, tile, first, steps, *refs):
    piece_refs = refs[:pieces]
    weight_refs = refs[pieces : pieces + 2]
    out_ref, rows_scr, route_scr, weight_scr, sems, weight_sems = refs[pieces + 2 + after :]
    full_width = weight_scr.shape[2]

    def fetch(i, act):
        columns = pl.ds((first + i) * tile, tile)
        for j in range(2):
            act(
                pltpu.make_async_copy(
                    weight_refs[j].at[0, :, columns],
                    weight_scr.at[j, i % SLOTS],
                    weight_sems.at[j, i % SLOTS],
                )
            )

    def start(copy):
        copy.start()

    def wait(copy):
        copy.wait()

    fetch(0, start)
    total_rows = rows_scr.shape[0]
    copies, ends = [], []
    for i in range(pieces):
        place = ends[-1] if ends else 0
        ends.append(place + piece_refs[i].shape[0])
        block = rows_scr.at[pl.ds(place, piece_refs[i].shape[0]), :]
        copies.append(pltpu.make_async_copy(piece_refs[i], block, sems.at[i]))
    for copy in copies:
        copy.start()
    for i in range(1, min(SLOTS - 1, steps)):
        fetch(i, start)

    def route_weights_of(block):
        small = rows_scr[block, full_width:].astype(jnp.float32)
        lane = lax.broadcasted_iota(jnp.int32, small.shape, 1)
        place = lax.axis_index("expert") * 3
        mine = (lane >= place) & (lane < place + 3)
        weight = jnp.sum(jnp.where(mine, small, 0.0), axis=1, keepdims=True)
        route_scr[block, :] = jnp.broadcast_to(0.5 * weight, small.shape)

    def work(i, block):
        rows = rows_scr[block, :full_width]
        gate = jnp.dot(rows, weight_scr[0, i % SLOTS], preferred_element_type=jnp.float32)
        up = jnp.dot(rows, weight_scr[1, i % SLOTS], preferred_element_type=jnp.float32)
        hidden = gate * (1.0 + jnp.tanh(0.5 * gate)) * up * route_scr[block, :1]
        out_ref[block, i * tile : (i + 1) * tile] = hidden.astype(jnp.bfloat16)

    cut = ends.index(total_rows // 2) + 1 if total_rows // 2 in ends else pieces
    for copy in copies[:cut]:
        copy.wait()
    first_rows = slice(0, ends[cut - 1])
    route_weights_of(first_rows)
    fetch(0, wait)
    if SLOTS - 1 < steps:
        fetch(SLOTS - 1, start)
    work(0, first_rows)
    if cut < pieces:
        for copy in copies[cut:]:
            copy.wait()
        other_rows = slice(ends[cut - 1], total_rows)
        route_weights_of(other_rows)
        work(0, other_rows)
    for i in range(1, steps):
        fetch(i, wait)
        if i + SLOTS - 1 < steps:
            fetch(i + SLOTS - 1, start)
        work(i, slice(0, total_rows))


def tile_of(weight):
    hidden = weight.shape[2]
    return next(t for t in (256, 128, hidden) if hidden % t == 0)


def hidden_rows(pieces, w_gate, w_up, after, first, steps, tile):
    rows = sum(p.shape[0] for p in pieces)
    full_width = w_gate.shape[1]
    hidden = steps * tile
    return pl.pallas_call(
        functools.partial(hidden_kernel, len(pieces), len(after), tile, first, steps),
        out_shape=jax.ShapeDtypeStruct((rows, hidden), jnp.bfloat16),
        in_specs=[anywhere()] * (len(pieces) + 2 + len(after)),
        out_specs=whole(),
        scratch_shapes=[
            pltpu.VMEM((rows, full_width + LANES), jnp.bfloat16),
            pltpu.VMEM((rows, LANES), jnp.float32),
            pltpu.VMEM((2, SLOTS, full_width, tile), jnp.bfloat16),
            pltpu.SemaphoreType.DMA((len(pieces),)),
            pltpu.SemaphoreType.DMA((2, SLOTS)),
        ],
        compiler_params=params((18 + rows // 64) * MIB),
        cost_estimate=pl.CostEstimate(
            flops=4 * rows * full_width * hidden,
            bytes_accessed=4 * full_width * hidden + 2 * rows * (full_width + hidden),
            transcendentals=rows * hidden,
        ),
        name="hidden_rows",
    )(*pieces, w_gate, w_up, *after)


def down_kernel(start, count, *refs):
    hidden_refs, down_ref, out_ref = refs[:count], refs[count], refs[-1]
    full_width = out_ref.shape[1]
    tile = 512 if full_width % 512 == 0 else full_width

    @pl.loop(0, full_width // tile, unroll=True)
    def _(i):
        columns = pl.ds(pl.multiple_of(i * tile, tile), tile)
        out = None
        depth = 0
        for hidden_ref in hidden_refs:
            rows = hidden_ref[start : start + out_ref.shape[0], :]
            block = down_ref[0, depth : depth + rows.shape[1], columns]
            term = jnp.dot(rows, block, preferred_element_type=jnp.float32)
            out = term if out is None else out + term
            depth += rows.shape[1]
        out_ref[:, columns] = out.astype(jnp.bfloat16)


def down_rows(hidden, w_down, start, rows, after):
    depth, full_width = w_down.shape[1:]
    hidden = [pltpu.with_memory_space_constraint(part, pltpu.VMEM) for part in hidden]
    return pl.pallas_call(
        functools.partial(down_kernel, start, len(hidden)),
        out_shape=jax.ShapeDtypeStruct((rows, full_width), jnp.bfloat16),
        in_specs=[whole()] * (len(hidden) + 1) + [anywhere()] * len(after),
        out_specs=whole(),
        compiler_params=params((4 + rows // 64) * MIB),
        cost_estimate=pl.CostEstimate(
            flops=2 * rows * depth * full_width,
            bytes_accessed=2 * rows * (depth + full_width),
            transcendentals=0,
        ),
        name="down_rows",
    )(*hidden, w_down, *after)


def many_rows(pieces, w_gate, w_up, w_down):
    outs = []
    tile = tile_of(w_gate)
    steps = w_gate.shape[2] // tile
    while pieces:
        count = 1
        while count < len(pieces) and sum(p.shape[0] for p in pieces[: count + 1]) <= LARGEST:
            count += 1
        hidden = hidden_rows(pieces[:count], w_gate, w_up, [], 0, steps, tile)
        outs.append(down_rows([hidden], w_down, 0, hidden.shape[0], []))
        pieces = pieces[count:]
    return jnp.concatenate(outs)


def final_kernel(parts, *refs):
    part_refs = refs[: parts + 2]
    out_ref, rows_scr, gains_scr, sems = refs[-4:]
    targets = [rows_scr.at[i] for i in range(parts + 1)] + [gains_scr]
    copies = [
        pltpu.make_async_copy(part_refs[i], targets[i], sems.at[i]) for i in range(parts + 2)
    ]
    for copy in copies:
        copy.start()
    for copy in copies:
        copy.wait()
    mixed = rows_scr[0].astype(jnp.float32)
    for i in range(1, parts):
        mixed = mixed + rows_scr[i].astype(jnp.float32)
    residual = rows_scr[parts].astype(jnp.float32) + mixed
    residual = residual.astype(jnp.bfloat16).astype(jnp.float32)
    total = jnp.sum(residual * residual, axis=1, keepdims=True)
    scale = lax.rsqrt(total / residual.shape[1] + epsilon)
    out_ref[...] = (residual * scale * gains_scr[1:2, :]).astype(jnp.bfloat16)


def final_rows(parts, raw, gains, after):
    rows, full_width = raw.shape
    return pl.pallas_call(
        functools.partial(final_kernel, len(parts)),
        out_shape=jax.ShapeDtypeStruct((rows, full_width), jnp.bfloat16),
        in_specs=[anywhere()] * (len(parts) + 2 + len(after)),
        out_specs=whole(),
        scratch_shapes=[
            pltpu.VMEM((len(parts) + 1, rows, full_width), jnp.bfloat16),
            pltpu.VMEM(gains.shape, jnp.float32),
            pltpu.SemaphoreType.DMA((len(parts) + 2,)),
        ],
        compiler_params=params(6 * MIB),
        cost_estimate=pl.CostEstimate(
            flops=8 * rows * full_width, bytes_accessed=12 * rows * full_width, transcendentals=rows
        ),
        name="final_rows",
    )(*parts, raw, gains, *after)


def head_kernel(pieces, tile, sub, earlier, *refs):
    piece_refs = refs[:pieces]
    head_ref, target_ref = refs[pieces : pieces + 2]
    earlier_refs = refs[pieces + 2 : pieces + 2 + earlier]
    out_refs, rows_scr, head_scr, sems, head_sems = refs[pieces + 2 + earlier :]
    for earlier_ref in earlier_refs:
        out_refs[: earlier_ref.shape[0], :] = earlier_ref[...]
    out_ref = out_refs.at[pl.ds(out_refs.shape[0] - 8, 8), :]
    vocab_part = head_ref.shape[0]
    steps = vocab_part // tile
    my_expert, my_tensor = lax.axis_index("expert"), lax.axis_index("tensor")
    n_tensor = lax.axis_size("tensor")

    def fetch(i):
        return pltpu.make_async_copy(
            head_ref.at[pl.ds(pl.multiple_of(i * tile, tile), tile), :],
            head_scr.at[i],
            head_sems.at[i],
        )

    copies = []
    for piece_ref in piece_refs:
        for start in range(0, piece_ref.shape[0], sub):
            far_expert, far_tensor = divmod(len(copies), n_tensor)
            block = (my_expert ^ far_expert) * n_tensor + (my_tensor ^ far_tensor)
            copies.append(
                pltpu.make_async_copy(
                    piece_ref.at[pl.ds(start, sub), :],
                    rows_scr.at[pl.ds(pl.multiple_of(block * sub, sub), sub), :],
                    sems.at[len(copies)],
                )
            )
    ahead = min(2, steps)
    fetch(0).start()
    for copy in copies:
        copy.start()
    for i in range(1, ahead):
        fetch(i).start()
    for copy in copies:
        copy.wait()
    lane = lax.broadcasted_iota(jnp.int32, out_ref.shape, 0)
    out_ref[...] = jnp.where(lane == 0, -jnp.inf, 0.0)
    targets = target_ref[...] - (my_expert * n_tensor + my_tensor) * vocab_part

    @pl.loop(0, steps)
    def _(i):
        fetch(i).wait()

        @pl.when(i + ahead < steps)
        def _():
            fetch(i + ahead).start()

        logits = lax.dot_general(
            head_scr[i],
            rows_scr[...],
            (((1,), (1,)), ((), ())),
            preferred_element_type=jnp.float32,
        )
        word = lax.broadcasted_iota(jnp.int32, logits.shape, 0) + i * tile
        old_top, old_total = out_ref[0:1, :], out_ref[1:2, :]
        top = jnp.maximum(old_top, jnp.max(logits, axis=0, keepdims=True))
        out_ref[0:1, :] = top
        out_ref[1:2, :] = old_total * jnp.exp(old_top - top) + jnp.sum(
            jnp.exp(logits - top), axis=0, keepdims=True
        )
        hit = word == targets
        out_ref[2:3, :] += jnp.sum(jnp.where(hit, logits, 0.0), axis=0, keepdims=True)


def head_terms(pieces, head_rows, targets, sub, earlier):
    rows = sum(p.shape[0] for p in pieces)
    vocab_part, full_width = head_rows.shape
    tile = next(t for t in (400, 200, 80, 8, vocab_part) if vocab_part % t == 0)
    return pl.pallas_call(
        functools.partial(head_kernel, len(pieces), tile, sub, len(earlier)),
        out_shape=jax.ShapeDtypeStruct((8 + sum(e.shape[0] for e in earlier), rows), jnp.float32),
        in_specs=[anywhere()] * (len(pieces) + 1) + [whole()] * (1 + len(earlier)),
        out_specs=whole(),
        scratch_shapes=[
            pltpu.VMEM((rows, full_width), jnp.bfloat16),
            pltpu.VMEM((vocab_part // tile, tile, full_width), jnp.bfloat16),
            pltpu.SemaphoreType.DMA((rows // sub,)),
            pltpu.SemaphoreType.DMA((vocab_part // tile,)),
        ],
        compiler_params=params((22 + rows // 64) * MIB),
        cost_estimate=pl.CostEstimate(
            flops=2 * rows * full_width * vocab_part,
            bytes_accessed=2 * full_width * (vocab_part + rows),
            transcendentals=rows * vocab_part,
        ),
        name="head_terms",
    )(*pieces, head_rows, targets, *earlier)


def join_kernel(last, *refs):
    out_ref = refs[-1]
    for line in range(0, out_ref.shape[0], 8):

        def each(offset):
            return [ref[line + offset : line + offset + 1, :] for ref in refs[:-1]]

        tops = each(0)
        top = functools.reduce(jnp.maximum, tops)
        total = sum(t * jnp.exp(m - top) for m, t in zip(tops, each(1)))
        target = sum(each(2))
        if last:
            out_ref[line : line + 1, :] = top + jnp.log(total) - target
        else:
            out_ref[line : line + 1, :] = top
            out_ref[line + 1 : line + 2, :] = total
            out_ref[line + 2 : line + 3, :] = target


def join_all(terms):
    for axis in ("tensor", "expert"):
        (terms,) = small_call(
            functools.partial(join_kernel, axis == "expert"),
            "join",
            far_first(gather_near(terms, axis)),
            [],
            [(terms.shape, jnp.float32)],
            [],
            2 * MIB,
        )
    return terms


def pack_kernel(kept_ref, got_ref, one_ref, two_ref, home_ref, side_ref):
    rows = home_ref.shape[0]
    half = rows // 2

    def both(d, first):
        block = slice(d * rows + first, d * rows + first + half)
        return kept_ref[block, :].astype(jnp.float32) + got_ref[block, :].astype(jnp.float32)

    one_ref[:half, :] = both(1, 0).astype(jnp.bfloat16)
    one_ref[half:, :] = both(3, 0).astype(jnp.bfloat16)
    two_ref[:half, :] = both(2, half).astype(jnp.bfloat16)
    two_ref[half:, :] = both(3, half).astype(jnp.bfloat16)
    home_ref[:half, :] = both(0, 0)
    home_ref[half:, :] = both(0, half)
    side_ref[0] = both(1, half)
    side_ref[1] = both(2, 0)


def pass_kernel(side_ref, one_ref, two_ref, *refs):
    pass_one_ref, pass_two_ref = refs[-2:]
    half = pass_one_ref.shape[0]
    pass_one_ref[...] = (side_ref[0] + two_ref[half:, :].astype(jnp.float32)).astype(jnp.bfloat16)
    pass_two_ref[...] = (side_ref[1] + one_ref[half:, :].astype(jnp.float32)).astype(jnp.bfloat16)


def total_kernel(count, column, *refs):
    home_ref, one_ref, two_ref, last_one_ref, last_two_ref = refs[:5]
    column_refs = refs[5 : 5 + column]
    outs = refs[5 + column : 5 + column + count]
    work, sems = refs[-2:]
    half = last_one_ref.shape[0]
    sub = outs[0].shape[0]
    me = lax.axis_index("tensor")
    copies = [
        pltpu.make_async_copy(
            column_refs[i], refs[-3].at[pl.ds(i * sub, sub), :], sems.at[i]
        )
        for i in range(column)
    ]
    for copy in copies:
        copy.start()
    upper = one_ref[:half, :].astype(jnp.float32) + last_two_ref[...].astype(jnp.float32)
    lower = two_ref[:half, :].astype(jnp.float32) + last_one_ref[...].astype(jnp.float32)
    work[:half, :] = home_ref[:half, :] + upper
    work[half:, :] = home_ref[half:, :] + lower
    for d in range(count):
        block = pl.ds(pl.multiple_of((me ^ d) * sub, sub), sub)
        outs[d][...] = work[block, :].astype(jnp.bfloat16)
    for copy in copies:
        copy.wait()


def totals_of(home, ones, lasts, count, sub, column):
    rows, full_width = home.shape
    piece = jax.ShapeDtypeStruct((sub, full_width), jnp.bfloat16)
    stacked = jax.ShapeDtypeStruct((sub * len(column), full_width), jnp.bfloat16)
    outs = pl.pallas_call(
        functools.partial(total_kernel, count, len(column)),
        out_shape=(piece,) * count + ((stacked,) if column else ()),
        in_specs=[whole()] * 5 + [anywhere()] * len(column),
        out_specs=(whole(),) * count + ((anywhere(),) if column else ()),
        scratch_shapes=[
            pltpu.VMEM((rows, full_width), jnp.float32),
            pltpu.SemaphoreType.DMA((max(1, len(column)),)),
        ],
        compiler_params=params(8 * MIB),
        cost_estimate=pl.CostEstimate(
            flops=4 * home.size, bytes_accessed=20 * home.size, transcendentals=0
        ),
        name="total",
    )(home, *ones, *lasts, *column)
    return list(outs[:count]), list(outs[count:])


def small_call(kernel, name, inputs, after, outs, scratch, limit):
    size = sum(x.size * x.dtype.itemsize for x in inputs)
    return pl.pallas_call(
        kernel,
        out_shape=tuple(jax.ShapeDtypeStruct(*out) for out in outs),
        in_specs=[whole()] * len(inputs) + [anywhere()] * len(after),
        out_specs=(whole(),) * len(outs),
        scratch_shapes=scratch,
        compiler_params=params(limit),
        cost_estimate=pl.CostEstimate(flops=size, bytes_accessed=2 * size, transcendentals=0),
        name=name,
    )(*inputs, *after)


def sum_plane(kept, got, rows, column):
    f32, b16 = jnp.float32, jnp.bfloat16
    n_tensor = lax.axis_size("tensor")
    count, full_width = kept.shape[0] // rows, kept.shape[1]
    half = rows // 2
    sub = rows // n_tensor
    if count == 4 and half % 16 == 0 and sub % 16 == 0:
        one, two, home, side = small_call(
            pack_kernel,
            "pack",
            [kept, got],
            [],
            [((rows, full_width), b16)] * 2
            + [((rows, full_width), f32), ((2, half, full_width), f32)],
            [],
            10 * MIB,
        )
        from_one, from_two = swap(one, "expert", 1), swap(two, "expert", 2)
        pass_one, pass_two = small_call(
            pass_kernel,
            "pass_on",
            [side, from_one, from_two],
            column[:0:-1],
            [((half, full_width), b16)] * 2,
            [],
            6 * MIB,
        )
        last_one, last_two = swap(pass_one, "expert", 1), swap(pass_two, "expert", 2)
        pieces, stacked = totals_of(
            home, [from_one, from_two], [last_one, last_two], n_tensor, sub, column
        )
        return pieces, [one, two], [pass_one, pass_two], stacked
    both = (kept.astype(f32) + got.astype(f32)).reshape(count, rows, full_width)
    total = both[0]
    for d in range(1, count):
        total = total + swap(both[d].astype(b16), "expert", d).astype(f32)
    total = total.astype(b16).reshape(n_tensor, sub, full_width)
    me = lax.axis_index("tensor")
    pieces = [lax.dynamic_index_in_dim(total, me ^ d, 0, False) for d in range(n_tensor)]
    return pieces, [], [], []


def on_device(
    tokens, routes, route_weights, norm_gain, final_gain, w_gate, w_up, w_down, head_weight, targets
):
    tok_rows, width = tokens.shape
    n_expert = lax.axis_size("expert")
    n_tensor = lax.axis_size("tensor")
    my_expert = lax.axis_index("expert")
    my_tensor = lax.axis_index("tensor")
    full_width = width * n_tensor
    own = tok_rows // n_tensor
    splits = 2 if own % 32 == 0 else 1
    sub = own // splits
    rows = sub * n_tensor

    blocks = begin(tokens, norm_gain, final_gain, n_tensor, splits)
    slices = [gather_near(block, "tensor") for block in blocks]
    gains = None
    planes, raws = [], []
    after = []
    for h in range(splits):
        normed, raw, *made = norm_rows(
            slices[h], [gains], routes, route_weights, splits, h, rows, after
        )
        if made:
            gains = made[0]
        plane, _ = gather_plane(normed, "expert", [])
        planes.append(plane)
        raws.append(raw)
        after = plane[3:]

    w_gate = pltpu.with_memory_space_constraint(w_gate, pltpu.HBM)
    w_up = pltpu.with_memory_space_constraint(w_up, pltpu.HBM)
    head_rows = pltpu.with_memory_space_constraint(head_weight.T, pltpu.HBM)
    target_rows = targets.reshape(n_expert, n_tensor, splits, sub)
    terms = []
    before = {}
    for h in range(splits):
        if 2 * n_expert * rows <= LARGEST:
            nearer = stack_rows(planes[h][:3], [] if before else sum((p[:0:-1] for p in slices[1:2]), []))
            away = [swap(nearer, "seq", 1)]
            if planes[h][3:]:
                away.append(swap(stack_rows(planes[h][3:], before.get("kept", [])), "seq", 1))
            half = n_expert * rows
            everything = planes[h] + away
            tile = tile_of(w_gate)
            count = w_gate.shape[2] // tile
            cuts = [0, (count + 1) // 2, count - 1, count] if h else [0, count]
            ties = [before.get(key, []) for key in ("packed", "passed", "totals")]
            hidden = [
                hidden_rows(
                    everything, w_gate, w_up, ties[i], cuts[i], cuts[i + 1] - cuts[i], tile
                )
                for i in range(len(cuts) - 1)
            ]
            later = planes[h + 1][1:3] if h + 1 < splits else []
            other = down_rows(hidden, w_down, half, half, later + before.get("sums", [])[::-1])
            kept = down_rows(hidden, w_down, 0, half, before.get("final", []))
        else:
            away = [swap(p, "seq", 1) for p in planes[h]]
            kept, other = many_rows(planes[h], w_gate, w_up, w_down), many_rows(
                away, w_gate, w_up, w_down
            )
        got = swap(other, "seq", 1)
        totals, packed, passed, stacked = sum_plane(kept, got, rows, before.get("column", []))
        sums = swap_each(totals[1:], "tensor")
        cut = []
        if before:
            plane, cut = gather_plane(stacked[0], "expert", [])
            wanted = target_rows[:, :, h - 1].reshape(1, -1)
            terms = [head_terms(plane, head_rows, wanted, sub, terms)]
        final = final_rows(far_first(totals[:1] + sums), raws[h], gains, [])
        column = gather_near(final, "tensor")
        before = {
            "kept": [kept],
            "packed": packed,
            "passed": passed,
            "totals": totals,
            "sums": sums,
            "final": [final],
            "column": column,
        }
    column = stack_line(column, cut)
    plane, _ = gather_plane(column, "expert", terms)
    wanted = target_rows[:, :, splits - 1].reshape(1, -1)
    terms = [head_terms(plane, head_rows, wanted, sub, terms)]
    losses = join_all(terms[0])[::8]
    start = (my_expert * n_tensor + my_tensor) * sub
    return lax.dynamic_slice_in_dim(losses, start, sub, 1).reshape(own)


def solution(mesh):
    return jax.shard_map(
        on_device,
        mesh=mesh,
        in_specs=(
            P(("seq", "expert"), "tensor"),
            P(("seq", "expert"), None),
            P(("seq", "expert"), None),
            P("tensor"),
            P("tensor"),
            P("expert", None, ("seq", "tensor")),
            P("expert", None, ("seq", "tensor")),
            P("expert", ("seq", "tensor"), None),
            P(None, ("expert", "tensor")),
            P("seq"),
        ),
        out_specs=P(("seq", "expert", "tensor")),
        check_vma=False,
    )
```

```python
import functools

import jax
import jax.numpy as jnp
from jax import lax
from jax.experimental import pallas as pl
from jax.experimental.pallas import tpu as pltpu
from jax.sharding import PartitionSpec as P

epsilon = 1e-05
LANES = 128
SLOTS = 3
LARGEST = 512
MIB = 1024 * 1024
VMEM_BYTES = 56 * 1024 * 1024


def params(limit=VMEM_BYTES):
    return pltpu.CompilerParams(vmem_limit_bytes=limit)


def whole():
    return pl.BlockSpec(memory_space=pltpu.VMEM)


def anywhere():
    return pl.BlockSpec(memory_space=pl.ANY)


def swap(x, axis, distance):
    size = lax.axis_size(axis)
    return lax.ppermute(x, axis, [(i, i ^ distance) for i in range(size)])


def gather_near(x, axis):
    return [x] + swap_each([x] * (lax.axis_size(axis) - 1), axis)


def swap_each(pieces, axis):
    return [swap(piece, axis, d + 1) for d, piece in enumerate(pieces)]


def far_first(pieces):
    return pieces[:1] + pieces[1:][::-1]


def gather_plane(x, axis, after):
    if lax.axis_size(axis) != 4:
        return gather_near(x, axis), []
    half = x.shape[0] // 2
    one, two = swap(x, axis, 1), swap(x, axis, 2)
    upper, lower = move_rows([two, one], [(0, 0, half, 0, 0), (1, half, half, 1, 0)], after)
    return [x, one, two, swap(upper, axis, 1), swap(lower, axis, 2)], [upper, lower]


def move_kernel(sources, targets, moves, *refs):
    out_refs, sems = refs[-targets - 1 : -1], refs[-1]
    copies = []
    for i, (source, start, count, target, place) in enumerate(moves):
        copies.append(
            pltpu.make_async_copy(
                refs[source].at[pl.ds(start, count), :],
                out_refs[target].at[pl.ds(place, count), :],
                sems.at[i],
            )
        )
    for copy in copies:
        copy.start()
    for copy in copies:
        copy.wait()


def move_rows(arrays, moves, after):
    targets = 1 + max(m[3] for m in moves)
    sizes = [sum(m[2] for m in moves if m[3] == t) for t in range(targets)]
    size = sum(sizes) * arrays[0].shape[1]
    return pl.pallas_call(
        functools.partial(move_kernel, len(arrays), targets, moves),
        out_shape=tuple(
            jax.ShapeDtypeStruct((rows, arrays[0].shape[1]), arrays[0].dtype) for rows in sizes
        ),
        in_specs=[anywhere()] * (len(arrays) + len(after)),
        out_specs=(anywhere(),) * targets,
        scratch_shapes=[pltpu.SemaphoreType.DMA((len(moves),))],
        compiler_params=params(MIB),
        cost_estimate=pl.CostEstimate(flops=0, bytes_accessed=4 * size, transcendentals=0),
        name="move_rows",
    )(*arrays, *after)


def stack_rows(arrays, after):
    moves = []
    place = 0
    for i, x in enumerate(arrays):
        moves.append((i, 0, x.shape[0], 0, place))
        place += x.shape[0]
    return move_rows(arrays, moves, after)[0]


def stack_line(pieces, after):
    count, size = len(pieces), pieces[0].shape[0]
    moves = [(i, 0, size, 0, (count - i if i else 0) * size) for i in range(count)]
    return move_rows(far_first(pieces), moves, after)[0]


def load_pieces(piece_refs, scratch, sems):
    copies = []
    start = 0
    for i in range(len(piece_refs)):
        count = piece_refs[i].shape[0]
        copies.append(
            pltpu.make_async_copy(piece_refs[i], scratch.at[pl.ds(start, count), :], sems.at[i])
        )
        start += count
    for copy in copies:
        copy.start()
    for copy in copies:
        copy.wait()


def begin_kernel(count, splits, *refs):
    block_refs, (tokens_scr, gains_scr, sems) = refs[3 : 3 + splits], refs[3 + splits :]
    targets = [tokens_scr, gains_scr.at[0], gains_scr.at[1]]
    copies = [pltpu.make_async_copy(refs[i], targets[i], sems.at[i]) for i in range(3)]
    for copy in copies:
        copy.start()
    for copy in copies:
        copy.wait()
    own_rows = tokens_scr.shape[0] // (count * splits)
    for i in range(count):
        for h in range(splits):
            start = (i * splits + h) * own_rows
            block_refs[h][i * own_rows : (i + 1) * own_rows, :] = tokens_scr[
                start : start + own_rows, :
            ]
    lines = []
    for i in range(2):
        gain = gains_scr[i]
        high = gain.astype(jnp.bfloat16).astype(jnp.float32)
        middle = (gain - high).astype(jnp.bfloat16).astype(jnp.float32)
        lines += [high, middle, gain - high - middle]
    lines.append(jnp.zeros((2, lines[0].shape[1]), jnp.float32))
    block_refs[0][count * own_rows :, :] = jnp.concatenate(lines).astype(jnp.bfloat16)


def begin(tokens, norm_gain, final_gain, count, splits):
    rows, width = tokens.shape
    sizes = [rows // splits + (0 if h else 8) for h in range(splits)]
    return pl.pallas_call(
        functools.partial(begin_kernel, count, splits),
        out_shape=tuple(jax.ShapeDtypeStruct((size, width), jnp.bfloat16) for size in sizes),
        in_specs=[anywhere()] * 3,
        out_specs=(whole(),) * splits,
        scratch_shapes=[
            pltpu.VMEM((rows, width), jnp.bfloat16),
            pltpu.VMEM((2, 1, width), jnp.float32),
            pltpu.SemaphoreType.DMA((3,)),
        ],
        compiler_params=params(4 * MIB),
        name="begin",
    )(
        pltpu.with_memory_space_constraint(tokens, pltpu.HBM),
        pltpu.with_memory_space_constraint(norm_gain.reshape(1, width), pltpu.HBM),
        pltpu.with_memory_space_constraint(final_gain.reshape(1, width), pltpu.HBM),
    )


def norm_kernel(splits, part, count, after, *refs):
    slices = refs[:1] + refs[1:count][::-1]
    routes_ref, weights_ref = refs[count : count + 2]
    rest = list(refs[count + 2 :])
    gains_in = rest.pop(0) if part else None
    rest = rest[after:]
    rows_ref, raw_ref = rest[:2]
    gains_ref = gains_in if part else rest[2]
    rows = rows_ref.shape[0]
    width = slices[0].shape[1]
    full_width = width * count
    own_rows = rows // count
    me = lax.axis_index("tensor")
    total = jnp.zeros((rows, 1), jnp.float32)
    for piece in slices:
        value = piece[:rows, :].astype(jnp.float32)
        total = total + jnp.sum(value * value, axis=1, keepdims=True)
    scale = lax.rsqrt(total / full_width + epsilon)
    start = pl.multiple_of(me * own_rows, own_rows)
    for d in range(count):
        columns = pl.ds(pl.multiple_of((me ^ d) * width, width), width)
        if not part:
            tail = slices[d][rows:, :].astype(jnp.float32)
            gains_ref[0:1, columns] = tail[0:1] + tail[1:2] + tail[2:3]
            gains_ref[1:2, columns] = tail[3:4] + tail[4:5] + tail[5:6]
        value = slices[d][:rows, :].astype(jnp.float32)
        rows_ref[:, columns] = (value * scale * gains_ref[0:1, columns]).astype(jnp.bfloat16)
        raw_ref[:, columns] = slices[d][pl.ds(start, own_rows), :]
    lane = lax.broadcasted_iota(jnp.int32, (own_rows, LANES), 1)
    expert = lane // 3
    kind = lane - expert * 3
    for i in range(count):
        block = pl.ds((i * splits + part) * own_rows, own_rows)
        weight = jnp.zeros((own_rows, LANES), jnp.float32)
        for j in range(routes_ref.shape[1]):
            named = routes_ref[block, j : j + 1] == expert
            weight = weight + jnp.where(named, weights_ref[block, j : j + 1], 0.0)
        high = weight.astype(jnp.bfloat16).astype(jnp.float32)
        middle = (weight - high).astype(jnp.bfloat16).astype(jnp.float32)
        low = weight - high - middle
        value = jnp.where(kind == 0, high, jnp.where(kind == 1, middle, low))
        rows_ref[i * own_rows : (i + 1) * own_rows, full_width:] = value.astype(jnp.bfloat16)


def norm_rows(slices, gains, routes, route_weights, splits, part, rows, after):
    width = slices[0].shape[1]
    count = len(slices)
    full_width = width * count
    gains = gains if part else []
    made = [] if part else [jax.ShapeDtypeStruct((8, full_width), jnp.float32)]
    return pl.pallas_call(
        functools.partial(norm_kernel, splits, part, count, len(after)),
        out_shape=(
            jax.ShapeDtypeStruct((rows, full_width + LANES), jnp.bfloat16),
            jax.ShapeDtypeStruct((rows // count, full_width), jnp.bfloat16),
            *made,
        ),
        in_specs=[whole()] * (count + 2 + len(gains)) + [anywhere()] * len(after),
        out_specs=(whole(),) * (2 + len(made)),
        compiler_params=params(6 * MIB),
        cost_estimate=pl.CostEstimate(
            flops=6 * rows * full_width, bytes_accessed=4 * rows * full_width, transcendentals=rows
        ),
        name="norm_rows",
    )(*far_first(slices), routes, route_weights, *gains, *after)


def hidden_kernel(pieces, after, tile, first, steps, *refs):
    piece_refs = refs[:pieces]
    weight_refs = refs[pieces : pieces + 2]
    out_ref, rows_scr, route_scr, weight_scr, sems, weight_sems = refs[pieces + 2 + after :]
    full_width = weight_scr.shape[2]

    def fetch(i, act):
        columns = pl.ds((first + i) * tile, tile)
        for j in range(2):
            act(
                pltpu.make_async_copy(
                    weight_refs[j].at[0, :, columns],
                    weight_scr.at[j, i % SLOTS],
                    weight_sems.at[j, i % SLOTS],
                )
            )

    def start(copy):
        copy.start()

    def wait(copy):
        copy.wait()

    fetch(0, start)
    load_pieces(piece_refs, rows_scr, sems)
    for i in range(1, min(SLOTS - 1, steps)):
        fetch(i, start)
    small = rows_scr[:, full_width:].astype(jnp.float32)
    lane = lax.broadcasted_iota(jnp.int32, small.shape, 1)
    place = lax.axis_index("expert") * 3
    mine = (lane >= place) & (lane < place + 3)
    weight = jnp.sum(jnp.where(mine, small, 0.0), axis=1, keepdims=True)
    route_scr[...] = jnp.broadcast_to(0.5 * weight, route_scr.shape)
    for i in range(steps):
        fetch(i, wait)
        if i + SLOTS - 1 < steps:
            fetch(i + SLOTS - 1, start)
        rows = rows_scr[:, :full_width]
        gate = jnp.dot(rows, weight_scr[0, i % SLOTS], preferred_element_type=jnp.float32)
        up = jnp.dot(rows, weight_scr[1, i % SLOTS], preferred_element_type=jnp.float32)
        hidden = gate * (1.0 + jnp.tanh(0.5 * gate)) * up * route_scr[:, :1]
        out_ref[:, i * tile : (i + 1) * tile] = hidden.astype(jnp.bfloat16)


def tile_of(weight):
    hidden = weight.shape[2]
    return next(t for t in (256, 128, hidden) if hidden % t == 0)


def hidden_rows(pieces, w_gate, w_up, after, first, steps, tile):
    rows = sum(p.shape[0] for p in pieces)
    full_width = w_gate.shape[1]
    hidden = steps * tile
    return pl.pallas_call(
        functools.partial(hidden_kernel, len(pieces), len(after), tile, first, steps),
        out_shape=jax.ShapeDtypeStruct((rows, hidden), jnp.bfloat16),
        in_specs=[anywhere()] * (len(pieces) + 2 + len(after)),
        out_specs=whole(),
        scratch_shapes=[
            pltpu.VMEM((rows, full_width + LANES), jnp.bfloat16),
            pltpu.VMEM((rows, LANES), jnp.float32),
            pltpu.VMEM((2, SLOTS, full_width, tile), jnp.bfloat16),
            pltpu.SemaphoreType.DMA((len(pieces),)),
            pltpu.SemaphoreType.DMA((2, SLOTS)),
        ],
        compiler_params=params((18 + rows // 64) * MIB),
        cost_estimate=pl.CostEstimate(
            flops=4 * rows * full_width * hidden,
            bytes_accessed=4 * full_width * hidden + 2 * rows * (full_width + hidden),
            transcendentals=rows * hidden,
        ),
        name="hidden_rows",
    )(*pieces, w_gate, w_up, *after)


def down_kernel(start, count, *refs):
    hidden_refs, down_ref, out_ref = refs[:count], refs[count], refs[-1]
    full_width = out_ref.shape[1]
    tile = 512 if full_width % 512 == 0 else full_width

    @pl.loop(0, full_width // tile, unroll=True)
    def _(i):
        columns = pl.ds(pl.multiple_of(i * tile, tile), tile)
        out = None
        depth = 0
        for hidden_ref in hidden_refs:
            rows = hidden_ref[start : start + out_ref.shape[0], :]
            block = down_ref[0, depth : depth + rows.shape[1], columns]
            term = jnp.dot(rows, block, preferred_element_type=jnp.float32)
            out = term if out is None else out + term
            depth += rows.shape[1]
        out_ref[:, columns] = out.astype(jnp.bfloat16)


def down_rows(hidden, w_down, start, rows, after):
    depth, full_width = w_down.shape[1:]
    hidden = [pltpu.with_memory_space_constraint(part, pltpu.VMEM) for part in hidden]
    return pl.pallas_call(
        functools.partial(down_kernel, start, len(hidden)),
        out_shape=jax.ShapeDtypeStruct((rows, full_width), jnp.bfloat16),
        in_specs=[whole()] * (len(hidden) + 1) + [anywhere()] * len(after),
        out_specs=whole(),
        compiler_params=params((4 + rows // 64) * MIB),
        cost_estimate=pl.CostEstimate(
            flops=2 * rows * depth * full_width,
            bytes_accessed=2 * rows * (depth + full_width),
            transcendentals=0,
        ),
        name="down_rows",
    )(*hidden, w_down, *after)


def many_rows(pieces, w_gate, w_up, w_down):
    outs = []
    tile = tile_of(w_gate)
    steps = w_gate.shape[2] // tile
    while pieces:
        count = 1
        while count < len(pieces) and sum(p.shape[0] for p in pieces[: count + 1]) <= LARGEST:
            count += 1
        hidden = hidden_rows(pieces[:count], w_gate, w_up, [], 0, steps, tile)
        outs.append(down_rows([hidden], w_down, 0, hidden.shape[0], []))
        pieces = pieces[count:]
    return jnp.concatenate(outs)


def final_kernel(parts, *refs):
    part_refs = refs[: parts + 2]
    out_ref, rows_scr, gains_scr, sems = refs[-4:]
    targets = [rows_scr.at[i] for i in range(parts + 1)] + [gains_scr]
    copies = [
        pltpu.make_async_copy(part_refs[i], targets[i], sems.at[i]) for i in range(parts + 2)
    ]
    for copy in copies:
        copy.start()
    for copy in copies:
        copy.wait()
    mixed = rows_scr[0].astype(jnp.float32)
    for i in range(1, parts):
        mixed = mixed + rows_scr[i].astype(jnp.float32)
    residual = rows_scr[parts].astype(jnp.float32) + mixed
    residual = residual.astype(jnp.bfloat16).astype(jnp.float32)
    total = jnp.sum(residual * residual, axis=1, keepdims=True)
    scale = lax.rsqrt(total / residual.shape[1] + epsilon)
    out_ref[...] = (residual * scale * gains_scr[1:2, :]).astype(jnp.bfloat16)


def final_rows(parts, raw, gains, after):
    rows, full_width = raw.shape
    return pl.pallas_call(
        functools.partial(final_kernel, len(parts)),
        out_shape=jax.ShapeDtypeStruct((rows, full_width), jnp.bfloat16),
        in_specs=[anywhere()] * (len(parts) + 2 + len(after)),
        out_specs=whole(),
        scratch_shapes=[
            pltpu.VMEM((len(parts) + 1, rows, full_width), jnp.bfloat16),
            pltpu.VMEM(gains.shape, jnp.float32),
            pltpu.SemaphoreType.DMA((len(parts) + 2,)),
        ],
        compiler_params=params(6 * MIB),
        cost_estimate=pl.CostEstimate(
            flops=8 * rows * full_width, bytes_accessed=12 * rows * full_width, transcendentals=rows
        ),
        name="final_rows",
    )(*parts, raw, gains, *after)


def head_kernel(pieces, tile, sub, earlier, *refs):
    piece_refs = refs[:pieces]
    head_ref, target_ref = refs[pieces : pieces + 2]
    earlier_refs = refs[pieces + 2 : pieces + 2 + earlier]
    out_refs, rows_scr, head_scr, sems, head_sems = refs[pieces + 2 + earlier :]
    for earlier_ref in earlier_refs:
        out_refs[: earlier_ref.shape[0], :] = earlier_ref[...]
    out_ref = out_refs.at[pl.ds(out_refs.shape[0] - 8, 8), :]
    vocab_part = head_ref.shape[0]
    steps = vocab_part // tile
    my_expert, my_tensor = lax.axis_index("expert"), lax.axis_index("tensor")
    n_tensor = lax.axis_size("tensor")

    def fetch(i):
        return pltpu.make_async_copy(
            head_ref.at[pl.ds(pl.multiple_of(i * tile, tile), tile), :],
            head_scr.at[i],
            head_sems.at[i],
        )

    copies = []
    for piece_ref in piece_refs:
        for start in range(0, piece_ref.shape[0], sub):
            far_expert, far_tensor = divmod(len(copies), n_tensor)
            block = (my_expert ^ far_expert) * n_tensor + (my_tensor ^ far_tensor)
            copies.append(
                pltpu.make_async_copy(
                    piece_ref.at[pl.ds(start, sub), :],
                    rows_scr.at[pl.ds(pl.multiple_of(block * sub, sub), sub), :],
                    sems.at[len(copies)],
                )
            )
    ahead = min(2, steps)
    fetch(0).start()
    for copy in copies:
        copy.start()
    for i in range(1, ahead):
        fetch(i).start()
    for copy in copies:
        copy.wait()
    lane = lax.broadcasted_iota(jnp.int32, out_ref.shape, 0)
    out_ref[...] = jnp.where(lane == 0, -jnp.inf, 0.0)
    targets = target_ref[...] - (my_expert * n_tensor + my_tensor) * vocab_part

    @pl.loop(0, steps)
    def _(i):
        fetch(i).wait()

        @pl.when(i + ahead < steps)
        def _():
            fetch(i + ahead).start()

        logits = lax.dot_general(
            head_scr[i],
            rows_scr[...],
            (((1,), (1,)), ((), ())),
            preferred_element_type=jnp.float32,
        )
        word = lax.broadcasted_iota(jnp.int32, logits.shape, 0) + i * tile
        old_top, old_total = out_ref[0:1, :], out_ref[1:2, :]
        top = jnp.maximum(old_top, jnp.max(logits, axis=0, keepdims=True))
        out_ref[0:1, :] = top
        out_ref[1:2, :] = old_total * jnp.exp(old_top - top) + jnp.sum(
            jnp.exp(logits - top), axis=0, keepdims=True
        )
        hit = word == targets
        out_ref[2:3, :] += jnp.sum(jnp.where(hit, logits, 0.0), axis=0, keepdims=True)


def head_terms(pieces, head_rows, targets, sub, earlier):
    rows = sum(p.shape[0] for p in pieces)
    vocab_part, full_width = head_rows.shape
    tile = next(t for t in (400, 200, 80, 8, vocab_part) if vocab_part % t == 0)
    return pl.pallas_call(
        functools.partial(head_kernel, len(pieces), tile, sub, len(earlier)),
        out_shape=jax.ShapeDtypeStruct((8 + sum(e.shape[0] for e in earlier), rows), jnp.float32),
        in_specs=[anywhere()] * (len(pieces) + 1) + [whole()] * (1 + len(earlier)),
        out_specs=whole(),
        scratch_shapes=[
            pltpu.VMEM((rows, full_width), jnp.bfloat16),
            pltpu.VMEM((vocab_part // tile, tile, full_width), jnp.bfloat16),
            pltpu.SemaphoreType.DMA((rows // sub,)),
            pltpu.SemaphoreType.DMA((vocab_part // tile,)),
        ],
        compiler_params=params((22 + rows // 64) * MIB),
        cost_estimate=pl.CostEstimate(
            flops=2 * rows * full_width * vocab_part,
            bytes_accessed=2 * full_width * (vocab_part + rows),
            transcendentals=rows * vocab_part,
        ),
        name="head_terms",
    )(*pieces, head_rows, targets, *earlier)


def join_kernel(last, *refs):
    out_ref = refs[-1]
    for line in range(0, out_ref.shape[0], 8):

        def each(offset):
            return [ref[line + offset : line + offset + 1, :] for ref in refs[:-1]]

        tops = each(0)
        top = functools.reduce(jnp.maximum, tops)
        total = sum(t * jnp.exp(m - top) for m, t in zip(tops, each(1)))
        target = sum(each(2))
        if last:
            out_ref[line : line + 1, :] = top + jnp.log(total) - target
        else:
            out_ref[line : line + 1, :] = top
            out_ref[line + 1 : line + 2, :] = total
            out_ref[line + 2 : line + 3, :] = target


def join_all(terms):
    for axis in ("tensor", "expert"):
        (terms,) = small_call(
            functools.partial(join_kernel, axis == "expert"),
            "join",
            far_first(gather_near(terms, axis)),
            [],
            [(terms.shape, jnp.float32)],
            [],
            2 * MIB,
        )
    return terms


def pack_kernel(kept_ref, got_ref, one_ref, two_ref, home_ref, side_ref):
    rows = home_ref.shape[0]
    half = rows // 2

    def both(d, first):
        block = slice(d * rows + first, d * rows + first + half)
        return kept_ref[block, :].astype(jnp.float32) + got_ref[block, :].astype(jnp.float32)

    one_ref[:half, :] = both(1, 0).astype(jnp.bfloat16)
    one_ref[half:, :] = both(3, 0).astype(jnp.bfloat16)
    two_ref[:half, :] = both(2, half).astype(jnp.bfloat16)
    two_ref[half:, :] = both(3, half).astype(jnp.bfloat16)
    home_ref[:half, :] = both(0, 0)
    home_ref[half:, :] = both(0, half)
    side_ref[0] = both(1, half)
    side_ref[1] = both(2, 0)


def pass_kernel(side_ref, one_ref, two_ref, *refs):
    pass_one_ref, pass_two_ref = refs[-2:]
    half = pass_one_ref.shape[0]
    pass_one_ref[...] = (side_ref[0] + two_ref[half:, :].astype(jnp.float32)).astype(jnp.bfloat16)
    pass_two_ref[...] = (side_ref[1] + one_ref[half:, :].astype(jnp.float32)).astype(jnp.bfloat16)


def total_kernel(count, column, *refs):
    home_ref, one_ref, two_ref, last_one_ref, last_two_ref = refs[:5]
    column_refs = refs[5 : 5 + column]
    outs = refs[5 + column : 5 + column + count]
    work, sems = refs[-2:]
    half = last_one_ref.shape[0]
    sub = outs[0].shape[0]
    me = lax.axis_index("tensor")
    copies = [
        pltpu.make_async_copy(
            column_refs[i], refs[-3].at[pl.ds(i * sub, sub), :], sems.at[i]
        )
        for i in range(column)
    ]
    for copy in copies:
        copy.start()
    upper = one_ref[:half, :].astype(jnp.float32) + last_two_ref[...].astype(jnp.float32)
    lower = two_ref[:half, :].astype(jnp.float32) + last_one_ref[...].astype(jnp.float32)
    work[:half, :] = home_ref[:half, :] + upper
    work[half:, :] = home_ref[half:, :] + lower
    for d in range(count):
        block = pl.ds(pl.multiple_of((me ^ d) * sub, sub), sub)
        outs[d][...] = work[block, :].astype(jnp.bfloat16)
    for copy in copies:
        copy.wait()


def totals_of(home, ones, lasts, count, sub, column):
    rows, full_width = home.shape
    piece = jax.ShapeDtypeStruct((sub, full_width), jnp.bfloat16)
    stacked = jax.ShapeDtypeStruct((sub * len(column), full_width), jnp.bfloat16)
    outs = pl.pallas_call(
        functools.partial(total_kernel, count, len(column)),
        out_shape=(piece,) * count + ((stacked,) if column else ()),
        in_specs=[whole()] * 5 + [anywhere()] * len(column),
        out_specs=(whole(),) * count + ((anywhere(),) if column else ()),
        scratch_shapes=[
            pltpu.VMEM((rows, full_width), jnp.float32),
            pltpu.SemaphoreType.DMA((max(1, len(column)),)),
        ],
        compiler_params=params(8 * MIB),
        cost_estimate=pl.CostEstimate(
            flops=4 * home.size, bytes_accessed=20 * home.size, transcendentals=0
        ),
        name="total",
    )(home, *ones, *lasts, *column)
    return list(outs[:count]), list(outs[count:])


def small_call(kernel, name, inputs, after, outs, scratch, limit):
    size = sum(x.size * x.dtype.itemsize for x in inputs)
    return pl.pallas_call(
        kernel,
        out_shape=tuple(jax.ShapeDtypeStruct(*out) for out in outs),
        in_specs=[whole()] * len(inputs) + [anywhere()] * len(after),
        out_specs=(whole(),) * len(outs),
        scratch_shapes=scratch,
        compiler_params=params(limit),
        cost_estimate=pl.CostEstimate(flops=size, bytes_accessed=2 * size, transcendentals=0),
        name=name,
    )(*inputs, *after)


def sum_plane(kept, got, rows, column):
    f32, b16 = jnp.float32, jnp.bfloat16
    n_tensor = lax.axis_size("tensor")
    count, full_width = kept.shape[0] // rows, kept.shape[1]
    half = rows // 2
    sub = rows // n_tensor
    if count == 4 and half % 16 == 0 and sub % 16 == 0:
        one, two, home, side = small_call(
            pack_kernel,
            "pack",
            [kept, got],
            [],
            [((rows, full_width), b16)] * 2
            + [((rows, full_width), f32), ((2, half, full_width), f32)],
            [],
            10 * MIB,
        )
        from_one, from_two = swap(one, "expert", 1), swap(two, "expert", 2)
        pass_one, pass_two = small_call(
            pass_kernel,
            "pass_on",
            [side, from_one, from_two],
            column[:0:-1],
            [((half, full_width), b16)] * 2,
            [],
            6 * MIB,
        )
        last_one, last_two = swap(pass_one, "expert", 1), swap(pass_two, "expert", 2)
        pieces, stacked = totals_of(
            home, [from_one, from_two], [last_one, last_two], n_tensor, sub, column
        )
        return pieces, [one, two], [pass_one, pass_two], stacked
    both = (kept.astype(f32) + got.astype(f32)).reshape(count, rows, full_width)
    total = both[0]
    for d in range(1, count):
        total = total + swap(both[d].astype(b16), "expert", d).astype(f32)
    total = total.astype(b16).reshape(n_tensor, sub, full_width)
    me = lax.axis_index("tensor")
    pieces = [lax.dynamic_index_in_dim(total, me ^ d, 0, False) for d in range(n_tensor)]
    return pieces, [], [], []


def on_device(
    tokens, routes, route_weights, norm_gain, final_gain, w_gate, w_up, w_down, head_weight, targets
):
    tok_rows, width = tokens.shape
    n_expert = lax.axis_size("expert")
    n_tensor = lax.axis_size("tensor")
    my_expert = lax.axis_index("expert")
    my_tensor = lax.axis_index("tensor")
    full_width = width * n_tensor
    own = tok_rows // n_tensor
    splits = 2 if own % 32 == 0 else 1
    sub = own // splits
    rows = sub * n_tensor

    blocks = begin(tokens, norm_gain, final_gain, n_tensor, splits)
    slices = [gather_near(block, "tensor") for block in blocks]
    gains = None
    planes, raws = [], []
    after = []
    for h in range(splits):
        normed, raw, *made = norm_rows(
            slices[h], [gains], routes, route_weights, splits, h, rows, after
        )
        if made:
            gains = made[0]
        plane, _ = gather_plane(normed, "expert", [])
        planes.append(plane)
        raws.append(raw)
        after = plane[3:]

    w_gate = pltpu.with_memory_space_constraint(w_gate, pltpu.HBM)
    w_up = pltpu.with_memory_space_constraint(w_up, pltpu.HBM)
    head_rows = pltpu.with_memory_space_constraint(head_weight.T, pltpu.HBM)
    target_rows = targets.reshape(n_expert, n_tensor, splits, sub)
    terms = []
    before = {}
    for h in range(splits):
        if 2 * n_expert * rows <= LARGEST:
            nearer = stack_rows(planes[h][:3], [] if before else sum((p[:0:-1] for p in slices[1:2]), []))
            away = [swap(nearer, "seq", 1)]
            if planes[h][3:]:
                away.append(swap(stack_rows(planes[h][3:], before.get("packed", [])), "seq", 1))
            half = n_expert * rows
            everything = planes[h] + away
            tile = tile_of(w_gate)
            count = w_gate.shape[2] // tile
            cuts = [0, count // 2, count // 2 + (count + 1) // 4, count] if h else [0, count]
            ties = [before.get(key, []) for key in ("packed", "passed", "totals")]
            hidden = [
                hidden_rows(
                    everything, w_gate, w_up, ties[i], cuts[i], cuts[i + 1] - cuts[i], tile
                )
                for i in range(len(cuts) - 1)
            ]
            later = planes[h + 1][1:3] if h + 1 < splits else []
            other = down_rows(hidden, w_down, half, half, later + before.get("sums", [])[::-1])
            kept = down_rows(hidden, w_down, 0, half, before.get("final", []))
        else:
            away = [swap(p, "seq", 1) for p in planes[h]]
            kept, other = many_rows(planes[h], w_gate, w_up, w_down), many_rows(
                away, w_gate, w_up, w_down
            )
        got = swap(other, "seq", 1)
        totals, packed, passed, stacked = sum_plane(kept, got, rows, before.get("column", []))
        sums = swap_each(totals[1:], "tensor")
        cut = []
        if before:
            plane, cut = gather_plane(stacked[0], "expert", [])
            wanted = target_rows[:, :, h - 1].reshape(1, -1)
            terms = [head_terms(plane, head_rows, wanted, sub, terms)]
        final = final_rows(far_first(totals[:1] + sums), raws[h], gains, [])
        column = gather_near(final, "tensor")
        before = {
            "kept": [kept],
            "packed": packed,
            "passed": passed,
            "totals": totals,
            "sums": sums,
            "final": [final],
            "column": column,
        }
    column = stack_line(column, cut)
    plane, _ = gather_plane(column, "expert", terms)
    wanted = target_rows[:, :, splits - 1].reshape(1, -1)
    terms = [head_terms(plane, head_rows, wanted, sub, terms)]
    losses = join_all(terms[0])[::8]
    start = (my_expert * n_tensor + my_tensor) * sub
    return lax.dynamic_slice_in_dim(losses, start, sub, 1).reshape(own)


def solution(mesh):
    return jax.shard_map(
        on_device,
        mesh=mesh,
        in_specs=(
            P(("seq", "expert"), "tensor"),
            P(("seq", "expert"), None),
            P(("seq", "expert"), None),
            P("tensor"),
            P("tensor"),
            P("expert", None, ("seq", "tensor")),
            P("expert", None, ("seq", "tensor")),
            P("expert", ("seq", "tensor"), None),
            P(None, ("expert", "tensor")),
            P("seq"),
        ),
        out_specs=P(("seq", "expert", "tensor")),
        check_vma=False,
    )
```
